32 devices in a mesh: dp: 8 (over z, y), krow: 4 (over x, core).
Axes of the slice: x: 2, y: 2, z: 4, core: 2. Of those that a mesh axis runs over, the one named last changes fastest.
Arguments:
- tokens: bfloat16 [64, 512, 768], P('dp', 'krow'), may hold values from -6 to 6
- segment_ids: int32 [64, 512], P('dp'), may hold values from 0 to 7, never falling along the last dimension, each value on 1 to 256 neighbouring positions
- segment_live: int32 [64, 8], P('dp'), may hold values 0 or 1
- w_query: bfloat16 [768, 768], replicated, may hold values from -0.21875 to 0.21875
- b_query: bfloat16 [768], replicated, may hold values from -3 to 3
- w_key: bfloat16 [768, 768], replicated, may hold values from -0.21875 to 0.21875
- w_value: bfloat16 [768, 768], replicated, may hold values from -0.21875 to 0.21875
- w_out: bfloat16 [768, 768], replicated, may hold values from -0.875 to 0.875
- b_out: bfloat16 [768], replicated, may hold values from -3 to 3
- attn_gain: bfloat16 [768], replicated, may hold values from 0.25 to 1.75
- attn_shift: bfloat16 [768], replicated, may hold values from -2 to 2
- w_up: bfloat16 [768, 3072], replicated, may hold values from -0.21875 to 0.21875
- b_up: bfloat16 [3072], replicated, may hold values from -3 to 3
- w_down: bfloat16 [3072, 768], replicated, may hold values from -0.109375 to 0.109375
- b_down: bfloat16 [768], replicated, may hold values from -3 to 3
- ffn_gain: bfloat16 [768], replicated, may hold values from 0.25 to 1.75
- ffn_shift: bfloat16 [768], replicated, may hold values from -2 to 2
- compress: bfloat16 [256, 512], replicated, may hold values from -0.375 to 0.375
- cotangent: bfloat16 [64, 512, 768], P('dp', 'krow'), may hold values from -6 to 6
Outputs:
- output: float32 [64, 512, 768], P('dp', 'krow')
- grad_tokens: float32 [64, 512, 768], P('dp', 'krow')
- grad_w_query: float32 [768, 768], P('krow', 'dp')
- grad_b_query: float32 [768], replicated
- grad_w_key: float32 [768, 768], P('krow', 'dp')
- grad_w_value: float32 [768, 768], P('krow', 'dp')
- grad_w_out: float32 [768, 768], P('krow', 'dp')
- grad_b_out: float32 [768], replicated
- grad_attn_gain: float32 [768], replicated
- grad_attn_shift: float32 [768], replicated
- grad_w_up: float32 [768, 3072], P('krow', 'dp')
- grad_b_up: float32 [3072], replicated
- grad_w_down: float32 [3072, 768], P('krow', 'dp')
- grad_b_down: float32 [768], replicated
- grad_ffn_gain: float32 [768], replicated
- grad_ffn_shift: float32 [768], replicated
- grad_compress: float32 [256, 512], P('krow', 'dp')
The draws below stay inside these ranges and needn't reach their ends.
Inputs may be any that keep to these rules, and one draw needn't show every extreme that they name: `segment_ids`: segment numbers never fall along a row; one segment of each row has exactly 256 positions.
All inputs are finite; a program needn't handle non-finite values. No bound on the sum of `segment_live` on one device may be relied on, other than what follows from the above.
Results may differ from the reference program's by a relative error of at most 0.024.
Values may be sent and summed in bfloat16 or wider, within the bound.
No kernel may reach another device: no remote copies, remote signals or barrier semaphores. Data moves between devices by JAX's collectives and lax.ppermute only.
A program may use at most 192 MiB of HBM per device.

```python
import math
import jax
import jax.numpy as jnp
import numpy as np
from jax import lax

H = 12
HD = 64
D = 768
FF = 3072
SEQ = 512
K = 256
NSEG = 8
ROWS = 64


def set_ends(values, stream_key, smallest, high):
    longest = values.shape.index(max(values.shape))
    spots = []
    for shift in (0, 1):
        where = [jax.random.randint(jax.random.fold_in(stream_key, axis), (), 0, length) for axis, length in enumerate(values.shape)]
        where[longest] = (where[longest] + shift) % values.shape[longest]
        spots.append(tuple(where))
    return values.at[spots[0]].set(smallest).at[spots[1]].set(high)


def levels(key, dims, shards, smallest, top_value):
    factor_of = 1.0
    for dim, shards_of in shards:
        heights = jax.random.uniform(jax.random.fold_in(jax.random.fold_in(key, 6), dim), (shards_of,), jnp.float32, smallest / len(shards), top_value / len(shards))
        factor_of = factor_of * jnp.repeat(jnp.exp(heights), dims[dim] // shards_of).reshape((-1,) + (1,) * (len(dims) - 1 - dim))
    return factor_of


def split_up(amount, total, limit, skew):
    portions = [(1 << 20) // math.isqrt(grade ** skew) + 1 for grade in range(2, amount + 1)]
    spare, given = total - limit - (amount - 1), [1] * (amount - 1)
    while spare > 0:
        movable = [i for i in range(amount - 1) if given[i] < limit]
        mass, left = sum([portions[i] for i in movable]), spare
        for i in movable:
            extra = min(limit - given[i], max(1, left * portions[i] // mass), spare)
            given[i] = given[i] + extra
            spare = spare - extra
    return np.array([limit] + given)


def ragged_sizes(rng, number_of, total, bound, lean):
    if number_of == 2:
        one = jax.random.randint(rng, (), max(1, total - bound), min(bound, total - 1) + 1)
        return jnp.stack([one, total - one])
    tallies = jnp.asarray(split_up(number_of, total, bound, lean), jnp.int32)
    twos = (number_of - 1) // 2
    donor, receiver = tallies[1:1 + 2 * twos:2], tallies[2:2 + 2 * twos:2]
    slack = jnp.minimum(donor - 1, bound - receiver)
    shifted = jax.random.randint(jax.random.fold_in(rng, 1), (twos,), 0, 1 << 20) % (slack + 1)
    tallies = tallies.at[1:1 + 2 * twos:2].set(donor - shifted).at[2:2 + 2 * twos:2].set(receiver + shifted)
    return tallies[jax.random.permutation(jax.random.fold_in(rng, 2), number_of)]


def scatter_about(own_key, extent, scale, reach, split=(), kind=jnp.bfloat16):
    gain = levels(own_key, extent, split, -0.22, 0.18) if split else 1.0
    values = jax.random.normal(own_key, extent, jnp.float32) * scale * gain
    return jnp.minimum(jnp.maximum(values, -reach), reach).astype(kind)


def setup_inputs(seed: int = 0) -> dict:
    key_of = jax.random.split(jax.random.key(seed), 20)
    return {
        "tokens": scatter_about(key_of[0], (ROWS, SEQ, D), 1.0, 6.0, ((0, 8), (1, 4))),
        "segment_ids": jax.vmap(lambda own: jnp.searchsorted(jnp.cumsum(ragged_sizes(own, NSEG, SEQ, SEQ // 2, 0)), jnp.arange(SEQ), side="right"))(jax.random.split(key_of[1], ROWS)).reshape((ROWS, SEQ)).astype(jnp.int32),
        "segment_live": set_ends((jax.random.randint(key_of[2], (ROWS, NSEG), 0, 4) < 3).astype(jnp.int32), jax.random.fold_in(key_of[2], 1), 0, 1),
        "w_query": scatter_about(key_of[3], (D, D), D ** -0.5, 0.21875),
        "b_query": scatter_about(key_of[4], (D,), 0.5, 3.0),
        "w_key": scatter_about(key_of[5], (D, D), D ** -0.5, 0.21875),
        "w_value": scatter_about(key_of[6], (D, D), D ** -0.5, 0.21875),
        "w_out": scatter_about(key_of[7], (D, D), (D // 16) ** -0.5, 0.875),
        "b_out": scatter_about(key_of[8], (D,), 0.5, 3.0),
        "attn_gain": jnp.clip(1.0 + 0.15 * jax.random.normal(key_of[9], (D,), jnp.float32), 0.25, 1.75).astype(jnp.bfloat16),
        "attn_shift": scatter_about(key_of[10], (D,), 0.3, 2.0),
        "w_up": scatter_about(key_of[11], (D, FF), D ** -0.5, 0.21875),
        "b_up": scatter_about(key_of[12], (FF,), 0.5, 3.0),
        "w_down": scatter_about(key_of[13], (FF, D), FF ** -0.5, 0.109375),
        "b_down": scatter_about(key_of[14], (D,), 0.5, 3.0),
        "ffn_gain": jnp.clip(1.0 + 0.15 * jax.random.normal(key_of[15], (D,), jnp.float32), 0.25, 1.75).astype(jnp.bfloat16),
        "ffn_shift": scatter_about(key_of[16], (D,), 0.3, 2.0),
        "compress": scatter_about(key_of[17], (K, SEQ), (SEQ // 2) ** -0.5, 0.375),
        "cotangent": scatter_about(key_of[18], (ROWS, SEQ, D), 1.0, 6.0, ((0, 8), (1, 4))),
    }


@jax.custom_vjp
def low(v):
    return lax.optimization_barrier(v.astype(jnp.bfloat16)).astype(jnp.float32)

@jax.custom_vjp
def low_back(v):
    return v

def low_keep(v):
    return (low(v), None)

def low_pass(kept, grad):
    return (grad,)

def back_keep(v):
    return (v, None)

def back_low(kept, grad):
    return (low(grad),)
low.defvjp(low_keep, low_pass)
low_back.defvjp(back_keep, back_low)
highest = lax.Precision.HIGHEST

def layer_norm(value, norm_gain, norm_shift):
    average = lax.optimization_barrier(jnp.mean(value, axis=-1, keepdims=True))
    centred = value - average
    spread = lax.optimization_barrier(jnp.mean(centred * centred, axis=-1, keepdims=True))
    return centred * lax.rsqrt(spread + 1e-05) * norm_gain + norm_shift

def forward_rows(tokens, live, w_query, b_query, w_key, w_value, w_out, b_out, attn_gain, attn_shift, w_up, b_up, w_down, b_down, ffn_gain, ffn_shift, compress):
    groups = tokens.shape[0]
    scale = 1.0 / math.sqrt(HD)
    query = low(low_back(jnp.einsum('gtd,de->gte', tokens, w_query, precision=highest) + b_query))
    packed = jnp.einsum('jt,gtd->gjd', compress, tokens * live[:, :, None], precision=highest)
    packed = low(low_back(packed))
    keys = low(low_back(jnp.einsum('gjd,de->gje', packed, w_key, precision=highest)))
    values = low(low_back(jnp.einsum('gjd,de->gje', packed, w_value, precision=highest)))
    q_heads = query.reshape(groups, SEQ, H, HD)
    k_heads = keys.reshape(groups, K, H, HD)
    v_heads = values.reshape(groups, K, H, HD)
    scores = low_back(jnp.einsum('gihe,gjhe->ghij', q_heads, k_heads, precision=highest) * scale)
    weights = jax.nn.softmax(scores, axis=-1)
    attended = jnp.einsum('ghij,gjhe->gihe', low(weights), v_heads, precision=highest).reshape(groups, SEQ, D)
    attended = low(low_back(attended))
    branch = low_back(jnp.einsum('gtd,de->gte', attended, w_out, precision=highest) + b_out)
    normed = layer_norm(tokens + branch, attn_gain, attn_shift)
    upward = low_back(jnp.einsum('gtd,df->gtf', low(normed), w_up, precision=highest) + b_up)
    activ = low(jax.nn.gelu(upward, approximate=False))
    downward = low_back(jnp.einsum('gtf,fd->gtd', activ, w_down, precision=highest) + b_down)
    return layer_norm(normed + downward, ffn_gain, ffn_shift)

def reference(tokens, segment_ids, segment_live, w_query, b_query, w_key, w_value, w_out, b_out, attn_gain, attn_shift, w_up, b_up, w_down, b_down, ffn_gain, ffn_shift, compress, cotangent):
    labels = jnp.arange(NSEG, dtype=jnp.int32)
    match = (segment_ids[:, :, None] == labels[None, None, :]).astype(jnp.float32)
    live = lax.optimization_barrier(jnp.sum(match * segment_live[:, None, :].astype(jnp.float32), axis=-1))
    params = tuple((p.astype(jnp.float32) for p in (w_query, b_query, w_key, w_value, w_out, b_out, attn_gain, attn_shift, w_up, b_up, w_down, b_down, ffn_gain, ffn_shift, compress)))
    group = math.gcd(ROWS, 8)
    blocks = ROWS // group
    token_blocks = tokens.astype(jnp.float32).reshape(blocks, group, SEQ, D)
    live_blocks = live.reshape(blocks, group, SEQ)
    cot_blocks = cotangent.astype(jnp.float32).reshape(blocks, group, SEQ, D)

    def one_group(totals, items):
        token_part, live_part, cot_part = items

        def apply_rows(token_in, *weights_in):
            return forward_rows(token_in, live_part, *weights_in)
        result, pullback = jax.vjp(apply_rows, token_part, *params)
        grads = pullback(cot_part)
        summed = tuple((first_part + second_part for first_part, second_part in zip(totals, grads[1:])))
        return (summed, (result, grads[0]))
    start_totals = tuple((jnp.zeros_like(p) for p in params))
    totals, (results, token_grads) = lax.scan(one_group, start_totals, (token_blocks, live_blocks, cot_blocks))
    output = results.reshape(ROWS, SEQ, D)
    grad_tokens = token_grads.reshape(ROWS, SEQ, D)
    g_wq, g_bq, g_wk, g_wv, g_wo, g_bo, g_ag, g_as, g_wu, g_bu, g_wd, g_bd, g_fg, g_fs, g_cp = totals
    return (output, grad_tokens, g_wq, g_bq, g_wk, g_wv, g_wo, g_bo, g_ag, g_as, g_wu, g_bu, g_wd, g_bd, g_fg, g_fs, g_cp)
```

```python
import functools
import math

import jax
import jax.numpy as jnp
from jax import lax
from jax.experimental import pallas as pl
from jax.experimental.pallas import tpu as pltpu
from jax.sharding import PartitionSpec as P

H = 12
HD = 64
f32 = jnp.float32
bf16 = jnp.bfloat16
VMEM_LIMIT = 60 * 1024 * 1024


def nn(a, b):
    return lax.dot_general(a, b, (((1,), (0,)), ((), ())), preferred_element_type=f32)


def nt(a, b):
    return lax.dot_general(a, b, (((1,), (1,)), ((), ())), preferred_element_type=f32)


def whole(shape):
    rank = len(shape)
    return pl.BlockSpec(shape, lambda *_: (0,) * rank, pipeline_mode=pl.Buffered(1))


def row_block(*shape):
    rank = len(shape)
    return pl.BlockSpec((1,) + shape, lambda r, *_: (r,) + (0,) * rank)


def kernel_params(limit=VMEM_LIMIT):
    return pltpu.CompilerParams(dimension_semantics=("arbitrary",), vmem_limit_bytes=limit)


def cost(flops, moved, trans=0):
    return pl.CostEstimate(flops=int(flops), bytes_accessed=int(moved), transcendentals=int(trans))


def add_to(ref, value, first):
    @pl.when(first)
    def _():
        ref[...] = value

    @pl.when(jnp.logical_not(first))
    def _():
        ref[...] += value


def col_sum(value):
    return jnp.sum(value, axis=0, keepdims=True)


def gelu_parts(u):
    t = 1.0 / (1.0 + (0.3275911 / math.sqrt(2.0)) * jnp.abs(u))
    e = jnp.exp(-0.5 * u * u)
    poly = t * (
        0.5 * 0.254829592
        + t
        * (
            0.5 * -0.284496736
            + t * (0.5 * 1.421413741 + t * (0.5 * -1.453152027 + t * (0.5 * 1.061405429)))
        )
    )
    tail = poly * e
    phi = jnp.where(u > 0, 1.0 - tail, tail)
    return u * phi, phi + u * (e * (1.0 / math.sqrt(2.0 * math.pi)))


def attn_fwd_kernel(n, *refs):
    toks = refs[:n]
    live, comp, wq, bq, wk, wv, wo, bo = refs[n : n + 8]
    q_t, pk, k, v, lse, att, xhat, rstd = refs[n + 8 : n + 16]
    tok, att_t = refs[n + 16 :]
    length = toks[0].shape[1]
    for i in range(n):
        tok[i * length : (i + 1) * length, :] = toks[i][0]
    masked = (comp[...].astype(f32) * live[0]).astype(bf16)
    x = tok[...]
    pk[0] = nn(masked, x).astype(bf16)
    for c in range(3):
        cols = slice(256 * c, 256 * c + 256)
        q = (nn(x, wq[:, cols]) + bq[:, cols]).astype(bf16) * jnp.asarray(1.0 / math.sqrt(HD), bf16)
        q_t[0, cols, :] = q.T
        k[0, :, cols] = nn(pk[0], wk[:, cols]).astype(bf16)
        v[0, :, cols] = nn(pk[0], wv[:, cols]).astype(bf16)
    lane = lax.broadcasted_iota(jnp.int32, (1, 2 * HD), 1)
    for pair in range(H // 2):
        cols = slice(2 * HD * pair, 2 * HD * (pair + 1))
        k_pair = k[0, :, cols]
        v_t = v[0, :, cols].T
        for half in range(2):
            h = 2 * pair + half
            mine = jnp.where((lane // HD) == half, k_pair, jnp.zeros_like(k_pair))
            s = nn(mine, q_t[0, cols, :])
            top = jnp.max(s, axis=0, keepdims=True)
            e = jnp.exp(s - top)
            total = jnp.sum(e, axis=0, keepdims=True)
            w = (e * (1.0 / total)).astype(bf16)
            lse[0, h : h + 1, :] = top + jnp.log(total)
            att_t[h * HD : (h + 1) * HD, :] = nn(v_t[half * HD : (half + 1) * HD, :], w).astype(bf16)
    for c in range(3):
        cols = slice(256 * c, 256 * c + 256)
        att[0, :, cols] = att_t[cols, :].T
    hidden = x.astype(f32) + nn(att[0], wo[...]) + bo[...]
    average = jnp.mean(hidden, axis=-1, keepdims=True)
    centred = hidden - average
    spread = jnp.mean(centred * centred, axis=-1, keepdims=True)
    r = lax.rsqrt(spread + 1e-05)
    xhat[0] = centred * r
    rstd[0] = jnp.broadcast_to(r, rstd.shape[1:])


def attn_fwd(toks, live, comp, wq, bq, wk, wv, wo, bo):
    rows, length, width = toks[0].shape
    n = len(toks)
    seq = n * length
    keys = comp.shape[0]
    in_specs = [row_block(length, width)] * n + [
        row_block(1, seq),
        whole((keys, seq)),
        whole((width, width)),
        whole((1, width)),
        whole((width, width)),
        whole((width, width)),
        whole((width, width)),
        whole((1, width)),
    ]
    outs = [
        ((width, seq), bf16),
        ((keys, width), bf16),
        ((keys, width), bf16),
        ((keys, width), bf16),
        ((16, seq), f32),
        ((seq, width), bf16),
        ((seq, width), f32),
        ((seq, 128), f32),
    ]
    return pl.pallas_call(
        functools.partial(attn_fwd_kernel, n),
        grid=(rows,),
        in_specs=in_specs,
        out_specs=[row_block(*shape) for shape, _ in outs],
        out_shape=[jax.ShapeDtypeStruct((rows,) + shape, dt) for shape, dt in outs],
        scratch_shapes=[pltpu.VMEM((seq, width), bf16), pltpu.VMEM((width, seq), bf16)],
        compiler_params=kernel_params(),
        cost_estimate=cost(rows * 5e9, 12e6, rows * H * seq * keys),
        name="attn_fwd",
    )(*toks, live, comp, wq, bq, wk, wv, wo, bo)


class Places:
    def __init__(self, n_dp, n_krow):
        self.core = 2
        self.x = n_krow // 2
        self.y = n_krow // 2
        self.z = n_dp // self.y

    def shape(self, rows, cols):
        return (self.y, self.z, self.x, rows, cols)


def put_up(places, ids, nl_t, d_up, keep, send, temp):
    width = nl_t.shape[0]
    rows = width // (2 * places.x)
    cols = keep.shape[-1]
    step = cols * places.y
    for zr in range(places.z):
        start = pl.multiple_of((ids[2] ^ zr) * step, 128)
        temp[...] = nn(nl_t[...], d_up[:, pl.ds(start, step)])
        for cr, out in enumerate((keep, send)):
            for x in range(places.x):
                first = pl.multiple_of((2 * x + (ids[0] ^ cr)) * rows, 16)
                for y in range(places.y):
                    out[ids[1] ^ y, zr, ids[3] ^ x] = temp[
                        pl.ds(first, rows), y * cols : (y + 1) * cols
                    ].astype(bf16)


def put_down(places, ids, d_t, act, keep, send):
    width = d_t.shape[0]
    rows = keep.shape[-2]
    cols = keep.shape[-1]
    for cr, out in enumerate((keep, send)):
        for xr in range(places.x):
            start = pl.multiple_of((2 * (ids[3] ^ xr) + (ids[0] ^ cr)) * cols, 128)
            res = nn(d_t[...], act[:, pl.ds(start, cols)]).astype(bf16)
            for z in range(places.z):
                for y in range(places.y):
                    d = z * places.y + y
                    out[ids[1] ^ y, ids[2] ^ z, xr] = res[d * rows : (d + 1) * rows, :]


def put_square(places, ids, temp, keep, send, lead=()):
    rows = keep.shape[-2]
    cols = keep.shape[-1]
    for cr, out in enumerate((keep, send)):
        for z in range(places.z):
            for y in range(places.y):
                d = z * places.y + y
                first = pl.multiple_of(2 * rows * d + rows * (ids[0] ^ cr), 16)
                for x in range(places.x):
                    out[lead + (ids[1] ^ y, ids[2] ^ z, ids[3] ^ x)] = temp[
                        pl.ds(first, rows), x * cols : (x + 1) * cols
                    ].astype(bf16)


def ffn_fwd_kernel(n, places, ids, *refs):
    cots = refs[:n]
    xhat, gain, shift, wu, bu, wd, bd, fgain, fshift = refs[n : n + 9]
    refs = refs[n + 9 :]
    outs = refs[:n]
    gp, dh2, g_fgain, g_fshift, g_bd = refs[n : n + 5]
    grads = refs[n + 5 : -2]
    act, d_t = refs[-2:]
    r = pl.program_id(0)
    seq = xhat.shape[1]
    length = outs[0].shape[1]
    ff = wu.shape[1]
    chunk = 512
    rows = pl.ds(pl.multiple_of(r * seq, seq), seq)
    normed = xhat[0] * gain[...] + shift[...]
    low = normed.astype(bf16)
    total = normed + bd[...]
    for c in range(ff // chunk):
        cols = slice(c * chunk, (c + 1) * chunk)
        u = nn(low, wu[:, cols]) + bu[:, cols]
        a, g = gelu_parts(u)
        a = a.astype(bf16)
        act[rows, cols] = a
        gp[0, :, cols] = g.astype(bf16)
        total = total + nn(a, wd[cols, :])
    average = jnp.mean(total, axis=-1, keepdims=True)
    centred = total - average
    spread = jnp.mean(centred * centred, axis=-1, keepdims=True)
    rs = lax.rsqrt(spread + 1e-05)
    hat = centred * rs
    result = (hat * fgain[...] + fshift[...]).astype(bf16)
    for i in range(n):
        outs[i][0] = result[i * length : (i + 1) * length, :]
    cot = jnp.concatenate([c[0] for c in cots], axis=0).astype(f32)
    first = r == 0
    add_to(g_fgain, col_sum(cot * hat), first)
    add_to(g_fshift, col_sum(cot), first)
    dhat = cot * fgain[...]
    d = rs * (
        dhat
        - jnp.mean(dhat, axis=-1, keepdims=True)
        - hat * jnp.mean(dhat * hat, axis=-1, keepdims=True)
    )
    dh2[0] = d
    d_low = d.astype(bf16)
    add_to(g_bd, col_sum(d_low.astype(f32)), first)
    for i in range(pl.cdiv(d_t.shape[1], seq)):

        @pl.when(r == i)
        def _():
            d_t[:, i * seq : (i + 1) * seq] = d_low.T

    @pl.when(r == pl.num_programs(0) - 1)
    def _():
        if places is None:
            for c in range(ff // 768):
                cols = slice(c * 768, (c + 1) * 768)
                grads[0][:, cols] = nn(d_t[...], act[:, cols]).astype(bf16)
        else:
            put_down(places, ids, d_t, act, *grads)


def ffn_fwd(places, ids, cots, xhat, gain, shift, wu, bu, wd, bd, fgain, fshift):
    rows, length, width = cots[0].shape
    n = len(cots)
    seq = n * length
    ff = wu.shape[1]
    vec = whole((1, width))
    in_specs = (
        [pl.BlockSpec(memory_space=pltpu.SMEM)]
        + [row_block(length, width)] * n
        + [
            row_block(seq, width),
            vec,
            vec,
            whole((width, ff)),
            whole((1, ff)),
            whole((ff, width)),
            vec,
            vec,
            vec,
        ]
    )
    outs = [((length, width), bf16)] * n + [((seq, ff), bf16), ((seq, width), f32)]
    if places is None:
        grads = [(width, ff)]
    else:
        dp = places.y * places.z
        grads = [places.shape(width // dp, ff // (2 * places.x))] * 2
    return pl.pallas_call(
        functools.partial(ffn_fwd_kernel, n, places),
        grid=(rows,),
        in_specs=in_specs,
        out_specs=[row_block(*shape) for shape, _ in outs] + [vec] * 3 + [whole(g) for g in grads],
        out_shape=[jax.ShapeDtypeStruct((rows,) + shape, dt) for shape, dt in outs]
        + [jax.ShapeDtypeStruct((1, width), f32)] * 3
        + [jax.ShapeDtypeStruct(g, bf16) for g in grads],
        scratch_shapes=[
            pltpu.VMEM((rows * seq, ff), bf16),
            pltpu.VMEM((width, rows * seq), bf16),
        ],
        compiler_params=kernel_params(),
        cost_estimate=cost(rows * seq * width * ff * 6, 24e6, rows * seq * ff * 2),
        name="ffn_fwd",
    )(ids, *cots, xhat, gain, shift, wu, bu, wd, bd, fgain, fshift)


def ffn_bwd_kernel(places, ids, *refs):
    gp, dh2, xhat, rstd, att, gain, shift, wu, wd, wo = refs[:10]
    dh1, da_t, g_bu, g_gain, g_shift, g_bo = refs[10:16]
    split = 1 if places is None else 2
    up, out = refs[16 : 16 + split], refs[16 + split : 16 + 2 * split]
    dup, nl_t, gwo, temp = refs[16 + 2 * split :]
    r = pl.program_id(0)
    first = r == 0
    seq = xhat.shape[1]
    ff = wu.shape[1]
    chunk = 512
    rows = pl.ds(pl.multiple_of(r * seq, seq), seq)
    d_low = dh2[0].astype(bf16)
    dn = dh2[0]
    for c in range(ff // chunk):
        cols = slice(c * chunk, (c + 1) * chunk)
        d = (gp[0, :, cols].astype(f32) * nt(d_low, wd[cols, :])).astype(bf16)
        dup[rows, cols] = d
        dn = dn + nt(d, wu[:, cols])
        s = col_sum(d.astype(f32))

        @pl.when(first)
        def _():
            g_bu[:, cols] = s

        @pl.when(jnp.logical_not(first))
        def _():
            g_bu[:, cols] += s

    hat = xhat[0]
    add_to(g_gain, col_sum(dn * hat), first)
    add_to(g_shift, col_sum(dn), first)
    dhat = dn * gain[...]
    d = rstd[0, :, 0:1] * (
        dhat
        - jnp.mean(dhat, axis=-1, keepdims=True)
        - hat * jnp.mean(dhat * hat, axis=-1, keepdims=True)
    )
    dh1[0] = d
    branch = d.astype(bf16)
    add_to(g_bo, col_sum(branch.astype(f32)), first)
    da_t[0] = nt(wo[...], branch).astype(bf16)
    add_to(gwo, nn(branch.T, att[0]), first)
    low = (hat * gain[...] + shift[...]).astype(bf16)
    for i in range(pl.cdiv(nl_t.shape[1], seq)):

        @pl.when(r == i)
        def _():
            nl_t[:, i * seq : (i + 1) * seq] = low.T

    @pl.when(r == pl.num_programs(0) - 1)
    def _():
        if places is None:
            for c in range(ff // 768):
                cols = slice(c * 768, (c + 1) * 768)
                up[0][:, cols] = nn(nl_t[...], dup[:, cols]).astype(bf16)
            out[0][...] = gwo[...].astype(bf16)
        else:
            put_up(places, ids, nl_t, dup, *up, temp)
            put_square(places, ids, gwo, *out)


def ffn_bwd(places, ids, gp, dh2, xhat, rstd, att, gain, shift, wu, wd, wo):
    rows, seq, ff = gp.shape
    width = wu.shape[0]
    vec = whole((1, width))
    in_specs = [
        pl.BlockSpec(memory_space=pltpu.SMEM),
        row_block(seq, ff),
        row_block(seq, width),
        row_block(seq, width),
        row_block(seq, 128),
        row_block(seq, width),
        vec,
        vec,
        whole((width, ff)),
        whole((ff, width)),
        whole((width, width)),
    ]
    outs = [((seq, width), f32), ((width, seq), bf16)]
    if places is None:
        grads = [(width, ff), (width, width)]
    else:
        dp = places.y * places.z
        grads = [places.shape(width // (2 * places.x), ff // dp)] * 2
        grads += [places.shape(width // (2 * dp), width // places.x)] * 2
    return pl.pallas_call(
        functools.partial(ffn_bwd_kernel, places),
        grid=(rows,),
        in_specs=in_specs,
        out_specs=[row_block(*shape) for shape, _ in outs]
        + [whole((1, ff))]
        + [vec] * 3
        + [whole(g) for g in grads],
        out_shape=[jax.ShapeDtypeStruct((rows,) + shape, dt) for shape, dt in outs]
        + [jax.ShapeDtypeStruct((1, ff), f32)]
        + [jax.ShapeDtypeStruct((1, width), f32)] * 3
        + [jax.ShapeDtypeStruct(g, bf16) for g in grads],
        scratch_shapes=[
            pltpu.VMEM((rows * seq, ff), bf16),
            pltpu.VMEM((width, rows * seq), bf16),
            pltpu.VMEM((width, width), f32),
            pltpu.VMEM((width, width), f32),
        ],
        compiler_params=kernel_params(),
        cost_estimate=cost(rows * seq * width * ff * 6, 30e6),
        name="ffn_bwd",
    )(ids, gp, dh2, xhat, rstd, att, gain, shift, wu, wd, wo)


def attn_bwd_kernel(n, places, ids, *refs):
    toks = refs[:n]
    q_t, pk, k, v, lse, da_t, comp_t, live_row, live_col, wq, wk, wv, dh1 = refs[n : n + 13]
    refs = refs[n + 13 :]
    outs = refs[:n]
    g_bq = refs[n]
    split = 1 if places is None else 2
    square, small = refs[n + 1 : n + 1 + split], refs[n + 1 + split : n + 1 + 2 * split]
    tok, dq_t, dk_t, dv_t, gq, gk, gv, gc = refs[n + 1 + 2 * split :]
    length = toks[0].shape[1]
    r = pl.program_id(0)
    first = r == 0
    for i in range(n):
        tok[i * length : (i + 1) * length, :] = toks[i][0]
    lane = lax.broadcasted_iota(jnp.int32, (1, 2 * HD), 1)
    scale = jnp.asarray(1.0 / math.sqrt(HD), f32)
    for pair in range(H // 2):
        cols = slice(2 * HD * pair, 2 * HD * (pair + 1))
        k_pair = k[0, :, cols]
        v_pair = v[0, :, cols]
        k_t = k_pair.T
        for half in range(2):
            h = 2 * pair + half
            head = slice(h * HD, (h + 1) * HD)
            mine = (lane // HD) == half
            s = nn(jnp.where(mine, k_pair, jnp.zeros_like(k_pair)), q_t[0, cols, :])
            w = jnp.exp(s - lse[0, h : h + 1, :])
            dw = nn(jnp.where(mine, v_pair, jnp.zeros_like(v_pair)), da_t[0, cols, :])
            dot = jnp.sum(w * dw, axis=0, keepdims=True)
            ds = (w * (dw - dot)).astype(bf16)
            dv_t[head, :] = nt(da_t[0, head, :], w.astype(bf16)).astype(bf16)
            dk_t[head, :] = nt(q_t[0, head, :], ds).astype(bf16)
            dq_t[head, :] = (nn(k_t[half * HD : (half + 1) * HD, :], ds) * scale).astype(bf16)
    add_to(gk, nn(dk_t[...], pk[0]), first)
    add_to(gv, nn(dv_t[...], pk[0]), first)
    add_to(gq, nn(dq_t[...], tok[...]), first)
    dp_t = (nn(wk[...], dk_t[...]) + nn(wv[...], dv_t[...])).astype(bf16)
    add_to(gc, nn(tok[...], dp_t) * live_col[0, :, 0:1], first)
    masked = (comp_t[...].astype(f32) * live_col[0, :, 0:1]).astype(bf16)
    dq = dq_t[...].T
    add_to(g_bq, col_sum(dq.astype(f32)), first)
    grad = dh1[0] + nt(dq, wq[...]) + nt(masked, dp_t)
    for i in range(n):
        outs[i][0] = grad[i * length : (i + 1) * length, :].astype(bf16)

    @pl.when(r == pl.num_programs(0) - 1)
    def _():
        for i, g in enumerate((gq, gk, gv)):
            if places is None:
                square[0][i] = g[...].astype(bf16)
            else:
                put_square(places, ids, g, *square, lead=(i,))
        if places is None:
            small[0][...] = gc[...].astype(bf16)
        else:
            rows, cols = small[0].shape[-2:]
            for cr, out in enumerate(small):
                for i in range(n):
                    for j in range(length // (2 * rows)):
                        d = (ids[4] ^ i) * (length // (2 * rows)) + j
                        y, z = d % places.y, d // places.y
                        start = pl.multiple_of(i * length + 2 * rows * j + rows * (ids[0] ^ cr), 16)
                        for x in range(places.x):
                            out[ids[1] ^ y, ids[2] ^ z, ids[3] ^ x] = gc[
                                pl.ds(start, rows), x * cols : (x + 1) * cols
                            ].astype(bf16)


def attn_bwd(places, ids, toks, q_t, pk, k, v, lse, da_t, comp_t, live_row, live_col, wq, wk, wv, dh1):
    rows, length, width = toks[0].shape
    n = len(toks)
    seq = n * length
    keys = comp_t.shape[1]
    in_specs = (
        [pl.BlockSpec(memory_space=pltpu.SMEM)]
        + [row_block(length, width)] * n
        + [
            row_block(width, seq),
            row_block(keys, width),
            row_block(keys, width),
            row_block(keys, width),
            row_block(16, seq),
            row_block(width, seq),
            whole((seq, keys)),
            row_block(1, seq),
            row_block(seq, 128),
            whole((width, width)),
            whole((width, width)),
            whole((width, width)),
            row_block(seq, width),
        ]
    )
    outs = [((length, width), bf16)] * n
    if places is None:
        grads = [(3, width, width), (seq, keys)]
    else:
        dp = places.y * places.z
        grads = [(3,) + places.shape(width // (2 * dp), width // places.x)] * 2
        grads += [places.shape(seq // (2 * dp), keys // places.x)] * 2
    return pl.pallas_call(
        functools.partial(attn_bwd_kernel, n, places),
        grid=(rows,),
        in_specs=in_specs,
        out_specs=[row_block(*shape) for shape, _ in outs]
        + [whole((1, width))]
        + [whole(g) for g in grads],
        out_shape=[jax.ShapeDtypeStruct((rows,) + shape, dt) for shape, dt in outs]
        + [jax.ShapeDtypeStruct((1, width), f32)]
        + [jax.ShapeDtypeStruct(g, bf16) for g in grads],
        scratch_shapes=[
            pltpu.VMEM((seq, width), bf16),
            pltpu.VMEM((width, seq), bf16),
            pltpu.VMEM((width, keys), bf16),
            pltpu.VMEM((width, keys), bf16),
            pltpu.VMEM((width, width), f32),
            pltpu.VMEM((width, width), f32),
            pltpu.VMEM((width, width), f32),
            pltpu.VMEM((seq, keys), f32),
        ],
        compiler_params=kernel_params(),
        cost_estimate=cost(rows * 9e9, 20e6, rows * H * seq * keys),
        name="attn_bwd",
    )(ids, *toks, q_t, pk, k, v, lse, da_t, comp_t, live_row, live_col, wq, wk, wv, dh1)


def gather_rows_kernel(n, ids, *refs):
    out = refs[n]
    for i in range(n):

        @pl.when(pl.program_id(0) == i)
        def _():
            out[...] = refs[i][...].astype(f32)


def gather_rows(ids, parts):
    n = len(parts)
    rows, length, width = parts[0].shape
    spec = pl.BlockSpec((rows, length, width), lambda i, ids: (0, 0, 0))
    return pl.pallas_call(
        functools.partial(gather_rows_kernel, n),
        grid_spec=pltpu.PrefetchScalarGridSpec(
            num_scalar_prefetch=1,
            grid=(n,),
            in_specs=[spec] * n,
            out_specs=pl.BlockSpec((rows, length, width), lambda i, ids: (ids[4] ^ i, 0, 0)),
        ),
        out_shape=jax.ShapeDtypeStruct((n * rows, length, width), f32),
        compiler_params=kernel_params(32 * 1024 * 1024),
        cost_estimate=cost(0, 6 * n * rows * length * width),
        name="gather_rows",
    )(ids, *parts)


def exchange(value, axis, size, relative):
    pairs = [(i, i ^ relative) for i in range(size)]
    return lax.ppermute(value, axis, pairs)


def total_of(parts):
    acc = parts[0].astype(f32)
    for part in parts[1:]:
        acc = acc + part.astype(f32)
    return acc


def reduce_blocks(places, n_dp, n_krow, keep, send, lead=0):
    at = (slice(None),) * lead
    came = exchange(send, "krow", n_krow, 1)
    parts = []
    for yr in range(places.y):
        parts.append((keep[at + (yr,)].astype(f32) + came[at + (yr,)].astype(f32)).astype(bf16))
    got = [parts[0]]
    for yr in range(1, places.y):
        got.append(exchange(parts[yr], "dp", n_dp, yr))
    got = [
        total_of([g[at + (zr,)] for g in got]).astype(bf16) for zr in range(places.z)
    ]
    mine = [got[0]]
    for zr in range(1, places.z):
        mine.append(exchange(got[zr], "dp", n_dp, zr * places.y))
    return total_of(mine).astype(bf16)


def finish_blocks(places, n_krow, part, lead=0):
    at = (slice(None),) * lead
    got = [part[at + (0,)]]
    for xr in range(1, places.x):
        got.append(exchange(part[at + (xr,)], "krow", n_krow, 2 * xr))
    return total_of(got)


def finish_square(places, n_krow, core, part, lead=0):
    at = (slice(None),) * lead
    cols = part.shape[-1] // 2
    mine = lax.dynamic_slice_in_dim(part, core * cols, cols, part.ndim - 1)
    other = lax.dynamic_slice_in_dim(part, (1 - core) * cols, cols, part.ndim - 1)
    here, there = [mine[at + (0,)]], [exchange(other[at + (0,)], "krow", n_krow, 1)]
    for xr in range(1, places.x):
        here.append(exchange(mine[at + (xr,)], "krow", n_krow, 2 * xr))
        there.append(exchange(other[at + (xr,)], "krow", n_krow, 2 * xr + 1))
    here, there = total_of(here), total_of(there)
    low = jnp.where(core == 0, here, there)
    high = jnp.where(core == 0, there, here)
    return jnp.swapaxes(jnp.concatenate([low, high], axis=lead), -1, -2)


def local(
    sizes,
    tokens,
    segment_ids,
    segment_live,
    w_query,
    b_query,
    w_key,
    w_value,
    w_out,
    b_out,
    attn_gain,
    attn_shift,
    w_up,
    b_up,
    w_down,
    b_down,
    ffn_gain,
    ffn_shift,
    compress,
    cotangent,
):
    n_dp, n_krow = sizes
    all_rows, length, width = tokens.shape
    rows = all_rows // n_krow
    seq = n_krow * length
    keys = compress.shape[0]
    ff = w_up.shape[1]
    krow, dp = lax.axis_index("krow"), lax.axis_index("dp")
    places = Places(n_dp, n_krow)
    ids = jnp.stack([krow % 2, dp % places.y, dp // places.y, krow // 2, krow]).astype(jnp.int32)
    fast = (
        width % (2 * places.x * 16) == 0
        and ff % (n_dp * 128) == 0
        and ff % (n_krow * 128) == 0
        and width % (2 * n_dp * 16) == 0
        and seq % (2 * n_dp * 16) == 0
        and width % (places.x * 128) == 0
        and keys % (places.x * 128) == 0
        and length % (seq // n_dp) == 0
    )
    where = places if fast else None

    def spread(value):
        parts = []
        for r in range(n_krow):
            part = lax.dynamic_slice_in_dim(value, (krow ^ r) * rows, rows, 0)
            parts.append(exchange(part, "krow", n_krow, r) if r else part)
        return parts

    def back(parts):
        got = [exchange(part, "krow", n_krow, r) if r else part for r, part in enumerate(parts)]
        return gather_rows(ids, got)

    def row(value):
        return value.astype(f32).reshape(1, -1)

    toks = spread(tokens)
    cot_source = lax.optimization_barrier((cotangent, toks[-1]))[0]
    cots = spread(cot_source)

    my_ids = lax.dynamic_slice_in_dim(segment_ids, krow * rows, rows, 0)
    my_live = lax.dynamic_slice_in_dim(segment_live, krow * rows, rows, 0)
    labels = jnp.arange(segment_live.shape[1], dtype=jnp.int32)
    live = jnp.sum(
        jnp.where(my_ids[:, :, None] == labels, my_live[:, None, :], 0).astype(f32), axis=-1
    )

    def relative(value, axis):
        return jnp.concatenate(
            [
                lax.dynamic_slice_in_dim(value, (krow ^ r) * length, length, axis)
                for r in range(n_krow)
            ],
            axis=axis,
        )

    live = relative(live, 1)
    comp = relative(compress, 1)
    live_row = live[:, None, :]
    live_col = jnp.broadcast_to(live[:, :, None], (rows, seq, 128))

    q_t, pk, k, v, lse, att, xhat, rstd = attn_fwd(
        toks, live_row, comp, w_query, row(b_query), w_key, w_value, w_out, row(b_out)
    )
    gain, shift = row(attn_gain), row(attn_shift)
    res = ffn_fwd(
        where, ids, cots, xhat, gain, shift, w_up, row(b_up), w_down, row(b_down),
        row(ffn_gain), row(ffn_shift),
    )
    outs, (gp, dh2, g_fgain, g_fshift, g_bd), g_down = (
        res[:n_krow],
        res[n_krow : n_krow + 5],
        res[n_krow + 5 :],
    )
    res = ffn_bwd(where, ids, gp, dh2, xhat, rstd, att, gain, shift, w_up, w_down, w_out)
    dh1, da_t, g_bu, g_gain, g_shift, g_bo = res[:6]
    split = 2 if fast else 1
    g_up, g_out = res[6 : 6 + split], res[6 + split :]
    res = attn_bwd(
        where, ids, toks, q_t, pk, k, v, lse, da_t, comp.T, live_row, live_col,
        w_query, w_key, w_value, dh1,
    )
    grads, g_bq = res[:n_krow], res[n_krow]
    g_square, g_comp = res[n_krow + 1 : n_krow + 1 + split], res[n_krow + 1 + split :]

    output = back(outs)
    grad_tokens = back(grads)

    vectors = jnp.concatenate(
        [v.reshape(-1) for v in (g_bq, g_bo, g_gain, g_shift, g_bu, g_bd, g_fgain, g_fshift)]
    ).reshape(-1, 128)
    if fast:
        vectors = vectors + exchange(vectors, "krow", n_krow, 1)
        for size, step, axis, count in (
            (places.x, 2, "krow", n_krow),
            (places.y, 1, "dp", n_dp),
            (places.z, places.y, "dp", n_dp),
        ):
            vectors = total_of(
                [exchange(vectors, axis, count, step * r) if r else vectors for r in range(size)]
            )
        core = krow % 2
        down = finish_blocks(places, n_krow, reduce_blocks(places, n_dp, n_krow, *g_down)).T
        up = finish_blocks(places, n_krow, reduce_blocks(places, n_dp, n_krow, *g_up))
        out = finish_square(places, n_krow, core, reduce_blocks(places, n_dp, n_krow, *g_out))
        square = finish_square(
            places, n_krow, core, reduce_blocks(places, n_dp, n_krow, *g_square, lead=1), lead=1
        )
        small = finish_square(places, n_krow, core, reduce_blocks(places, n_dp, n_krow, *g_comp))
    else:
        vectors = lax.psum(vectors, ("dp", "krow"))

        def scattered(value):
            part = lax.psum_scatter(value, "krow", scatter_dimension=value.ndim - 2, tiled=True)
            return lax.psum_scatter(
                part, "dp", scatter_dimension=value.ndim - 1, tiled=True
            ).astype(f32)

        down = scattered(g_down[0].T)
        up = scattered(g_up[0])
        out = scattered(g_out[0].T)
        square = jnp.stack([scattered(g_square[0][i].T) for i in range(3)])
        blocks = g_comp[0].reshape(n_krow, length, keys)
        blocks = jnp.concatenate(
            [lax.dynamic_slice_in_dim(blocks, krow ^ r, 1, 0) for r in range(n_krow)]
        )
        small = scattered(blocks.reshape(seq, keys).T)

    pieces = []
    start = 0
    for size in (width, width, width, width, ff, width, width, width):
        pieces.append(vectors.reshape(-1)[start : start + size])
        start += size
    return (
        output,
        grad_tokens,
        square[0],
        pieces[0],
        square[1],
        square[2],
        out,
        pieces[1],
        pieces[2],
        pieces[3],
        up,
        pieces[4],
        down,
        pieces[5],
        pieces[6],
        pieces[7],
        small,
    )


def solution(mesh):
    rows = P("dp", "krow", None)
    per_row = P("dp", None)
    block = P("krow", "dp")
    in_specs = (rows, per_row, per_row) + (P(),) * 15 + (rows,)
    out_specs = (
        (rows, rows, block, P(), block, block, block)
        + (P(),) * 3
        + (block, P(), block)
        + (P(),) * 3
        + (block,)
    )
    sizes = (mesh.shape["dp"], mesh.shape["krow"])
    return jax.shard_map(
        functools.partial(local, sizes),
        mesh=mesh,
        in_specs=in_specs,
        out_specs=out_specs,
        check_vma=False,
    )
```

```python
import functools
import math

import jax
import jax.numpy as jnp
from jax import lax
from jax.experimental import pallas as pl
from jax.experimental.pallas import tpu as pltpu
from jax.sharding import PartitionSpec as P

H = 12
HD = 64
f32 = jnp.float32
bf16 = jnp.bfloat16


def nn(a, b):
    return lax.dot_general(a, b, (((1,), (0,)), ((), ())), preferred_element_type=f32)


def nt(a, b):
    return lax.dot_general(a, b, (((1,), (1,)), ((), ())), preferred_element_type=f32)


def whole(shape):
    rank = len(shape)
    return pl.BlockSpec(shape, lambda *_: (0,) * rank, pipeline_mode=pl.Buffered(1))


def fetch_strips(src, dst, sems, ids, other, half, dp):
    copies = []
    for d in range(dp):
        first = pl.multiple_of(2 * half * d + half * (ids[0] ^ other), 16)
        copies.append(
            pltpu.make_async_copy(
                src.at[pl.ds(first, half), :], dst.at[d * half : (d + 1) * half, :], sems.at[d]
            )
        )
        copies[-1].start()
    return copies


def resident():
    return pl.BlockSpec(memory_space=pltpu.VMEM)


def in_hbm(*values):
    return [pltpu.with_memory_space_constraint(v, pltpu.HBM) for v in values]


def fetch(sources, places, sems):
    copies = [
        pltpu.make_async_copy(src, dst, sems.at[i])
        for i, (src, dst) in enumerate(zip(sources, places))
    ]

    @pl.when(pl.program_id(0) == 0)
    def _():
        for copy in copies:
            copy.start()

    def wait(*which):
        @pl.when(pl.program_id(0) == 0)
        def _():
            for i in which:
                copies[i].wait()

    return wait


def anywhere(values):
    return [pl.BlockSpec(memory_space=pl.ANY)] * len(values)


def row_block(*shape):
    rank = len(shape)
    return pl.BlockSpec((1,) + shape, lambda r, *_: (r,) + (0,) * rank)


def kernel_params(mebibytes):
    return pltpu.CompilerParams(dimension_semantics=("arbitrary",), vmem_limit_bytes=mebibytes * 1024 * 1024)


def cost(flops, moved, trans=0):
    return pl.CostEstimate(flops=int(flops), bytes_accessed=int(moved), transcendentals=int(trans))


def add_to(ref, value, first):
    @pl.when(first)
    def _():
        ref[...] = value

    @pl.when(jnp.logical_not(first))
    def _():
        ref[...] += value


def col_sum(value):
    return jnp.sum(value, axis=0, keepdims=True)


def gelu_parts(u):
    phi = 0.5 + 0.5 * lax.erf(u * (1.0 / math.sqrt(2.0)))
    density = jnp.exp(-0.5 * u * u) * (1.0 / math.sqrt(2.0 * math.pi))
    return u * phi, phi + u * density


def attn_fwd_kernel(n, *refs):
    toks = refs[:n]
    live, comp, wq_hbm, bq, wk_hbm, wv_hbm, wo_hbm, bo = refs[n : n + 8]
    q_t, pk, k, v, lse, att, xhat, rstd = refs[n + 8 : n + 16]
    tok, att_t, wq, wk, wv, wo, sems = refs[n + 16 :]
    wait = fetch((wq_hbm, wk_hbm, wv_hbm, wo_hbm), (wq, wk, wv, wo), sems)
    length = toks[0].shape[1]
    for i in range(n):
        tok[i * length : (i + 1) * length, :] = toks[i][0]
    masked = (comp[...].astype(f32) * live[0]).astype(bf16)
    x = tok[...]
    pk[0] = nn(masked, x).astype(bf16)
    wait(0, 1, 2)
    for c in range(3):
        cols = slice(256 * c, 256 * c + 256)
        q = (nn(x, wq[:, cols]) + bq[:, cols]).astype(bf16) * jnp.asarray(1.0 / math.sqrt(HD), bf16)
        q_t[0, cols, :] = q.T
        k[0, :, cols] = nn(pk[0], wk[:, cols]).astype(bf16)
        v[0, :, cols] = nn(pk[0], wv[:, cols]).astype(bf16)
    lane = lax.broadcasted_iota(jnp.int32, (1, 2 * HD), 1)
    for pair in range(H // 2):
        cols = slice(2 * HD * pair, 2 * HD * (pair + 1))
        k_pair = k[0, :, cols]
        v_t = v[0, :, cols].T
        for half in range(2):
            h = 2 * pair + half
            mine = jnp.where((lane // HD) == half, k_pair, jnp.zeros_like(k_pair))
            s = nn(mine, q_t[0, cols, :])
            top = jnp.max(s, axis=0, keepdims=True)
            e = jnp.exp(s - top)
            total = jnp.sum(e, axis=0, keepdims=True)
            w = (e * (1.0 / total)).astype(bf16)
            lse[0, h : h + 1, :] = top + jnp.log(total)
            att_t[h * HD : (h + 1) * HD, :] = nn(v_t[half * HD : (half + 1) * HD, :], w).astype(bf16)
    for c in range(3):
        cols = slice(256 * c, 256 * c + 256)
        att[0, :, cols] = att_t[cols, :].T
    wait(3)
    hidden = x.astype(f32) + nn(att[0], wo[...]) + bo[...]
    average = jnp.mean(hidden, axis=-1, keepdims=True)
    centred = hidden - average
    spread = jnp.mean(centred * centred, axis=-1, keepdims=True)
    r = lax.rsqrt(spread + 1e-05)
    xhat[0] = centred * r
    rstd[0] = jnp.broadcast_to(r, rstd.shape[1:])


def attn_fwd(toks, live, comp, wq, bq, wk, wv, wo, bo):
    rows, length, width = toks[0].shape
    n = len(toks)
    seq = n * length
    keys = comp.shape[0]
    in_specs = [row_block(length, width)] * n + [
        row_block(1, seq),
        whole((keys, seq)),
        pl.BlockSpec(memory_space=pl.ANY),
        whole((1, width)),
        pl.BlockSpec(memory_space=pl.ANY),
        pl.BlockSpec(memory_space=pl.ANY),
        pl.BlockSpec(memory_space=pl.ANY),
        whole((1, width)),
    ]
    outs = [
        ((width, seq), bf16),
        ((keys, width), bf16),
        ((keys, width), bf16),
        ((keys, width), bf16),
        ((16, seq), f32),
        ((seq, width), bf16),
        ((seq, width), f32),
        ((seq, 128), f32),
    ]
    return pl.pallas_call(
        functools.partial(attn_fwd_kernel, n),
        grid=(rows,),
        in_specs=in_specs,
        out_specs=[row_block(*shape) for shape, _ in outs],
        out_shape=[jax.ShapeDtypeStruct((rows,) + shape, dt) for shape, dt in outs],
        scratch_shapes=[pltpu.VMEM((seq, width), bf16), pltpu.VMEM((width, seq), bf16)]
        + [pltpu.VMEM((width, width), bf16)] * 4
        + [pltpu.SemaphoreType.DMA((4,))],
        compiler_params=kernel_params(30),
        cost_estimate=cost(rows * 5e9, 12e6, rows * H * seq * keys),
        name="attn_fwd",
    )(*toks, live, comp, *in_hbm(wq), bq, *in_hbm(wk, wv, wo), bo)


def ffn_fwd_kernel(n, *refs):
    cots = refs[:n]
    xhat, gain, shift, wu, bu, wd, bd, fgain, fshift = refs[n : n + 9]
    refs = refs[n + 9 :]
    outs = refs[:n]
    act, gp, dh2, d_t, sums = refs[n:]
    first = pl.program_id(0) == 0
    length = outs[0].shape[1]
    ff = wu.shape[1]
    chunk = 512
    count = ff // chunk
    normed = xhat[0] * gain[...] + shift[...]
    low = normed.astype(bf16)

    def up(c):
        cols = slice(c * chunk, (c + 1) * chunk)
        return nn(low, wu[:, cols]) + bu[:, cols]

    for c in range(count):
        cols = slice(c * chunk, (c + 1) * chunk)
        a, g = gelu_parts(up(c))
        act[0, :, cols] = a.astype(bf16)
        gp[0, :, cols] = g.astype(bf16)
    total = normed + bd[...] + nn(act[0], wd[...])
    average = jnp.mean(total, axis=-1, keepdims=True)
    centred = total - average
    spread = jnp.mean(centred * centred, axis=-1, keepdims=True)
    rs = lax.rsqrt(spread + 1e-05)
    hat = centred * rs
    result = (hat * fgain[...] + fshift[...]).astype(bf16)
    for i in range(n):
        outs[i][0] = result[i * length : (i + 1) * length, :]
    cot = jnp.concatenate([c[0] for c in cots], axis=0).astype(f32)
    dhat = cot * fgain[...]
    d = rs * (
        dhat
        - jnp.mean(dhat, axis=-1, keepdims=True)
        - hat * jnp.mean(dhat * hat, axis=-1, keepdims=True)
    )
    dh2[0] = d
    d_low = d.astype(bf16)
    d_t[...] = d_low.T
    add_to(
        sums,
        jnp.concatenate(
            [col_sum(cot * hat), col_sum(cot), col_sum(d_low.astype(f32)), jnp.zeros((5, d.shape[1]), f32)],
            axis=0,
        ),
        first,
    )


def ffn_fwd(cots, xhat, gain, shift, wu, bu, wd, bd, fgain, fshift):
    rows, length, width = cots[0].shape
    n = len(cots)
    seq = n * length
    ff = wu.shape[1]
    vec = whole((1, width))
    in_specs = [row_block(length, width)] * n + [
        row_block(seq, width),
        vec,
        vec,
        resident(),
        whole((1, ff)),
        resident(),
        vec,
        vec,
        vec,
    ]
    outs = [((length, width), bf16)] * n + [
        ((seq, ff), bf16),
        ((seq, ff), bf16),
        ((seq, width), f32),
    ]
    return pl.pallas_call(
        functools.partial(ffn_fwd_kernel, n),
        grid=(rows,),
        in_specs=in_specs,
        out_specs=[row_block(*shape) for shape, _ in outs]
        + [pl.BlockSpec((width, seq), lambda r: (0, r))]
        + [whole((8, width))],
        out_shape=[jax.ShapeDtypeStruct((rows,) + shape, dt) for shape, dt in outs]
        + [jax.ShapeDtypeStruct((width, rows * seq), bf16)]
        + [jax.ShapeDtypeStruct((8, width), f32)],
        compiler_params=kernel_params(34),
        cost_estimate=cost(rows * seq * width * ff * 4, 34e6, rows * seq * ff * 2),
        name="ffn_fwd",
    )(*cots, xhat, gain, shift, wu, bu, wd, bd, fgain, fshift)


def ffn_bwd_kernel(*refs):
    gp, dh2, xhat, rstd, gain, shift, wu, wd, wo = refs[:9]
    dup, dh1, da_t, nl_t, br_t, sums = refs[-6:]
    first = pl.program_id(0) == 0
    ff = wu.shape[1]
    chunk = 512
    count = ff // chunk
    d_low = dh2[0].astype(bf16)

    def back(c):
        return nt(d_low, wd[c * chunk : (c + 1) * chunk, :])

    for c in range(count):
        cols = slice(c * chunk, (c + 1) * chunk)
        dup[0, :, cols] = (gp[0, :, cols].astype(f32) * back(c)).astype(bf16)
    tile = min(256, dh2.shape[1])
    for i in range(dh2.shape[1] // tile):
        part = slice(i * tile, (i + 1) * tile)
        for j in range(dh2.shape[2] // 256):
            cols = slice(j * 256, (j + 1) * 256)
            dh1[0, part, cols] = dh2[0, part, cols] + nt(dup[0, part, :], wu[cols, :])
    dn = dh1[0]
    hat = xhat[0]
    dhat = dn * gain[...]
    d = rstd[0, :, 0:1] * (
        dhat
        - jnp.mean(dhat, axis=-1, keepdims=True)
        - hat * jnp.mean(dhat * hat, axis=-1, keepdims=True)
    )
    dh1[0] = d
    branch = d.astype(bf16)
    add_to(
        sums,
        jnp.concatenate(
            [col_sum(dn * hat), col_sum(dn), col_sum(branch.astype(f32)), jnp.zeros((5, d.shape[1]), f32)],
            axis=0,
        ),
        first,
    )
    da_t[0] = nt(wo[...], branch).astype(bf16)
    br_t[...] = branch.T
    nl_t[...] = (hat * gain[...] + shift[...]).astype(bf16).T


def ffn_bwd(gp, dh2, xhat, rstd, gain, shift, wu, wd, wo, after=()):
    rows, seq, ff = gp.shape
    width = wu.shape[0]
    vec = whole((1, width))
    in_specs = [
        row_block(seq, ff),
        row_block(seq, width),
        row_block(seq, width),
        row_block(seq, 128),
        vec,
        vec,
        resident(),
        resident(),
        resident(),
    ] + anywhere(after)
    outs = [((seq, ff), bf16), ((seq, width), f32), ((width, seq), bf16)]
    turned = pl.BlockSpec((width, seq), lambda r: (0, r))
    return pl.pallas_call(
        ffn_bwd_kernel,
        grid=(rows,),
        in_specs=in_specs,
        out_specs=[row_block(*shape) for shape, _ in outs]
        + [turned] * 2
        + [whole((8, width))],
        out_shape=[jax.ShapeDtypeStruct((rows,) + shape, dt) for shape, dt in outs]
        + [jax.ShapeDtypeStruct((width, rows * seq), bf16)] * 2
        + [jax.ShapeDtypeStruct((8, width), f32)],
        compiler_params=kernel_params(34),
        cost_estimate=cost(rows * seq * width * ff * 4.5, 34e6),
        name="ffn_bwd",
    )(gp, dh2, xhat, rstd, gain, shift, wu, wd, wo, *after)


def attn_bwd_kernel(n, *refs):
    toks = refs[:n]
    q_t, k, v, lse, da_t, comp_t, live_col, wq_hbm, wk_hbm, wv_hbm, dh1 = refs[n : n + 11]
    refs = refs[-(n + 10) :]
    outs = refs[:n]
    dq_t, dk_t, dv_t, g_bq, small, tok, wq, wk, wv, sems = refs[n:]
    wait = fetch((wq_hbm, wk_hbm, wv_hbm), (wq, wk, wv), sems)
    length = toks[0].shape[1]
    for i in range(n):
        tok[i * length : (i + 1) * length, :] = toks[i][0]
    lane = lax.broadcasted_iota(jnp.int32, (1, 2 * HD), 1)
    scale = jnp.asarray(1.0 / math.sqrt(HD), f32)
    for pair in range(H // 2):
        cols = slice(2 * HD * pair, 2 * HD * (pair + 1))
        k_pair = k[0, :, cols]
        v_pair = v[0, :, cols]
        k_t = k_pair.T
        for half in range(2):
            h = 2 * pair + half
            head = slice(h * HD, (h + 1) * HD)
            mine = (lane // HD) == half
            s = nn(jnp.where(mine, k_pair, jnp.zeros_like(k_pair)), q_t[0, cols, :])
            w = jnp.exp(s - lse[0, h : h + 1, :])
            dw = nn(jnp.where(mine, v_pair, jnp.zeros_like(v_pair)), da_t[0, cols, :])
            dot = jnp.sum(w * dw, axis=0, keepdims=True)
            ds = (w * (dw - dot)).astype(bf16)
            dv_t[0, head, :] = nt(da_t[0, head, :], w.astype(bf16)).astype(bf16)
            dk_t[0, head, :] = nt(q_t[0, head, :], ds).astype(bf16)
            dq_t[0, head, :] = (nn(k_t[half * HD : (half + 1) * HD, :], ds) * scale).astype(bf16)
    wait(0, 1, 2)
    dp_t = (nn(wk[...], dk_t[0]) + nn(wv[...], dv_t[0])).astype(bf16)
    small[0] = (nn(tok[...], dp_t) * live_col[0, :, 0:1]).astype(bf16)
    masked = (comp_t[...].astype(f32) * live_col[0, :, 0:1]).astype(bf16)
    dq = dq_t[0].T
    g_bq[0] = col_sum(dq.astype(f32))
    grad = dh1[0] + nt(dq, wq[...]) + nt(masked, dp_t)
    for i in range(n):
        outs[i][0] = grad[i * length : (i + 1) * length, :].astype(bf16)


def attn_bwd(toks, q_t, k, v, lse, da_t, comp_t, live_col, wq, wk, wv, dh1, after=()):
    rows, length, width = toks[0].shape
    n = len(toks)
    seq = n * length
    keys = comp_t.shape[1]
    in_specs = (
        [row_block(length, width)] * n
        + [
            row_block(width, seq),
            row_block(keys, width),
            row_block(keys, width),
            row_block(16, seq),
            row_block(width, seq),
            whole((seq, keys)),
            row_block(seq, 128),
            pl.BlockSpec(memory_space=pl.ANY),
            pl.BlockSpec(memory_space=pl.ANY),
            pl.BlockSpec(memory_space=pl.ANY),
            row_block(seq, width),
        ]
        + anywhere(after)
    )
    outs = [((length, width), bf16)] * n + [
        ((width, seq), bf16),
        ((width, keys), bf16),
        ((width, keys), bf16),
        ((1, width), f32),
        ((seq, keys), bf16),
    ]
    return pl.pallas_call(
        functools.partial(attn_bwd_kernel, n),
        grid=(rows,),
        in_specs=in_specs,
        out_specs=[row_block(*shape) for shape, _ in outs],
        out_shape=[jax.ShapeDtypeStruct((rows,) + shape, dt) for shape, dt in outs],
        scratch_shapes=[pltpu.VMEM((seq, width), bf16)]
        + [pltpu.VMEM((width, width), bf16)] * 3
        + [pltpu.SemaphoreType.DMA((3,))],
        compiler_params=kernel_params(28),
        cost_estimate=cost(rows * 8e9, 24e6, rows * H * seq * keys),
        name="attn_bwd",
    )(*toks, q_t, k, v, lse, da_t, comp_t, live_col, *in_hbm(wq, wk, wv), dh1, *after)


class Places:
    def __init__(self, n_dp, n_krow):
        self.x = n_krow // 2
        self.y = n_krow // 2
        self.z = n_dp // self.y
        self.dp = n_dp

    def shape(self, rows, cols):
        return (2, 2, self.z, rows, cols)

    def put(self, out, x, y, z, block, cut, low, high):
        out[x, y, z, low : low + cut] = block[:cut]
        out[y, x, z, high : high + block.shape[0] - cut] = block[cut:]


def down_grad(places, other, cut, ids, d_t, act, after=()):
    width, tokens = d_t.shape
    rows, seq, ff = act.shape
    cols = ff // (2 * places.x)
    height = width // places.dp
    shape = places.shape(height, cols)

    def kernel(ids, d_ref, act_ref, *refs):
        xr = pl.program_id(0)
        res = nn(d_ref[...], act_ref[...].reshape(rows * seq, cols)).astype(bf16)
        for z in range(places.z):
            for y in range(places.y):
                d = z * places.y + y
                block = res[d * height : (d + 1) * height, :]
                places.put(refs[-1], xr, ids[1] ^ y, ids[2] ^ z, block, cut, 0, cut)

    return pl.pallas_call(
        kernel,
        grid_spec=pltpu.PrefetchScalarGridSpec(
            num_scalar_prefetch=1,
            grid=(places.x,),
            in_specs=[
                whole((width, tokens)),
                pl.BlockSpec(
                    (rows, seq, cols), lambda i, ids: (0, 0, 2 * (ids[3] ^ i) + (ids[0] ^ other))
                ),
            ]
            + anywhere(after),
            out_specs=whole(shape),
        ),
        out_shape=jax.ShapeDtypeStruct(shape, bf16),
        compiler_params=kernel_params(16),
        cost_estimate=cost(width * tokens * ff, 8e6),
        name="down_grad",
    )(ids, d_t, act, *after)


def up_grad(places, other, cuts, ids, nl_t, dup, br_t, att, after=()):
    width, tokens = nl_t.shape
    rows, seq, ff = dup.shape
    krows = width // (2 * places.x)
    cols = ff // places.dp
    half = width // (2 * places.dp)
    step = cols * places.y
    cut_up, cut_out = cuts
    shape = places.shape(krows + half, cols)
    cut = cut_up + cut_out

    def kernel(ids, nl_ref, dup_ref, br_ref, att_ref, *refs):
        out, g_bu = refs[-9], refs[-8]
        lhs, temp, att_vm, nl_sems, br_sems, att_sem, _ = refs[-7:]
        zr = pl.program_id(0)

        @pl.when(zr == 0)
        def _():
            copies = []
            for x in range(places.x):
                first = pl.multiple_of((2 * x + (ids[0] ^ other)) * krows, 16)
                copies.append(
                    pltpu.make_async_copy(
                        nl_ref.at[pl.ds(first, krows), :],
                        lhs.at[x * krows : (x + 1) * krows, :],
                        nl_sems.at[x],
                    )
                )
                copies[-1].start()
            fetch_strips(br_ref, temp, br_sems, ids, other, half, places.dp)
            pltpu.make_async_copy(att_ref, att_vm, att_sem).start()
            lhs[places.x * krows :, :] = jnp.ones((16, tokens), bf16)
            for copy in copies:
                copy.wait()

        res = nn(lhs[...], dup_ref[...].reshape(tokens, step))
        g_bu[...] = res[places.x * krows : places.x * krows + 8]
        res = res.astype(bf16)
        for x in range(places.x):
            for y in range(places.y):
                block = res[x * krows : (x + 1) * krows, y * cols : (y + 1) * cols]
                places.put(out, ids[3] ^ x, ids[1] ^ y, zr, block, cut_up, 0, cut)

        @pl.when(zr == places.z - 1)
        def _():
            pltpu.make_async_copy(att_ref, att_vm, att_sem).wait()
            for d in range(places.dp):
                pltpu.make_async_copy(
                    br_ref.at[d * half : (d + 1) * half, :],
                    temp.at[d * half : (d + 1) * half, :],
                    br_sems.at[d],
                ).wait()
            res = nn(temp[...], att_vm[...].reshape(tokens, width)).astype(bf16)
            for z in range(places.z):
                for y in range(places.y):
                    d = z * places.y + y
                    for x in range(places.x):
                        block = res[d * half : (d + 1) * half, x * cols : (x + 1) * cols]
                        places.put(
                            out, ids[3] ^ x, ids[1] ^ y, ids[2] ^ z, block, cut_out,
                            cut_up, cut + krows - cut_up,
                        )

    return pl.pallas_call(
        kernel,
        grid_spec=pltpu.PrefetchScalarGridSpec(
            num_scalar_prefetch=1,
            grid=(places.z,),
            in_specs=[
                pl.BlockSpec(memory_space=pl.ANY),
                pl.BlockSpec((rows, seq, step), lambda i, ids: (0, 0, ids[2] ^ i)),
                pl.BlockSpec(memory_space=pl.ANY),
                pl.BlockSpec(memory_space=pl.ANY),
            ]
            + anywhere(after),
            out_specs=[whole(shape)]
            + [pl.BlockSpec((8, step), lambda i, ids: (0, ids[2] ^ i))],
            scratch_shapes=[
                pltpu.VMEM((places.x * krows + 16, tokens), bf16),
                pltpu.VMEM((width // 2, tokens), bf16),
                pltpu.VMEM(att.shape, bf16),
                pltpu.SemaphoreType.DMA((places.x,)),
                pltpu.SemaphoreType.DMA((places.dp,)),
                pltpu.SemaphoreType.DMA,
                pltpu.VMEM((8, 128), f32),
            ],
        ),
        out_shape=[jax.ShapeDtypeStruct(shape, bf16)]
        + [jax.ShapeDtypeStruct((8, ff), f32)],
        compiler_params=kernel_params(18),
        cost_estimate=cost(width * tokens * (ff + width), 12e6),
        name="up_grad",
    )(ids, nl_t, dup, br_t, att, *after)


def square_grad(places, other, cut, ids, d_ts, sources, small, length, sums, after=()):
    n_rows, width, _ = d_ts[0].shape
    half = width // (2 * places.dp)
    cols = width // places.x
    count = len(d_ts)
    _, seq, keys = small.shape
    s_half, s_cols = seq // (2 * places.dp), keys // places.x
    extra = s_half // 2
    shape = places.shape(count * half + extra, cols)
    flat_s = [p for source in sources for p, _ in source]
    specs = [
        pl.BlockSpec((1,) + p.shape[1:], lambda i, ids, own=own: (own, 0, 0))
        for source in sources
        for p, own in source
    ]
    split = len(sources[0])
    index = [range(split)] + [range(split, len(flat_s))] * (count - 1)
    n_sums = len(sums)
    sum_specs = [whole(v.shape) for v in sums]
    lengths = [n_rows * d.shape[2] for d in d_ts]
    n_out = 2 if sums else 1
    after = list(after)

    def kernel(ids, *refs):
        d_refs, refs = refs[:count], refs[count:]
        s_refs, refs = refs[: len(flat_s)], refs[len(flat_s) :]
        small_ref, refs = refs[0], refs[1:]
        parts, refs = refs[:n_sums], refs[n_sums + len(after) :]
        outs, refs = refs[:n_out], refs[n_out:]
        lhs, (rhs, total, sems) = refs[:count], refs[count:]
        copies = []
        for m in range(count):
            copies.append([])
            start = 0
            for r in range(n_rows):
                src = d_refs[m]
                for d in range(places.dp):
                    first = pl.multiple_of(2 * half * d + half * (ids[0] ^ other), 16)
                    copy = pltpu.make_async_copy(
                        src.at[r, pl.ds(first, half), :],
                        lhs[m].at[d * half : (d + 1) * half, start : start + src.shape[2]],
                        sems.at[m, r, d],
                    )
                    copy.start()
                    copies[-1].append(copy)
                start += src.shape[2]
        total[...] = total_of([small_ref[r] for r in range(n_rows)])
        for i in range(seq // length):
            for j in range(length // (2 * s_half)):
                d = (ids[4] ^ i) * (length // (2 * s_half)) + j
                yr, zr = ids[1] ^ (d % places.y), ids[2] ^ (d // places.y)
                first = i * length + 2 * s_half * j + s_half * (ids[0] ^ other)
                block = total[pl.ds(pl.multiple_of(first, 16), s_half), :].astype(bf16)
                for x in range(places.x):
                    for part in range(2):
                        outs[0][
                            yr,
                            ids[3] ^ x,
                            zr,
                            count * half :,
                            part * s_cols : (part + 1) * s_cols,
                        ] = block[part * extra : (part + 1) * extra, x * s_cols : (x + 1) * s_cols]
        if sums:
            g_bq, one, two, g_bu = parts
            vec = outs[1]
            acc = total_of([g_bq[r] for r in range(n_rows)])
            vec[...] = jnp.zeros(vec.shape, f32)
            vec[0:1, :] = acc
            vec[1:4, :] = one[0:3, :]
            vec[4:7, :] = two[0:3, :]
            for i in range(g_bu.shape[1] // width):
                vec[7 + i : 8 + i, :] = g_bu[0:1, i * width : (i + 1) * width]
        for m in range(count):
            start = 0
            for i in index[m]:
                rhs[start : start + s_refs[i].shape[1], :] = s_refs[i][0]
                start += s_refs[i].shape[1]
            for copy in copies[m]:
                copy.wait()
            res = nn(lhs[m][...], rhs[:start, :]).astype(bf16)
            for z in range(places.z):
                for y in range(places.y):
                    d = z * places.y + y
                    for x in range(places.x):
                        block = res[d * half : (d + 1) * half, x * cols : (x + 1) * cols]
                        places.put(
                            outs[0], ids[3] ^ x, ids[1] ^ y, ids[2] ^ z, block, cut,
                            m * cut, count * cut + m * (half - cut),
                        )

    return pl.pallas_call(
        kernel,
        grid_spec=pltpu.PrefetchScalarGridSpec(
            num_scalar_prefetch=1,
            grid=(1,),
            in_specs=anywhere(d_ts) + specs + [whole(small.shape)] + sum_specs + anywhere(after),
            out_specs=[whole(shape)] + ([whole((16, width))] if sums else []),
            scratch_shapes=[pltpu.VMEM((width // 2, n), bf16) for n in lengths]
            + [
                pltpu.VMEM((max(lengths), width), bf16),
                pltpu.VMEM((seq, keys), f32),
                pltpu.SemaphoreType.DMA((count, n_rows, places.dp)),
            ],
        ),
        out_shape=[jax.ShapeDtypeStruct(shape, bf16)]
        + ([jax.ShapeDtypeStruct((16, width), f32)] if sums else []),
        compiler_params=kernel_params(16),
        cost_estimate=cost(2.2e9, 12e6),
        name="square_grad",
    )(ids, *d_ts, *flat_s, small, *sums, *after)


def gather_rows(ids, parts, after=()):
    n = len(parts)
    rows, length, width = parts[0].shape

    def kernel(ids, *refs):
        out = refs[-1]
        for i in range(n):

            @pl.when(pl.program_id(0) == i)
            def _():
                out[...] = refs[i][...].astype(f32)

    spec = whole((rows, length, width))
    return pl.pallas_call(
        kernel,
        grid_spec=pltpu.PrefetchScalarGridSpec(
            num_scalar_prefetch=1,
            grid=(n,),
            in_specs=[spec] * n + anywhere(after),
            out_specs=pl.BlockSpec((rows, length, width), lambda i, ids: (ids[4] ^ i, 0, 0)),
        ),
        out_shape=jax.ShapeDtypeStruct((n * rows, length, width), f32),
        compiler_params=kernel_params(10),
        cost_estimate=cost(0, 6 * n * rows * length * width),
        name="gather_rows",
    )(ids, *parts, *after)


def exchange(value, axis, size, relative):
    pairs = [(i, i ^ relative) for i in range(size)]
    return lax.ppermute(value, axis, pairs)


def total_of(parts):
    acc = parts[0].astype(f32)
    for part in parts[1:]:
        acc = acc + part.astype(f32)
    return acc


def call(name, kernel, grid, ins, specs, outs, out_specs, after=(), scratch=()):
    def wrapped(*refs):
        kernel(*refs[: len(ins)], *refs[len(ins) + len(after) :])

    moved = sum(math.prod(shape) * 8 for shape, _ in outs)
    return pl.pallas_call(
        wrapped,
        grid=grid,
        in_specs=list(specs) + anywhere(after),
        out_specs=out_specs,
        out_shape=[jax.ShapeDtypeStruct(shape, dt) for shape, dt in outs],
        scratch_shapes=list(scratch),
        compiler_params=kernel_params(8),
        cost_estimate=cost(moved, moved),
        name=name,
    )(*ins, *after)


class Reduction:
    def __init__(self, places, n_dp, n_krow, cut):
        self.places, self.n_dp, self.n_krow, self.cut = places, n_dp, n_krow, cut

    def along(self, axis, value, relative):
        if axis == "x":
            return exchange(value, "krow", self.n_krow, 2 * relative)
        if axis == "y":
            return exchange(value, "dp", self.n_dp, relative)
        return exchange(value, "dp", self.n_dp, relative * self.places.y)

    def core(self, send):
        self.came = exchange(send, "krow", self.n_krow, 1)

    def first(self, keep, after=()):
        self.keep = keep
        _, _, nz, rows, cols = keep.shape
        cut = self.cut
        self.heights = (cut, rows - cut)

        def kernel(k, c, first, second):
            total = total_of([k[0], c[0]]).astype(bf16)
            first[...] = total[:, :, :cut]
            second[...] = total[:, :, cut:]

        spec = pl.BlockSpec((1, 2, 1, rows, cols), lambda z: (1, 0, z, 0, 0))
        res = call(
            "first_sum", kernel, (nz,), [keep, self.came], [spec] * 2,
            [((2, nz, h, cols), bf16) for h in self.heights],
            [pl.BlockSpec((2, 1, h, cols), lambda z: (0, z, 0, 0)) for h in self.heights],
            after,
        )
        self.one = [self.along(axis, r, 1) for axis, r in zip("xy", res)]
        return res

    def second(self, after=()):
        _, _, nz, rows, cols = self.keep.shape
        cut = self.cut

        def kernel(k, c, g, h, first, second):
            first[0] = total_of([k[0, 0, 0, :cut], c[0, 0, 0, :cut], g[0, 0]]).astype(bf16)
            second[0] = total_of([k[0, 0, 0, cut:], c[0, 0, 0, cut:], h[0, 0]]).astype(bf16)

        spec = pl.BlockSpec((1, 1, 1, rows, cols), lambda z: (0, 1, z, 0, 0))
        res = call(
            "second_sum", kernel, (nz,), [self.keep, self.came] + self.one,
            [spec] * 2
            + [pl.BlockSpec((1, 1, h, cols), lambda z: (1, z, 0, 0)) for h in self.heights],
            [((nz, h, cols), bf16) for h in self.heights],
            [pl.BlockSpec((1, h, cols), lambda z: (z, 0, 0)) for h in self.heights],
            after,
        )
        self.two = [self.along(axis, r, 1) for axis, r in zip("yx", res)]
        return res

    def third(self, after=()):
        _, _, nz, rows, cols = self.keep.shape
        cut = self.cut

        def kernel(k, c, g1, h1, g2, h2, odd, even):
            for z in range(nz):
                out = odd if z % 2 else even
                for part, one, two in ((slice(0, cut), g1, g2), (slice(cut, rows), h1, h2)):
                    value = total_of([k[0, 0, z, part], c[0, 0, z, part], one[0, z], two[z]])
                    out[z // 2, part, :] = value.astype(out.dtype)

        shape = (nz // 2, rows, cols)
        spec = pl.BlockSpec((1, 1, nz, rows, cols), lambda i: (0, 0, 0, 0, 0))
        odd, self.even = call(
            "third_sum", kernel, (1,), [self.keep, self.came] + self.one + self.two,
            [spec] * 2
            + [pl.BlockSpec((1, nz, h, cols), lambda i: (0, 0, 0, 0)) for h in self.heights]
            + [pl.BlockSpec((nz, h, cols), lambda i: (0, 0, 0)) for h in self.heights],
            [(shape, bf16), (shape, f32)], [whole(shape)] * 2, after,
        )
        self.three = self.along("z", odd, 1)
        return [odd]

    def fourth(self, after=()):
        _, rows, cols = self.even.shape

        def kernel(e, g, send, mine):
            send[...] = total_of([e[1], g[1]]).astype(bf16)
            mine[...] = total_of([e[0], g[0]])

        shape = (rows, cols)
        send, mine = call(
            "fourth_sum", kernel, (1,), [self.even, self.three], [whole(self.even.shape)] * 2,
            [(shape, bf16), (shape, f32)], [whole(shape)] * 2, after,
        )
        self.terms = [mine, self.along("z", send, 2)]
        return [send]


def finish_down(red, after=()):
    rows, cols = red.terms[0].shape
    n = len(red.terms)

    def kernel(*refs):
        refs[n][...] = total_of([r[...] for r in refs[:n]]).T

    return call(
        "finish_down", kernel, (1,), red.terms, [whole((rows, cols))] * n,
        [((cols, rows), f32)], [whole((cols, rows))], after,
    )


def finish_up(red, cuts, krows, half, after=()):
    rows, cols = red.terms[0].shape
    n = len(red.terms)
    cut_up, cut_out = cuts
    rest = krows - cut_up

    def kernel(*refs):
        up, out = refs[n], refs[n + 1]
        total = total_of([r[...] for r in refs[:n]])
        low = cut_up + cut_out
        up[:cut_up] = total[:cut_up]
        up[cut_up:] = total[low : low + rest]
        out[:cut_out] = total[cut_up:low]
        out[cut_out:] = total[low + rest :]

    shapes = [(krows, cols), (half, cols)]
    return call(
        "finish_up", kernel, (1,), red.terms, [whole((rows, cols))] * n,
        [(shape, f32) for shape in shapes], [whole(shape) for shape in shapes], after,
    )


def finish_square(red, ids, out_rows, cut, half, count, s_cols, after=()):
    rows, cols = red.terms[0].shape
    n = len(red.terms)
    extra = rows - count * half
    mine_cols = cols // 2
    height = (count + 1) * half + 2 * extra

    def kernel(ids, out_ref, *refs):
        terms, (mine, other, temp) = refs[:n], refs[n:]
        total = total_of([r[...] for r in terms])
        rest = half - cut
        temp[:half] = out_ref[...]
        for m in range(count):
            at = half * (m + 1)
            temp[at : at + cut] = total[m * cut : (m + 1) * cut]
            low = count * cut + m * rest
            temp[at + cut : at + half] = total[low : low + rest]
        core = ids[0]
        square = (count + 1) * half
        lo, hi = temp[:square, :mine_cols], temp[:square, mine_cols:]
        mine[:square, :] = jnp.where(core == 0, lo, hi)
        other[:square, :] = jnp.where(core == 0, hi, lo).astype(bf16)
        h = s_cols // 2
        mine[square:, :] = jnp.zeros((2 * extra, mine_cols), f32)
        other[square:, :] = jnp.zeros((2 * extra, mine_cols), bf16)
        for part in range(2):
            tail = total[count * half :, part * s_cols : (part + 1) * s_cols]
            at = square + part * extra
            lo, hi = tail[:, :h], tail[:, h:]
            mine[at : at + extra, :h] = jnp.where(core == 0, lo, hi)
            other[at : at + extra, :h] = jnp.where(core == 0, hi, lo).astype(bf16)

    return call(
        "finish_square", kernel, (1,), [ids, out_rows] + red.terms,
        [pl.BlockSpec(memory_space=pltpu.SMEM), whole(out_rows.shape)]
        + [whole((rows, cols))] * n,
        [((height, mine_cols), f32), ((height, mine_cols), bf16)],
        [whole((height, mine_cols))] * 2,
        after,
        [pltpu.VMEM(((count + 1) * half, cols), f32)],
    )


def finish_vectors(vec, ff, after=()):
    width = vec.shape[1]
    sizes = (width,) * 7 + (ff,)

    def kernel(v, *pieces):
        for i in range(7):
            pieces[i][...] = v[i, :]
        for i in range(ff // width):
            pieces[7][i * width : (i + 1) * width] = v[7 + i, :]

    return call(
        "finish_vectors", kernel, (1,), [vec], [whole(vec.shape)],
        [((size,), f32) for size in sizes], [whole((size,)) for size in sizes], after,
    )


def finish_columns(ids, mine, there, half, count, extra, s_half_cols):
    mine_cols = mine.shape[1]
    square = count * half

    def kernel(ids, mine, there, *refs):
        outs, temp = refs[:-1], refs[-1]
        core = ids[0]

        def merge(at, height, cols, out):
            a, b = mine[at : at + height, :cols], there[at : at + height, :cols].astype(f32)
            low, high = jnp.where(core == 0, a, b), jnp.where(core == 0, b, a)
            out[...] = jnp.concatenate([low, high], axis=0).T

        for m in range(count):
            merge(m * half, half, mine_cols, outs[m])
        merge(square, 2 * extra, s_half_cols, outs[count])

    shapes = [(mine_cols, 2 * half)] * count + [(s_half_cols, 4 * extra)]
    return call(
        "finish_columns", kernel, (1,), [ids, mine, there],
        [pl.BlockSpec(memory_space=pltpu.SMEM), whole(mine.shape), whole(there.shape)],
        [(shape, f32) for shape in shapes], [whole(shape) for shape in shapes],
        (), [pltpu.VMEM((8, 128), f32)],
    )


def local(
    sizes,
    tokens,
    segment_ids,
    segment_live,
    w_query,
    b_query,
    w_key,
    w_value,
    w_out,
    b_out,
    attn_gain,
    attn_shift,
    w_up,
    b_up,
    w_down,
    b_down,
    ffn_gain,
    ffn_shift,
    compress,
    cotangent,
):
    n_dp, n_krow = sizes
    all_rows, length, width = tokens.shape
    rows = all_rows // n_krow
    seq = n_krow * length
    keys = compress.shape[0]
    ff = w_up.shape[1]
    krow, dp = lax.axis_index("krow"), lax.axis_index("dp")
    places = Places(n_dp, n_krow)
    ids = jnp.stack([krow % 2, dp % places.y, dp // places.y, krow // 2, krow]).astype(jnp.int32)
    fast = (
        width % (2 * places.x * 32) == 0
        and ff % (n_dp * 128) == 0
        and ff % (n_krow * 128) == 0
        and width % (2 * n_dp * 16) == 0
        and seq % (2 * n_dp * 32) == 0
        and width % (places.x * 128) == 0
        and keys % (places.x * 128) == 0
        and length % (seq // n_dp) == 0
        and ff // n_dp == width // places.x
        and 2 * (keys // places.x) <= width // places.x
        and places.x == 2
        and places.y == 2
        and places.z == 4
        and rows > 1
    )

    def spread(value):
        parts = []
        for r in range(n_krow):
            part = lax.dynamic_slice_in_dim(value, (krow ^ r) * rows, rows, 0)
            parts.append(exchange(part, "krow", n_krow, r) if r else part)
        return parts

    def back(parts):
        return [exchange(part, "krow", n_krow, r) if r else part for r, part in enumerate(parts)]

    def row(value):
        return value.astype(f32).reshape(1, -1)

    toks = spread(tokens)
    cot_source = lax.optimization_barrier((cotangent, toks[-1]))[0]
    cots = spread(cot_source)

    my_ids = lax.dynamic_slice_in_dim(segment_ids, krow * rows, rows, 0)
    my_live = lax.dynamic_slice_in_dim(segment_live, krow * rows, rows, 0)
    labels = jnp.arange(segment_live.shape[1], dtype=jnp.int32)
    live = jnp.sum(
        jnp.where(my_ids[:, :, None] == labels, my_live[:, None, :], 0).astype(f32), axis=-1
    )

    def relative(value, axis):
        return jnp.concatenate(
            [
                lax.dynamic_slice_in_dim(value, (krow ^ r) * length, length, axis)
                for r in range(n_krow)
            ],
            axis=axis,
        )

    live = relative(live, 1)
    comp = relative(compress, 1)
    live_row = live[:, None, :]
    live_col = jnp.broadcast_to(live[:, :, None], (rows, seq, 128))
    comp_t = comp.T
    gain, shift = row(attn_gain), row(attn_shift)

    q_t, pk, k, v, lse, att, xhat, rstd = attn_fwd(
        toks, live_row, comp, w_query, row(b_query), w_key, w_value, w_out, row(b_out)
    )
    res = ffn_fwd(
        cots, xhat, gain, shift, w_up, row(b_up), w_down, row(b_down), row(ffn_gain), row(ffn_shift)
    )
    outs, (act, gp, dh2, d_t, sums_two) = res[:n_krow], res[n_krow:]
    out_parts = back(outs)
    ahead = []
    if fast:
        cut_down = 32
        cuts_up = (width // n_krow // 2, 16)
        cut_square = 16
        half = width // (2 * n_dp)
        down = Reduction(places, n_dp, n_krow, cut_down)
        up = Reduction(places, n_dp, n_krow, sum(cuts_up))
        square = Reduction(places, n_dp, n_krow, 3 * cut_square)
        send = down_grad(places, 1, cut_down, ids, d_t, act)
        down.core(send)
        keep = down_grad(places, 0, cut_down, ids, d_t, act, after=[send])
        ahead = list(down.first(keep))

    dup, dh1, da_t, nl_t, br_t, sums_one = ffn_bwd(
        gp, dh2, xhat, rstd, gain, shift, w_up, w_down, w_out, after=ahead
    )

    if fast:
        ahead = down.second([nl_t] + list(out_parts))
        send, _ = up_grad(places, 1, cuts_up, ids, nl_t, dup, br_t, att, after=ahead)
        up.core(send)
        keep, g_bu = up_grad(places, 0, cuts_up, ids, nl_t, dup, br_t, att, after=[send])
        ahead = up.first(keep)
        ahead = down.third(ahead)

    res = attn_bwd(
        toks, q_t, k, v, lse, da_t, comp_t, live_col, w_query, w_key, w_value, dh1, after=ahead
    )
    grad_parts, bwd = res[:n_krow], res[n_krow:]

    if fast:
        sources = [[(t, r) for r in range(rows) for t in toks], [(pk, r) for r in range(rows)]]
        ahead = up.second([bwd[0], down.three])
        ahead = down.fourth(ahead)
        send, vec = square_grad(
            places, 1, cut_square, ids, bwd[:3], sources, bwd[4], length,
            [bwd[3], sums_one, sums_two, g_bu], after=ahead,
        )
        square.core(send)
        got = exchange(vec, "krow", n_krow, 1)
        (keep,) = square_grad(
            places, 0, cut_square, ids, bwd[:3], sources, bwd[4], length, [], after=[send]
        )
        vec = vec + got
        ahead = up.third([keep, vec])
        ahead = square.first(keep, ahead)
        vec = vec + square.along("x", vec, 1)
        grad_parts = back(lax.optimization_barrier((grad_parts, ahead))[0])
        ahead = up.fourth([vec, *ahead])
        vec = vec + square.along("y", vec, 1)
        ahead = square.second([vec, *ahead])
        output = gather_rows(ids, out_parts, after=ahead)
        (g_down,) = finish_down(down, after=[output])
        vec = vec + square.along("z", vec, 1)
        ahead = square.third([vec, g_down])
        g_up, out_rows = finish_up(up, cuts_up, width // n_krow, half, after=ahead)
        vec = vec + square.along("z", vec, 2)
        ahead = square.fourth([vec, out_rows])
        pieces = finish_vectors(vec, ff, after=ahead)
        grad_tokens = gather_rows(ids, grad_parts, after=pieces[:1])
        s_cols = keys // places.x
        mine, other = finish_square(
            square, ids, out_rows, cut_square, half, 3, s_cols, after=[grad_tokens]
        )
        there = exchange(other, "krow", n_krow, 1)
        g_out, g_q, g_k, g_v, g_comp = finish_columns(
            ids, mine, there, half, 4, seq // (4 * n_dp), s_cols // 2
        )
    else:
        grad_parts = back(grad_parts)
        g_bu = jnp.sum(dup.astype(f32), axis=(0, 1)).reshape(-1, width)
        g_bq = jnp.sum(bwd[3], axis=0)
        vectors = jnp.concatenate([g_bq, sums_one[:3], sums_two[:3], g_bu], axis=0)
        output = gather_rows(ids, out_parts)
        grad_tokens = gather_rows(ids, grad_parts)
        vectors = lax.psum(vectors.reshape(-1), ("dp", "krow"))
        pieces = []
        start = 0
        for size in (width,) * 7 + (ff,):
            pieces.append(vectors[start : start + size])
            start += size

        def scattered(value):
            value = value.astype(bf16)
            part = lax.psum_scatter(value, "krow", scatter_dimension=0, tiled=True)
            return lax.psum_scatter(part, "dp", scatter_dimension=1, tiled=True).astype(f32)

        def product(a, b):
            return lax.dot_general(a, b, (((1,), (0,)), ((), ())), preferred_element_type=f32)

        token_rows = jnp.concatenate(toks, axis=1)
        d_q, d_k, d_v = [jnp.swapaxes(d, 0, 1).reshape(width, -1) for d in bwd[:3]]
        pk = pk.reshape(-1, width)
        g_q = scattered(product(d_q, token_rows.reshape(-1, width)).T)
        g_k = scattered(product(d_k, pk).T)
        g_v = scattered(product(d_v, pk).T)
        g_out = scattered(product(br_t, att.reshape(-1, width)).T)
        g_up = scattered(product(nl_t, dup.reshape(-1, ff)))
        g_down = scattered(product(d_t, act.reshape(-1, ff)).T)
        blocks = jnp.sum(bwd[4].astype(f32), axis=0).reshape(n_krow, length, keys)
        blocks = jnp.concatenate(
            [lax.dynamic_slice_in_dim(blocks, krow ^ r, 1, 0) for r in range(n_krow)]
        )
        g_comp = scattered(blocks.reshape(seq, keys).T)

    g_bq, g_gain, g_shift, g_bo, g_fgain, g_fshift, g_bd, g_bu = pieces
    return (
        output,
        grad_tokens,
        g_q,
        g_bq,
        g_k,
        g_v,
        g_out,
        g_bo,
        g_gain,
        g_shift,
        g_up,
        g_bu,
        g_down,
        g_bd,
        g_fgain,
        g_fshift,
        g_comp,
    )


def solution(mesh):
    rows = P("dp", "krow", None)
    per_row = P("dp", None)
    block = P("krow", "dp")
    in_specs = (rows, per_row, per_row) + (P(),) * 15 + (rows,)
    out_specs = (
        (rows, rows, block, P(), block, block, block)
        + (P(),) * 3
        + (block, P(), block)
        + (P(),) * 3
        + (block,)
    )
    sizes = (mesh.shape["dp"], mesh.shape["krow"])
    return jax.shard_map(
        functools.partial(local, sizes),
        mesh=mesh,
        in_specs=in_specs,
        out_specs=out_specs,
        check_vma=False,
    )
```

```python
import functools
import math

import jax
import jax.numpy as jnp
from jax import lax
from jax.experimental import pallas as pl
from jax.experimental.pallas import tpu as pltpu
from jax.sharding import PartitionSpec as P

H = 12
HD = 64
f32 = jnp.float32
bf16 = jnp.bfloat16


def nn(a, b):
    return lax.dot_general(a, b, (((1,), (0,)), ((), ())), preferred_element_type=f32)


def nt(a, b):
    return lax.dot_general(a, b, (((1,), (1,)), ((), ())), preferred_element_type=f32)


def whole(shape):
    rank = len(shape)
    return pl.BlockSpec(shape, lambda *_: (0,) * rank, pipeline_mode=pl.Buffered(1))


def fetch_strips(src, dst, sems, ids, other, half, dp):
    copies = []
    for d in range(dp):
        first = pl.multiple_of(2 * half * d + half * (ids[0] ^ other), 16)
        copies.append(
            pltpu.make_async_copy(
                src.at[pl.ds(first, half), :], dst.at[d * half : (d + 1) * half, :], sems.at[d]
            )
        )
        copies[-1].start()
    return copies


def resident():
    return pl.BlockSpec(memory_space=pltpu.VMEM)


def out_hbm(shape, dtype):
    return pltpu.HBM(shape, dtype)


def in_hbm(*values):
    return [pltpu.with_memory_space_constraint(v, pltpu.HBM) for v in values]


def fetch(sources, places, sems):
    copies = [
        pltpu.make_async_copy(src, dst, sems.at[i])
        for i, (src, dst) in enumerate(zip(sources, places))
    ]

    @pl.when(pl.program_id(0) == 0)
    def _():
        for copy in copies:
            copy.start()

    def wait(*which):
        @pl.when(pl.program_id(0) == 0)
        def _():
            for i in which:
                copies[i].wait()

    return wait


def anywhere(values):
    return [pl.BlockSpec(memory_space=pl.ANY)] * len(values)


def row_block(*shape):
    rank = len(shape)
    return pl.BlockSpec((1,) + shape, lambda r, *_: (r,) + (0,) * rank)


def kernel_params(mebibytes):
    return pltpu.CompilerParams(dimension_semantics=("arbitrary",), vmem_limit_bytes=mebibytes * 1024 * 1024)


def cost(flops, moved, trans=0):
    return pl.CostEstimate(flops=int(flops), bytes_accessed=int(moved), transcendentals=int(trans))


def add_to(ref, value, first):
    @pl.when(first)
    def _():
        ref[...] = value

    @pl.when(jnp.logical_not(first))
    def _():
        ref[...] += value


def col_sum(value):
    return jnp.sum(value, axis=0, keepdims=True)


def gelu_parts(u):
    phi = 0.5 + 0.5 * lax.erf(u * (1.0 / math.sqrt(2.0)))
    density = jnp.exp(-0.5 * u * u) * (1.0 / math.sqrt(2.0 * math.pi))
    return u * phi, phi + u * density


def attn_fwd_kernel(n, *refs):
    toks = refs[:n]
    live, comp, wq_hbm, bq, wk_hbm, wv_hbm, wo_hbm, bo = refs[n : n + 8]
    q_t, pk, k, v, lse, att, xhat, rstd = refs[n + 8 : n + 16]
    tok, att_t, wq, wk, wv, wo, sems = refs[n + 16 :]
    wait = fetch((wq_hbm, wk_hbm, wv_hbm, wo_hbm), (wq, wk, wv, wo), sems)
    length = toks[0].shape[1]
    for i in range(n):
        tok[i * length : (i + 1) * length, :] = toks[i][0]
    masked = (comp[...].astype(f32) * live[0]).astype(bf16)
    x = tok[...]
    pk[0] = nn(masked, x).astype(bf16)
    wait(0, 1, 2)
    for c in range(3):
        cols = slice(256 * c, 256 * c + 256)
        q = (nn(x, wq[:, cols]) + bq[:, cols]).astype(bf16) * jnp.asarray(1.0 / math.sqrt(HD), bf16)
        q_t[0, cols, :] = q.T
        k[0, :, cols] = nn(pk[0], wk[:, cols]).astype(bf16)
        v[0, :, cols] = nn(pk[0], wv[:, cols]).astype(bf16)
    lane = lax.broadcasted_iota(jnp.int32, (1, 2 * HD), 1)
    for pair in range(H // 2):
        cols = slice(2 * HD * pair, 2 * HD * (pair + 1))
        k_pair = k[0, :, cols]
        v_t = v[0, :, cols].T
        for half in range(2):
            h = 2 * pair + half
            mine = jnp.where((lane // HD) == half, k_pair, jnp.zeros_like(k_pair))
            s = nn(mine, q_t[0, cols, :])
            top = jnp.max(s, axis=0, keepdims=True)
            e = jnp.exp(s - top)
            total = jnp.sum(e, axis=0, keepdims=True)
            w = (e * (1.0 / total)).astype(bf16)
            lse[0, h : h + 1, :] = top + jnp.log(total)
            att_t[h * HD : (h + 1) * HD, :] = nn(v_t[half * HD : (half + 1) * HD, :], w).astype(bf16)
    for c in range(3):
        cols = slice(256 * c, 256 * c + 256)
        att[0, :, cols] = att_t[cols, :].T
    wait(3)
    hidden = x.astype(f32) + nn(att[0], wo[...]) + bo[...]
    average = jnp.mean(hidden, axis=-1, keepdims=True)
    centred = hidden - average
    spread = jnp.mean(centred * centred, axis=-1, keepdims=True)
    r = lax.rsqrt(spread + 1e-05)
    xhat[0] = centred * r
    rstd[0] = jnp.broadcast_to(r, rstd.shape[1:])


def attn_fwd(toks, live, comp, wq, bq, wk, wv, wo, bo):
    rows, length, width = toks[0].shape
    n = len(toks)
    seq = n * length
    keys = comp.shape[0]
    in_specs = [row_block(length, width)] * n + [
        row_block(1, seq),
        whole((keys, seq)),
        pl.BlockSpec(memory_space=pl.ANY),
        whole((1, width)),
        pl.BlockSpec(memory_space=pl.ANY),
        pl.BlockSpec(memory_space=pl.ANY),
        pl.BlockSpec(memory_space=pl.ANY),
        whole((1, width)),
    ]
    outs = [
        ((width, seq), bf16),
        ((keys, width), bf16),
        ((keys, width), bf16),
        ((keys, width), bf16),
        ((16, seq), f32),
        ((seq, width), bf16),
        ((seq, width), f32),
        ((seq, 128), f32),
    ]
    return pl.pallas_call(
        functools.partial(attn_fwd_kernel, n),
        grid=(rows,),
        in_specs=in_specs,
        out_specs=[row_block(*shape) for shape, _ in outs],
        out_shape=[out_hbm((rows,) + shape, dt) for shape, dt in outs],
        scratch_shapes=[pltpu.VMEM((seq, width), bf16), pltpu.VMEM((width, seq), bf16)]
        + [pltpu.VMEM((width, width), bf16)] * 4
        + [pltpu.SemaphoreType.DMA((4,))],
        compiler_params=kernel_params(30),
        cost_estimate=cost(rows * 5e9, 12e6, rows * H * seq * keys),
        name="attn_fwd",
    )(*toks, live, comp, *in_hbm(wq), bq, *in_hbm(wk, wv, wo), bo)


def ffn_fwd_kernel(n, *refs):
    cots = refs[:n]
    xhat, gain, shift, wu, bu, wd, bd, fgain, fshift = refs[n : n + 9]
    refs = refs[n + 9 :]
    outs = refs[:n]
    act, gp, dh2, d_t, sums = refs[n:]
    r = pl.program_id(0)
    first = r == 0
    length = outs[0].shape[1]
    ff = wu.shape[1]
    chunk = 512
    count = ff // chunk
    normed = xhat[0] * gain[...] + shift[...]
    low = normed.astype(bf16)

    def up(c):
        cols = slice(c * chunk, (c + 1) * chunk)
        return nn(low, wu[:, cols]) + bu[:, cols]

    for c in range(count):
        cols = slice(c * chunk, (c + 1) * chunk)
        a, g = gelu_parts(up(c))
        act[r, :, cols] = a.astype(bf16)
        gp[0, :, cols] = g.astype(bf16)
    total = normed + bd[...] + nn(act[r], wd[...])
    average = jnp.mean(total, axis=-1, keepdims=True)
    centred = total - average
    spread = jnp.mean(centred * centred, axis=-1, keepdims=True)
    rs = lax.rsqrt(spread + 1e-05)
    hat = centred * rs
    result = (hat * fgain[...] + fshift[...]).astype(bf16)
    for i in range(n):
        outs[i][0] = result[i * length : (i + 1) * length, :]
    cot = jnp.concatenate([c[0] for c in cots], axis=0).astype(f32)
    dhat = cot * fgain[...]
    d = rs * (
        dhat
        - jnp.mean(dhat, axis=-1, keepdims=True)
        - hat * jnp.mean(dhat * hat, axis=-1, keepdims=True)
    )
    dh2[0] = d
    d_low = d.astype(bf16)
    seq = d_low.shape[0]
    d_t[:, pl.ds(pl.multiple_of(r * seq, seq), seq)] = d_low.T
    add_to(
        sums,
        jnp.concatenate(
            [col_sum(cot * hat), col_sum(cot), col_sum(d_low.astype(f32)), jnp.zeros((5, d.shape[1]), f32)],
            axis=0,
        ),
        first,
    )


def ffn_fwd(cots, xhat, gain, shift, wu, bu, wd, bd, fgain, fshift):
    rows, length, width = cots[0].shape
    n = len(cots)
    seq = n * length
    ff = wu.shape[1]
    vec = whole((1, width))
    in_specs = [row_block(length, width)] * n + [
        row_block(seq, width),
        vec,
        vec,
        resident(),
        whole((1, ff)),
        resident(),
        vec,
        vec,
        vec,
    ]
    outs = [((length, width), bf16)] * n
    more = [((seq, ff), bf16), ((seq, width), f32)]
    return pl.pallas_call(
        functools.partial(ffn_fwd_kernel, n),
        grid=(rows,),
        in_specs=in_specs,
        out_specs=[row_block(*shape) for shape, _ in outs]
        + [resident()]
        + [row_block(*shape) for shape, _ in more]
        + [resident()]
        + [whole((8, width))],
        out_shape=[jax.ShapeDtypeStruct((rows,) + shape, dt) for shape, dt in outs]
        + [pltpu.VMEM((rows, seq, ff), bf16)]
        + [jax.ShapeDtypeStruct((rows,) + shape, dt) for shape, dt in more]
        + [jax.ShapeDtypeStruct((width, rows * seq), bf16)]
        + [jax.ShapeDtypeStruct((8, width), f32)],
        compiler_params=kernel_params(26),
        cost_estimate=cost(rows * seq * width * ff * 4, 34e6, rows * seq * ff * 2),
        name="ffn_fwd",
    )(*cots, xhat, gain, shift, wu, bu, wd, bd, fgain, fshift)


def ffn_bwd_kernel(*refs):
    gp, dh2, xhat, rstd, gain, shift, wu, wd, wo = refs[:9]
    dup, dh1, da_t, nl_t, br_t, sums = refs[-6:]
    r = pl.program_id(0)
    first = r == 0
    ff = wu.shape[1]
    chunk = 512
    count = ff // chunk
    d_low = dh2[0].astype(bf16)

    def back(c):
        return nt(d_low, wd[c * chunk : (c + 1) * chunk, :])

    for c in range(count):
        cols = slice(c * chunk, (c + 1) * chunk)
        dup[r, :, cols] = (gp[0, :, cols].astype(f32) * back(c)).astype(bf16)
    tile = min(256, dh2.shape[1])
    for i in range(dh2.shape[1] // tile):
        part = slice(i * tile, (i + 1) * tile)
        for j in range(dh2.shape[2] // 256):
            cols = slice(j * 256, (j + 1) * 256)
            dh1[0, part, cols] = dh2[0, part, cols] + nt(dup[r, part, :], wu[cols, :])
    dn = dh1[0]
    hat = xhat[0]
    dhat = dn * gain[...]
    d = rstd[0, :, 0:1] * (
        dhat
        - jnp.mean(dhat, axis=-1, keepdims=True)
        - hat * jnp.mean(dhat * hat, axis=-1, keepdims=True)
    )
    dh1[0] = d
    branch = d.astype(bf16)
    add_to(
        sums,
        jnp.concatenate(
            [col_sum(dn * hat), col_sum(dn), col_sum(branch.astype(f32)), jnp.zeros((5, d.shape[1]), f32)],
            axis=0,
        ),
        first,
    )
    da_t[0] = nt(wo[...], branch).astype(bf16)
    br_t[...] = branch.T
    nl_t[...] = (hat * gain[...] + shift[...]).astype(bf16).T


def ffn_bwd(gp, dh2, xhat, rstd, gain, shift, wu, wd, wo, after=()):
    rows, seq, ff = gp.shape
    width = wu.shape[0]
    vec = whole((1, width))
    in_specs = [
        row_block(seq, ff),
        row_block(seq, width),
        row_block(seq, width),
        row_block(seq, 128),
        vec,
        vec,
        resident(),
        resident(),
        resident(),
    ] + anywhere(after)
    outs = [((seq, width), f32), ((width, seq), bf16)]
    turned = pl.BlockSpec((width, seq), lambda r: (0, r))
    return pl.pallas_call(
        ffn_bwd_kernel,
        grid=(rows,),
        in_specs=in_specs,
        out_specs=[resident()]
        + [row_block(*shape) for shape, _ in outs]
        + [turned] * 2
        + [whole((8, width))],
        out_shape=[pltpu.VMEM((rows, seq, ff), bf16)]
        + [jax.ShapeDtypeStruct((rows,) + shape, dt) for shape, dt in outs]
        + [jax.ShapeDtypeStruct((width, rows * seq), bf16)] * 2
        + [jax.ShapeDtypeStruct((8, width), f32)],
        compiler_params=kernel_params(26),
        cost_estimate=cost(rows * seq * width * ff * 4.5, 34e6),
        name="ffn_bwd",
    )(gp, dh2, xhat, rstd, gain, shift, wu, wd, wo, *after)


def attn_bwd_kernel(n, *refs):
    toks = refs[:n]
    q_t, k, v, lse, da_t, comp_t, live_col, wq_hbm, wk_hbm, wv_hbm, dh1 = refs[n : n + 11]
    refs = refs[-(n + 10) :]
    outs = refs[:n]
    dq_t, dk_t, dv_t, g_bq, small, tok, wq, wk, wv, sems = refs[n:]
    wait = fetch((wq_hbm, wk_hbm, wv_hbm), (wq, wk, wv), sems)
    length = toks[0].shape[1]
    for i in range(n):
        tok[i * length : (i + 1) * length, :] = toks[i][0]
    lane = lax.broadcasted_iota(jnp.int32, (1, 2 * HD), 1)
    scale = jnp.asarray(1.0 / math.sqrt(HD), f32)
    for pair in range(H // 2):
        cols = slice(2 * HD * pair, 2 * HD * (pair + 1))
        k_pair = k[0, :, cols]
        v_pair = v[0, :, cols]
        k_t = k_pair.T
        for half in range(2):
            h = 2 * pair + half
            head = slice(h * HD, (h + 1) * HD)
            mine = (lane // HD) == half
            s = nn(jnp.where(mine, k_pair, jnp.zeros_like(k_pair)), q_t[0, cols, :])
            w = jnp.exp(s - lse[0, h : h + 1, :])
            dw = nn(jnp.where(mine, v_pair, jnp.zeros_like(v_pair)), da_t[0, cols, :])
            dot = jnp.sum(w * dw, axis=0, keepdims=True)
            ds = (w * (dw - dot)).astype(bf16)
            dv_t[0, head, :] = nt(da_t[0, head, :], w.astype(bf16)).astype(bf16)
            dk_t[0, head, :] = nt(q_t[0, head, :], ds).astype(bf16)
            dq_t[0, head, :] = (nn(k_t[half * HD : (half + 1) * HD, :], ds) * scale).astype(bf16)
    wait(0, 1, 2)
    dp_t = (nn(wk[...], dk_t[0]) + nn(wv[...], dv_t[0])).astype(bf16)
    small[0] = (nn(tok[...], dp_t) * live_col[0, :, 0:1]).astype(bf16)
    masked = (comp_t[...].astype(f32) * live_col[0, :, 0:1]).astype(bf16)
    dq = dq_t[0].T
    g_bq[0] = col_sum(dq.astype(f32))
    grad = dh1[0] + nt(dq, wq[...]) + nt(masked, dp_t)
    for i in range(n):
        outs[i][0] = grad[i * length : (i + 1) * length, :].astype(bf16)


def attn_bwd(toks, q_t, k, v, lse, da_t, comp_t, live_col, wq, wk, wv, dh1, after=()):
    rows, length, width = toks[0].shape
    n = len(toks)
    seq = n * length
    keys = comp_t.shape[1]
    in_specs = (
        [row_block(length, width)] * n
        + [
            row_block(width, seq),
            row_block(keys, width),
            row_block(keys, width),
            row_block(16, seq),
            row_block(width, seq),
            whole((seq, keys)),
            row_block(seq, 128),
            pl.BlockSpec(memory_space=pl.ANY),
            pl.BlockSpec(memory_space=pl.ANY),
            pl.BlockSpec(memory_space=pl.ANY),
            row_block(seq, width),
        ]
        + anywhere(after)
    )
    outs = [((length, width), bf16)] * n + [
        ((width, seq), bf16),
        ((width, keys), bf16),
        ((width, keys), bf16),
        ((1, width), f32),
        ((seq, keys), bf16),
    ]
    return pl.pallas_call(
        functools.partial(attn_bwd_kernel, n),
        grid=(rows,),
        in_specs=in_specs,
        out_specs=[row_block(*shape) for shape, _ in outs],
        out_shape=[jax.ShapeDtypeStruct((rows,) + shape, dt) for shape, dt in outs],
        scratch_shapes=[pltpu.VMEM((seq, width), bf16)]
        + [pltpu.VMEM((width, width), bf16)] * 3
        + [pltpu.SemaphoreType.DMA((3,))],
        compiler_params=kernel_params(28),
        cost_estimate=cost(rows * 8e9, 24e6, rows * H * seq * keys),
        name="attn_bwd",
    )(*toks, q_t, k, v, lse, da_t, comp_t, live_col, *in_hbm(wq, wk, wv), dh1, *after)


class Places:
    def __init__(self, n_dp, n_krow):
        self.x = n_krow // 2
        self.y = n_krow // 2
        self.z = n_dp // self.y
        self.dp = n_dp

    def shape(self, rows, cols):
        return (2, 2, self.z, rows, cols)

    def put(self, out, x, y, z, block, cut, low, high):
        out[x, y, z, low : low + cut] = block[:cut]
        out[y, x, z, high : high + block.shape[0] - cut] = block[cut:]


def down_grad(places, other, cut, ids, d_t, act, after=()):
    width, tokens = d_t.shape
    rows, seq, ff = act.shape
    cols = ff // (2 * places.x)
    height = width // places.dp
    shape = places.shape(height, cols)

    def kernel(ids, d_ref, act_ref, *refs):
        xr = pl.program_id(0)
        start = pl.multiple_of((2 * (ids[3] ^ xr) + (ids[0] ^ other)) * cols, 128)
        block = act_ref[:, :, pl.ds(start, cols)].reshape(rows * seq, cols)
        res = nn(d_ref[...], block).astype(bf16)
        for z in range(places.z):
            for y in range(places.y):
                d = z * places.y + y
                block = res[d * height : (d + 1) * height, :]
                places.put(refs[-1], xr, ids[1] ^ y, ids[2] ^ z, block, cut, 0, cut)

    return pl.pallas_call(
        kernel,
        grid_spec=pltpu.PrefetchScalarGridSpec(
            num_scalar_prefetch=1,
            grid=(places.x,),
            in_specs=[
                resident(),
                resident(),
            ]
            + anywhere(after),
            out_specs=whole(shape),
        ),
        out_shape=jax.ShapeDtypeStruct(shape, bf16),
        compiler_params=kernel_params(16),
        cost_estimate=cost(width * tokens * ff, 8e6),
        name="down_grad",
    )(ids, d_t, act, *after)


def up_grad(places, other, cuts, ids, nl_t, dup, br_t, att, one, two, after=()):
    width, tokens = nl_t.shape
    rows, seq, ff = dup.shape
    krows = width // (2 * places.x)
    cols = ff // places.dp
    half = width // (2 * places.dp)
    step = cols * places.y
    cut_up, cut_out = cuts
    shape = places.shape(krows + half + 32, cols)
    cut = cut_up + cut_out

    def kernel(ids, nl_ref, dup_ref, br_ref, att_ref, one_ref, two_ref, *refs):
        out = refs[-9]
        lhs, temp, att_vm, nl_sems, br_sems, att_sem, g_bu, vecs = refs[-8:]
        zr = pl.program_id(0)

        @pl.when(zr == 0)
        def _():
            copies = []
            for x in range(places.x):
                first = pl.multiple_of((2 * x + (ids[0] ^ other)) * krows, 16)
                copies.append(
                    pltpu.make_async_copy(
                        nl_ref.at[pl.ds(first, krows), :],
                        lhs.at[x * krows : (x + 1) * krows, :],
                        nl_sems.at[x],
                    )
                )
                copies[-1].start()
            fetch_strips(br_ref, temp, br_sems, ids, other, half, places.dp)
            pltpu.make_async_copy(att_ref, att_vm, att_sem).start()
            lhs[places.x * krows :, :] = jnp.ones((16, tokens), bf16)
            for copy in copies:
                copy.wait()

        start = pl.multiple_of((ids[2] ^ zr) * step, 128)
        res = nn(lhs[...], dup_ref[:, :, pl.ds(start, step)].reshape(tokens, step))
        g_bu[:, pl.ds(start, step)] = res[places.x * krows : places.x * krows + 8]
        res = res.astype(bf16)
        for x in range(places.x):
            for y in range(places.y):
                block = res[x * krows : (x + 1) * krows, y * cols : (y + 1) * cols]
                places.put(out, ids[3] ^ x, ids[1] ^ y, zr, block, cut_up, 0, cut)

        @pl.when(zr == places.z - 1)
        def _():
            vecs[...] = jnp.zeros(vecs.shape, f32)
            at = 0
            for ref, count in ((one_ref, 3), (two_ref, 3), (g_bu, 1)):
                for i in range(count):
                    for j in range(ref.shape[1] // cols):
                        vecs[at : at + 1, :] = ref[i : i + 1, j * cols : (j + 1) * cols]
                        at += 1
            low = vecs[...].astype(bf16)
            for i in range(2):
                for j in range(2):
                    for z in range(places.z):
                        out[i, j, z, krows + half :] = low
            pltpu.make_async_copy(att_ref, att_vm, att_sem).wait()
            for d in range(places.dp):
                pltpu.make_async_copy(
                    br_ref.at[d * half : (d + 1) * half, :],
                    temp.at[d * half : (d + 1) * half, :],
                    br_sems.at[d],
                ).wait()
            res = nn(temp[...], att_vm[...].reshape(tokens, width)).astype(bf16)
            for z in range(places.z):
                for y in range(places.y):
                    d = z * places.y + y
                    for x in range(places.x):
                        block = res[d * half : (d + 1) * half, x * cols : (x + 1) * cols]
                        places.put(
                            out, ids[3] ^ x, ids[1] ^ y, ids[2] ^ z, block, cut_out,
                            cut_up, cut + krows - cut_up,
                        )

    return pl.pallas_call(
        kernel,
        grid_spec=pltpu.PrefetchScalarGridSpec(
            num_scalar_prefetch=1,
            grid=(places.z,),
            in_specs=[
                pl.BlockSpec(memory_space=pl.ANY),
                resident(),
                pl.BlockSpec(memory_space=pl.ANY),
                pl.BlockSpec(memory_space=pl.ANY),
                whole(one.shape),
                whole(two.shape),
            ]
            + anywhere(after),
            out_specs=whole(shape),
            scratch_shapes=[
                pltpu.VMEM((places.x * krows + 16, tokens), bf16),
                pltpu.VMEM((width // 2, tokens), bf16),
                pltpu.VMEM(att.shape, bf16),
                pltpu.SemaphoreType.DMA((places.x,)),
                pltpu.SemaphoreType.DMA((places.dp,)),
                pltpu.SemaphoreType.DMA,
                pltpu.VMEM((8, ff), f32),
                pltpu.VMEM((32, cols), f32),
            ],
        ),
        out_shape=jax.ShapeDtypeStruct(shape, bf16),
        compiler_params=kernel_params(18),
        cost_estimate=cost(width * tokens * (ff + width), 12e6),
        name="up_grad",
    )(ids, nl_t, dup, br_t, att, one, two, *after)


def square_grad(places, other, cut, ids, d_ts, sources, small, length, g_bq, after=()):
    n_rows, width, _ = d_ts[0].shape
    half = width // (2 * places.dp)
    cols = width // places.x
    count = len(d_ts)
    _, seq, keys = small.shape
    s_half, s_cols = seq // (2 * places.dp), keys // places.x
    extra = s_half // 2
    shape = places.shape(count * half + extra, cols)
    flat_s = [p for source in sources for p, _ in source]
    specs = [
        pl.BlockSpec((1,) + p.shape[1:], lambda i, ids, own=own: (own, 0, 0))
        for source in sources
        for p, own in source
    ]
    split = len(sources[0])
    index = [range(split)] + [range(split, len(flat_s))] * (count - 1)
    lengths = [n_rows * d.shape[2] for d in d_ts]
    after = list(after)

    def kernel(ids, *refs):
        d_refs, refs = refs[:count], refs[count:]
        s_refs, refs = refs[: len(flat_s)], refs[len(flat_s) :]
        small_ref, refs = refs[0], refs[1:]
        g_bq, refs = refs[0], refs[1 + len(after) :]
        outs, refs = refs[:1], refs[1:]
        lhs, (rhs, total, vec, sems) = refs[:count], refs[count:]
        copies = []
        for m in range(count):
            copies.append([])
            start = 0
            for r in range(n_rows):
                src = d_refs[m]
                for d in range(places.dp):
                    first = pl.multiple_of(2 * half * d + half * (ids[0] ^ other), 16)
                    copy = pltpu.make_async_copy(
                        src.at[r, pl.ds(first, half), :],
                        lhs[m].at[d * half : (d + 1) * half, start : start + src.shape[2]],
                        sems.at[m, r, d],
                    )
                    copy.start()
                    copies[-1].append(copy)
                start += src.shape[2]
        total[...] = total_of([small_ref[r] for r in range(n_rows)])
        for i in range(seq // length):
            for j in range(length // (2 * s_half)):
                d = (ids[4] ^ i) * (length // (2 * s_half)) + j
                yr, zr = ids[1] ^ (d % places.y), ids[2] ^ (d // places.y)
                first = i * length + 2 * s_half * j + s_half * (ids[0] ^ other)
                block = total[pl.ds(pl.multiple_of(first, 16), s_half), :].astype(bf16)
                for x in range(places.x):
                    for part in range(2):
                        outs[0][
                            yr,
                            ids[3] ^ x,
                            zr,
                            count * half :,
                            part * s_cols : (part + 1) * s_cols,
                        ] = block[part * extra : (part + 1) * extra, x * s_cols : (x + 1) * s_cols]
        vec[...] = jnp.zeros(vec.shape, f32)
        acc = total_of([g_bq[r] for r in range(n_rows)])
        for i in range(width // 128):
            vec[i : i + 1, :] = acc[:, i * 128 : (i + 1) * 128]
        low = vec[...].astype(bf16)
        for i in range(2):
            for j in range(2):
                for z in range(places.z):
                    outs[0][i, j, z, count * half :, 2 * s_cols : 2 * s_cols + 128] = low
        for m in range(count):
            start = 0
            for i in index[m]:
                rhs[start : start + s_refs[i].shape[1], :] = s_refs[i][0]
                start += s_refs[i].shape[1]
            for copy in copies[m]:
                copy.wait()
            res = nn(lhs[m][...], rhs[:start, :]).astype(bf16)
            for z in range(places.z):
                for y in range(places.y):
                    d = z * places.y + y
                    for x in range(places.x):
                        block = res[d * half : (d + 1) * half, x * cols : (x + 1) * cols]
                        places.put(
                            outs[0], ids[3] ^ x, ids[1] ^ y, ids[2] ^ z, block, cut,
                            m * cut, count * cut + m * (half - cut),
                        )

    return pl.pallas_call(
        kernel,
        grid_spec=pltpu.PrefetchScalarGridSpec(
            num_scalar_prefetch=1,
            grid=(1,),
            in_specs=anywhere(d_ts)
            + specs
            + [whole(small.shape), whole(g_bq.shape)]
            + anywhere(after),
            out_specs=whole(shape),
            scratch_shapes=[pltpu.VMEM((width // 2, n), bf16) for n in lengths]
            + [
                pltpu.VMEM((max(lengths), width), bf16),
                pltpu.VMEM((seq, keys), f32),
                pltpu.VMEM((extra, 128), f32),
                pltpu.SemaphoreType.DMA((count, n_rows, places.dp)),
            ],
        ),
        out_shape=jax.ShapeDtypeStruct(shape, bf16),
        compiler_params=kernel_params(16),
        cost_estimate=cost(2.2e9, 12e6),
        name="square_grad",
    )(ids, *d_ts, *flat_s, small, g_bq, *after)


def gather_rows(ids, parts, after=()):
    n = len(parts)
    rows, length, width = parts[0].shape

    def kernel(ids, *refs):
        out, token = refs[-2:]
        token[...] = jnp.zeros(token.shape, f32)
        for i in range(n):

            @pl.when(pl.program_id(0) == i)
            def _():
                out[...] = refs[i][...].astype(f32)

    spec = whole((rows, length, width))
    return pl.pallas_call(
        kernel,
        grid_spec=pltpu.PrefetchScalarGridSpec(
            num_scalar_prefetch=1,
            grid=(n,),
            in_specs=[spec] * n + anywhere(after),
            out_specs=[
                pl.BlockSpec((rows, length, width), lambda i, ids: (ids[4] ^ i, 0, 0)),
                whole((8, 128)),
            ],
        ),
        out_shape=[out_hbm((n * rows, length, width), f32), jax.ShapeDtypeStruct((8, 128), f32)],
        compiler_params=kernel_params(10),
        cost_estimate=cost(0, 6 * n * rows * length * width),
        name="gather_rows",
    )(ids, *parts, *after)


def exchange(value, axis, size, relative):
    pairs = [(i, i ^ relative) for i in range(size)]
    return lax.ppermute(value, axis, pairs)


def total_of(parts):
    acc = parts[0].astype(f32)
    for part in parts[1:]:
        acc = acc + part.astype(f32)
    return acc


def call(name, kernel, grid, ins, specs, outs, out_specs, after=(), scratch=()):
    def wrapped(*refs):
        kernel(*refs[: len(ins)], *refs[len(ins) + len(after) :])

    moved = sum(math.prod(shape) * 8 for shape, _ in outs)
    return pl.pallas_call(
        wrapped,
        grid=grid,
        in_specs=list(specs) + anywhere(after),
        out_specs=out_specs,
        out_shape=[jax.ShapeDtypeStruct(shape, dt) for shape, dt in outs],
        scratch_shapes=list(scratch),
        compiler_params=kernel_params(8),
        cost_estimate=cost(moved, moved),
        name=name,
    )(*ins, *after)


class Reduction:
    def __init__(self, places, n_dp, n_krow, cut):
        self.places, self.n_dp, self.n_krow, self.cut = places, n_dp, n_krow, cut

    def along(self, axis, value, relative):
        if axis == "x":
            return exchange(value, "krow", self.n_krow, 2 * relative)
        if axis == "y":
            return exchange(value, "dp", self.n_dp, relative)
        return exchange(value, "dp", self.n_dp, relative * self.places.y)

    def core(self, send):
        self.came = exchange(send, "krow", self.n_krow, 1)

    def first(self, keep, after=()):
        self.keep = keep
        _, _, nz, rows, cols = keep.shape
        cut = self.cut
        self.heights = (cut, rows - cut)

        def kernel(k, c, first, second):
            total = total_of([k[0], c[0]]).astype(bf16)
            first[...] = total[:, :, :cut]
            second[...] = total[:, :, cut:]

        spec = pl.BlockSpec((1, 2, 1, rows, cols), lambda z: (1, 0, z, 0, 0))
        res = call(
            "first_sum", kernel, (nz,), [keep, self.came], [spec] * 2,
            [((2, nz, h, cols), bf16) for h in self.heights],
            [pl.BlockSpec((2, 1, h, cols), lambda z: (0, z, 0, 0)) for h in self.heights],
            after,
        )
        self.one = [self.along(axis, r, 1) for axis, r in zip("xy", res)]
        return res

    def second(self, after=()):
        _, _, nz, rows, cols = self.keep.shape
        cut = self.cut

        def kernel(k, c, g, h, first, second):
            first[0] = total_of([k[0, 0, 0, :cut], c[0, 0, 0, :cut], g[0, 0]]).astype(bf16)
            second[0] = total_of([k[0, 0, 0, cut:], c[0, 0, 0, cut:], h[0, 0]]).astype(bf16)

        spec = pl.BlockSpec((1, 1, 1, rows, cols), lambda z: (0, 1, z, 0, 0))
        res = call(
            "second_sum", kernel, (nz,), [self.keep, self.came] + self.one,
            [spec] * 2
            + [pl.BlockSpec((1, 1, h, cols), lambda z: (1, z, 0, 0)) for h in self.heights],
            [((nz, h, cols), bf16) for h in self.heights],
            [pl.BlockSpec((1, h, cols), lambda z: (z, 0, 0)) for h in self.heights],
            after,
        )
        self.two = [self.along(axis, r, 1) for axis, r in zip("yx", res)]
        return res

    def third(self, after=()):
        _, _, nz, rows, cols = self.keep.shape
        cut = self.cut

        def kernel(k, c, g1, h1, g2, h2, odd, even):
            for z in range(nz):
                out = odd if z % 2 else even
                for part, one, two in ((slice(0, cut), g1, g2), (slice(cut, rows), h1, h2)):
                    value = total_of([k[0, 0, z, part], c[0, 0, z, part], one[0, z], two[z]])
                    out[z // 2, part, :] = value.astype(out.dtype)

        shape = (nz // 2, rows, cols)
        spec = pl.BlockSpec((1, 1, nz, rows, cols), lambda i: (0, 0, 0, 0, 0))
        odd, self.even = call(
            "third_sum", kernel, (1,), [self.keep, self.came] + self.one + self.two,
            [spec] * 2
            + [pl.BlockSpec((1, nz, h, cols), lambda i: (0, 0, 0, 0)) for h in self.heights]
            + [pl.BlockSpec((nz, h, cols), lambda i: (0, 0, 0)) for h in self.heights],
            [(shape, bf16), (shape, f32)], [whole(shape)] * 2, after,
        )
        self.three = self.along("z", odd, 1)
        return [odd]

    def fourth(self, after=()):
        _, rows, cols = self.even.shape

        def kernel(e, g, send, mine):
            send[...] = total_of([e[1], g[1]]).astype(bf16)
            mine[...] = total_of([e[0], g[0]])

        shape = (rows, cols)
        send, mine = call(
            "fourth_sum", kernel, (1,), [self.even, self.three], [whole(self.even.shape)] * 2,
            [(shape, bf16), (shape, f32)], [whole(shape)] * 2, after,
        )
        self.terms = [mine, self.along("z", send, 2)]
        return [send]


def finish_down(red, after=()):
    rows, cols = red.terms[0].shape
    n = len(red.terms)

    def kernel(*refs):
        refs[n][...] = total_of([r[...] for r in refs[:n]])

    return call(
        "finish_down", kernel, (1,), red.terms, [whole((rows, cols))] * n,
        [((rows, cols), f32)], [whole((rows, cols))], after,
    )


def finish_up(red, cuts, krows, half, width, ff, after=()):
    rows, cols = red.terms[0].shape
    n = len(red.terms)
    cut_up, cut_out = cuts
    rest = krows - cut_up
    sizes = (width,) * 6 + (ff,)

    def kernel(*refs):
        up, out = refs[n], refs[n + 1]
        total = total_of([r[...] for r in refs[:n]])
        low = cut_up + cut_out
        up[:cut_up] = total[:cut_up]
        up[cut_up:] = total[low : low + rest]
        out[:cut_out] = total[cut_up:low]
        out[cut_out:] = total[low + rest : krows + half]
        at = krows + half
        for piece, size in zip(refs[n + 2 :], sizes):
            for i in range(size // cols):
                piece[i * cols : (i + 1) * cols] = total[at, :]
                at += 1

    shapes = [(krows, cols), (half, cols)] + [(size,) for size in sizes]
    return call(
        "finish_up", kernel, (1,), red.terms, [whole((rows, cols))] * n,
        [(shape, f32) for shape in shapes], [whole(shape) for shape in shapes], after,
    )


def finish_square(red, ids, out_rows, cut, half, count, s_cols, after=()):
    rows, cols = red.terms[0].shape
    n = len(red.terms)
    extra = rows - count * half
    mine_cols = cols // 2
    width = cols * red.places.x
    height = (count + 1) * half + 2 * extra

    def kernel(ids, out_ref, *refs):
        terms, (mine, other, g_bq, temp) = refs[:n], refs[n:]
        total = total_of([r[...] for r in terms])
        rest = half - cut
        temp[:half] = out_ref[...]
        for m in range(count):
            at = half * (m + 1)
            temp[at : at + cut] = total[m * cut : (m + 1) * cut]
            low = count * cut + m * rest
            temp[at + cut : at + half] = total[low : low + rest]
        core = ids[0]
        square = (count + 1) * half
        lo, hi = temp[:square, :mine_cols], temp[:square, mine_cols:]
        mine[:square, :] = jnp.where(core == 0, lo, hi)
        other[:square, :] = jnp.where(core == 0, hi, lo).astype(bf16)
        h = s_cols // 2
        mine[square:, :] = jnp.zeros((2 * extra, mine_cols), f32)
        other[square:, :] = jnp.zeros((2 * extra, mine_cols), bf16)
        for part in range(2):
            tail = total[count * half :, part * s_cols : (part + 1) * s_cols]
            at = square + part * extra
            lo, hi = tail[:, :h], tail[:, h:]
            mine[at : at + extra, :h] = jnp.where(core == 0, lo, hi)
            other[at : at + extra, :h] = jnp.where(core == 0, hi, lo).astype(bf16)
        for i in range(width // 128):
            g_bq[i * 128 : (i + 1) * 128] = total[count * half + i, 2 * s_cols : 2 * s_cols + 128]

    return call(
        "finish_square", kernel, (1,), [ids, out_rows] + red.terms,
        [pl.BlockSpec(memory_space=pltpu.SMEM), whole(out_rows.shape)]
        + [whole((rows, cols))] * n,
        [((height, mine_cols), f32), ((height, mine_cols), bf16), ((width,), f32)],
        [whole((height, mine_cols))] * 2 + [whole((width,))],
        after,
        [pltpu.VMEM(((count + 1) * half, cols), f32)],
    )


def finish_columns(ids, mine, there, half, count, extra, s_half_cols):
    mine_cols = mine.shape[1]
    square = count * half

    def kernel(ids, mine, there, *refs):
        outs, temp = refs[:-1], refs[-1]
        core = ids[0]

        def merge(at, height, cols, out):
            a, b = mine[at : at + height, :cols], there[at : at + height, :cols].astype(f32)
            low, high = jnp.where(core == 0, a, b), jnp.where(core == 0, b, a)
            out[...] = jnp.concatenate([low, high], axis=0).T

        for m in range(count):
            merge(m * half, half, mine_cols, outs[m])
        merge(square, 2 * extra, s_half_cols, outs[count])

    shapes = [(mine_cols, 2 * half)] * count + [(s_half_cols, 4 * extra)]
    return call(
        "finish_columns", kernel, (1,), [ids, mine, there],
        [pl.BlockSpec(memory_space=pltpu.SMEM), whole(mine.shape), whole(there.shape)],
        [(shape, f32) for shape in shapes], [whole(shape) for shape in shapes],
        (), [pltpu.VMEM((8, 128), f32)],
    )


def local(
    sizes,
    tokens,
    segment_ids,
    segment_live,
    w_query,
    b_query,
    w_key,
    w_value,
    w_out,
    b_out,
    attn_gain,
    attn_shift,
    w_up,
    b_up,
    w_down,
    b_down,
    ffn_gain,
    ffn_shift,
    compress,
    cotangent,
):
    n_dp, n_krow = sizes
    all_rows, length, width = tokens.shape
    rows = all_rows // n_krow
    seq = n_krow * length
    keys = compress.shape[0]
    ff = w_up.shape[1]
    krow, dp = lax.axis_index("krow"), lax.axis_index("dp")
    places = Places(n_dp, n_krow)
    ids = jnp.stack([krow % 2, dp % places.y, dp // places.y, krow // 2, krow]).astype(jnp.int32)
    fast = (
        width % (2 * places.x * 32) == 0
        and ff % (n_dp * 128) == 0
        and ff % (n_krow * 128) == 0
        and width % (2 * n_dp * 16) == 0
        and seq % (2 * n_dp * 32) == 0
        and width % (places.x * 128) == 0
        and keys % (places.x * 128) == 0
        and length % (seq // n_dp) == 0
        and ff // n_dp == width // places.x
        and 2 * (keys // places.x) + 128 <= width // places.x
        and width <= 128 * (seq // (4 * n_dp))
        and places.x == 2
        and places.y == 2
        and places.z == 4
        and rows > 1
    )

    def spread(value):
        parts = []
        for r in range(n_krow):
            part = lax.dynamic_slice_in_dim(value, (krow ^ r) * rows, rows, 0)
            parts.append(exchange(part, "krow", n_krow, r) if r else part)
        return parts

    def back(parts):
        return [exchange(part, "krow", n_krow, r) if r else part for r, part in enumerate(parts)]

    def row(value):
        return value.astype(f32).reshape(1, -1)

    toks = spread(tokens)
    cot_source = lax.optimization_barrier((cotangent, toks[-1]))[0]
    cots = spread(cot_source)

    my_ids = lax.dynamic_slice_in_dim(segment_ids, krow * rows, rows, 0)
    my_live = lax.dynamic_slice_in_dim(segment_live, krow * rows, rows, 0)
    labels = jnp.arange(segment_live.shape[1], dtype=jnp.int32)
    live = jnp.sum(
        jnp.where(my_ids[:, :, None] == labels, my_live[:, None, :], 0).astype(f32), axis=-1
    )

    def relative(value, axis):
        return jnp.concatenate(
            [
                lax.dynamic_slice_in_dim(value, (krow ^ r) * length, length, axis)
                for r in range(n_krow)
            ],
            axis=axis,
        )

    live = relative(live, 1)
    comp = relative(compress, 1)
    live_row = live[:, None, :]
    live_col = jnp.broadcast_to(live[:, :, None], (rows, seq, 128))
    comp_t = comp.T
    gain, shift = row(attn_gain), row(attn_shift)

    q_t, pk, k, v, lse, att, xhat, rstd = attn_fwd(
        toks, live_row, comp, w_query, row(b_query), w_key, w_value, w_out, row(b_out)
    )
    res = ffn_fwd(
        cots, xhat, gain, shift, w_up, row(b_up), w_down, row(b_down), row(ffn_gain), row(ffn_shift)
    )
    outs, (act, gp, dh2, d_t, sums_two) = res[:n_krow], res[n_krow:]
    out_parts = back(outs)
    ahead = []
    if fast:
        cut_down = 32
        cuts_up = (width // n_krow // 2, 32)
        cut_square = 16
        half = width // (2 * n_dp)
        down = Reduction(places, n_dp, n_krow, cut_down)
        up = Reduction(places, n_dp, n_krow, sum(cuts_up))
        square = Reduction(places, n_dp, n_krow, 3 * cut_square)
        send = down_grad(places, 1, cut_down, ids, d_t, act)
        down.core(send)
        keep = down_grad(places, 0, cut_down, ids, d_t, act, after=[send])
        ahead = list(down.first(keep))

    dup, dh1, da_t, nl_t, br_t, sums_one = ffn_bwd(
        gp, dh2, xhat, rstd, gain, shift, w_up, w_down, w_out, after=ahead
    )

    if fast:
        ahead = down.second([sums_one] + list(out_parts))
        parts = nl_t, dup, br_t, att, sums_one, sums_two
        send = up_grad(places, 1, cuts_up, ids, *parts, after=ahead)
        up.core(send)
        keep = up_grad(places, 0, cuts_up, ids, *parts, after=[send])
        ahead = up.first(keep)
        ahead = down.third(ahead)

    res = attn_bwd(
        toks, q_t, k, v, lse, da_t, comp_t, live_col, w_query, w_key, w_value, dh1, after=ahead
    )
    grad_parts, bwd = res[:n_krow], res[n_krow:]

    if fast:
        sources = [[(t, r) for r in range(rows) for t in toks], [(pk, r) for r in range(rows)]]
        ahead = up.second([bwd[3], down.three])
        ahead = down.fourth(ahead)
        parts = bwd[:3], sources, bwd[4], length, bwd[3]
        send = square_grad(places, 1, cut_square, ids, *parts, after=ahead)
        square.core(send)
        keep = square_grad(places, 0, cut_square, ids, *parts, after=[send])
        ahead = square.first(keep)
        ahead = up.third(ahead)
        grad_parts = back(lax.optimization_barrier((grad_parts, ahead))[0])
        output, token = gather_rows(ids, out_parts, after=ahead)
        ahead = up.fourth([token])
        ahead = square.second(ahead)
        (g_down,) = finish_down(down, after=ahead)
        g_up, out_rows, *pieces = finish_up(
            up, cuts_up, width // n_krow, half, width, ff, after=[g_down]
        )
        g_down = g_down.T
        ahead = square.third([out_rows] + grad_parts)
        grad_tokens, token = gather_rows(ids, grad_parts, after=ahead)
        square.fourth([token])
        s_cols = keys // places.x
        mine, other, g_bq = finish_square(square, ids, out_rows, cut_square, half, 3, s_cols)
        pieces = [g_bq] + pieces
        there = exchange(other, "krow", n_krow, 1)
        g_out, g_q, g_k, g_v, g_comp = finish_columns(
            ids, mine, there, half, 4, seq // (4 * n_dp), s_cols // 2
        )
    else:
        grad_parts = back(grad_parts)
        g_bu = jnp.sum(dup.astype(f32), axis=(0, 1)).reshape(-1, width)
        g_bq = jnp.sum(bwd[3], axis=0)
        vectors = jnp.concatenate([g_bq, sums_one[:3], sums_two[:3], g_bu], axis=0)
        output, _ = gather_rows(ids, out_parts)
        grad_tokens, _ = gather_rows(ids, grad_parts)
        vectors = lax.psum(vectors.reshape(-1), ("dp", "krow"))
        pieces = []
        start = 0
        for size in (width,) * 7 + (ff,):
            pieces.append(vectors[start : start + size])
            start += size

        def scattered(value):
            value = value.astype(bf16)
            part = lax.psum_scatter(value, "krow", scatter_dimension=0, tiled=True)
            return lax.psum_scatter(part, "dp", scatter_dimension=1, tiled=True).astype(f32)

        def product(a, b):
            return lax.dot_general(a, b, (((1,), (0,)), ((), ())), preferred_element_type=f32)

        token_rows = jnp.concatenate(toks, axis=1)
        d_q, d_k, d_v = [jnp.swapaxes(d, 0, 1).reshape(width, -1) for d in bwd[:3]]
        pk = pk.reshape(-1, width)
        g_q = scattered(product(d_q, token_rows.reshape(-1, width)).T)
        g_k = scattered(product(d_k, pk).T)
        g_v = scattered(product(d_v, pk).T)
        g_out = scattered(product(br_t, att.reshape(-1, width)).T)
        g_up = scattered(product(nl_t, dup.reshape(-1, ff)))
        g_down = scattered(product(d_t, act.reshape(-1, ff)).T)
        blocks = jnp.sum(bwd[4].astype(f32), axis=0).reshape(n_krow, length, keys)
        blocks = jnp.concatenate(
            [lax.dynamic_slice_in_dim(blocks, krow ^ r, 1, 0) for r in range(n_krow)]
        )
        g_comp = scattered(blocks.reshape(seq, keys).T)

    g_bq, g_gain, g_shift, g_bo, g_fgain, g_fshift, g_bd, g_bu = pieces
    return (
        output,
        grad_tokens,
        g_q,
        g_bq,
        g_k,
        g_v,
        g_out,
        g_bo,
        g_gain,
        g_shift,
        g_up,
        g_bu,
        g_down,
        g_bd,
        g_fgain,
        g_fshift,
        g_comp,
    )


def solution(mesh):
    rows = P("dp", "krow", None)
    per_row = P("dp", None)
    block = P("krow", "dp")
    in_specs = (rows, per_row, per_row) + (P(),) * 15 + (rows,)
    out_specs = (
        (rows, rows, block, P(), block, block, block)
        + (P(),) * 3
        + (block, P(), block)
        + (P(),) * 3
        + (block,)
    )
    sizes = (mesh.shape["dp"], mesh.shape["krow"])
    return jax.shard_map(
        functools.partial(local, sizes),
        mesh=mesh,
        in_specs=in_specs,
        out_specs=out_specs,
        check_vma=False,
    )
```

```python
import functools
import math

import jax
import jax.numpy as jnp
from jax import lax
from jax.experimental import pallas as pl
from jax.experimental.pallas import tpu as pltpu
from jax.sharding import PartitionSpec as P

H = 12
HD = 64
f32 = jnp.float32
bf16 = jnp.bfloat16


def nn(a, b):
    return lax.dot_general(a, b, (((1,), (0,)), ((), ())), preferred_element_type=f32)


def nt(a, b):
    return lax.dot_general(a, b, (((1,), (1,)), ((), ())), preferred_element_type=f32)


def whole(shape):
    rank = len(shape)
    return pl.BlockSpec(shape, lambda *_: (0,) * rank, pipeline_mode=pl.Buffered(1))


def fetch_strips(src, dst, sems, ids, other, half, dp):
    copies = []
    for d in range(dp):
        first = pl.multiple_of(2 * half * d + half * (ids[0] ^ other), 16)
        copies.append(
            pltpu.make_async_copy(
                src.at[pl.ds(first, half), :], dst.at[d * half : (d + 1) * half, :], sems.at[d]
            )
        )
        copies[-1].start()
    return copies


def resident():
    return pl.BlockSpec(memory_space=pltpu.VMEM)


def out_hbm(shape, dtype):
    return pltpu.HBM(shape, dtype)


def in_hbm(*values):
    return [pltpu.with_memory_space_constraint(v, pltpu.HBM) for v in values]


def fetch(sources, places, sems):
    copies = [
        pltpu.make_async_copy(src, dst, sems.at[i])
        for i, (src, dst) in enumerate(zip(sources, places))
    ]

    @pl.when(pl.program_id(0) == 0)
    def _():
        for copy in copies:
            copy.start()

    def wait(*which):
        @pl.when(pl.program_id(0) == 0)
        def _():
            for i in which:
                copies[i].wait()

    return wait


def anywhere(values):
    return [pl.BlockSpec(memory_space=pl.ANY)] * len(values)


def row_block(*shape):
    rank = len(shape)
    return pl.BlockSpec((1,) + shape, lambda r, *_: (r,) + (0,) * rank)


def parts_of(n, rows, length, width, paired):
    single = (row_block(length, width), (rows, length, width))
    if not paired:
        return [single[0]] * n, [single[1]] * n
    both = (pl.BlockSpec((2, 1, length, width), lambda r, *_: (0, r, 0, 0)), (2, rows, length, width))
    return [single[0]] * 2 + [both[0]], [single[1]] * 2 + [both[1]]


def put_part(outs, n, i, value):
    if len(outs) == n or i < 2:
        outs[i][0] = value
    else:
        outs[2][i - 2, 0] = value


def kernel_params(mebibytes):
    return pltpu.CompilerParams(dimension_semantics=("arbitrary",), vmem_limit_bytes=mebibytes * 1024 * 1024)


def cost(flops, moved, trans=0):
    return pl.CostEstimate(flops=int(flops), bytes_accessed=int(moved), transcendentals=int(trans))


def add_to(ref, value, first):
    @pl.when(first)
    def _():
        ref[...] = value

    @pl.when(jnp.logical_not(first))
    def _():
        ref[...] += value


def col_sum(value):
    return jnp.sum(value, axis=0, keepdims=True)


def gelu_parts(u):
    phi = 0.5 + 0.5 * lax.erf(u * (1.0 / math.sqrt(2.0)))
    density = jnp.exp(-0.5 * u * u) * (1.0 / math.sqrt(2.0 * math.pi))
    return u * phi, phi + u * density


def attn_fwd_kernel(n, *refs):
    toks = refs[:n]
    live, comp, wq_hbm, bq, wk_hbm, wv_hbm, wo_hbm, bo = refs[n : n + 8]
    q_t, pk, k, v, lse, att, xhat, rstd = refs[n + 8 : n + 16]
    tok, att_t, wq, wk, wv, wo, sems = refs[n + 16 :]
    wait = fetch((wq_hbm, wk_hbm, wv_hbm, wo_hbm), (wq, wk, wv, wo), sems)
    length = toks[0].shape[1]
    for i in range(n):
        tok[i * length : (i + 1) * length, :] = toks[i][0]
    masked = (comp[...].astype(f32) * live[0]).astype(bf16)
    x = tok[...]
    pk[0] = nn(masked, x).astype(bf16)
    wait(0, 1, 2)
    for c in range(3):
        cols = slice(256 * c, 256 * c + 256)
        q = (nn(x, wq[:, cols]) + bq[:, cols]).astype(bf16) * jnp.asarray(1.0 / math.sqrt(HD), bf16)
        q_t[0, cols, :] = q.T
        k[0, :, cols] = nn(pk[0], wk[:, cols]).astype(bf16)
        v[0, :, cols] = nn(pk[0], wv[:, cols]).astype(bf16)
    lane = lax.broadcasted_iota(jnp.int32, (1, 2 * HD), 1)
    for pair in range(H // 2):
        cols = slice(2 * HD * pair, 2 * HD * (pair + 1))
        k_pair = k[0, :, cols]
        v_t = v[0, :, cols].T
        for half in range(2):
            h = 2 * pair + half
            mine = jnp.where((lane // HD) == half, k_pair, jnp.zeros_like(k_pair))
            s = nn(mine, q_t[0, cols, :])
            top = jnp.max(s, axis=0, keepdims=True)
            e = jnp.exp(s - top)
            total = jnp.sum(e, axis=0, keepdims=True)
            w = (e * (1.0 / total)).astype(bf16)
            lse[0, h : h + 1, :] = top + jnp.log(total)
            att_t[h * HD : (h + 1) * HD, :] = nn(v_t[half * HD : (half + 1) * HD, :], w).astype(bf16)
    for c in range(3):
        cols = slice(256 * c, 256 * c + 256)
        att[0, :, cols] = att_t[cols, :].T
    wait(3)
    hidden = x.astype(f32) + nn(att[0], wo[...]) + bo[...]
    average = jnp.mean(hidden, axis=-1, keepdims=True)
    centred = hidden - average
    spread = jnp.mean(centred * centred, axis=-1, keepdims=True)
    r = lax.rsqrt(spread + 1e-05)
    xhat[0] = centred * r
    rstd[0] = jnp.broadcast_to(r, rstd.shape[1:])


def attn_fwd(toks, live, comp, wq, bq, wk, wv, wo, bo):
    rows, length, width = toks[0].shape
    n = len(toks)
    seq = n * length
    keys = comp.shape[0]
    in_specs = [row_block(length, width)] * n + [
        row_block(1, seq),
        whole((keys, seq)),
        pl.BlockSpec(memory_space=pl.ANY),
        whole((1, width)),
        pl.BlockSpec(memory_space=pl.ANY),
        pl.BlockSpec(memory_space=pl.ANY),
        pl.BlockSpec(memory_space=pl.ANY),
        whole((1, width)),
    ]
    outs = [
        ((width, seq), bf16),
        ((keys, width), bf16),
        ((keys, width), bf16),
        ((keys, width), bf16),
        ((16, seq), f32),
        ((seq, width), bf16),
        ((seq, width), f32),
        ((seq, 128), f32),
    ]
    return pl.pallas_call(
        functools.partial(attn_fwd_kernel, n),
        grid=(rows,),
        in_specs=in_specs,
        out_specs=[row_block(*shape) for shape, _ in outs],
        out_shape=[out_hbm((rows,) + shape, dt) for shape, dt in outs],
        scratch_shapes=[pltpu.VMEM((seq, width), bf16), pltpu.VMEM((width, seq), bf16)]
        + [pltpu.VMEM((width, width), bf16)] * 4
        + [pltpu.SemaphoreType.DMA((4,))],
        compiler_params=kernel_params(30),
        cost_estimate=cost(rows * 5e9, 12e6, rows * H * seq * keys),
        name="attn_fwd",
    )(*toks, live, comp, *in_hbm(wq), bq, *in_hbm(wk, wv, wo), bo)


def ffn_fwd_kernel(n, n_out, *refs):
    cots = refs[:n]
    xhat, gain, shift, wu, bu, wd, bd, fgain, fshift = refs[n : n + 9]
    refs = refs[n + 9 :]
    outs = refs[:n_out]
    act, gp, dh2, d_t, sums = refs[n_out:]
    r = pl.program_id(0)
    first = r == 0
    length = cots[0].shape[1]
    ff = wu.shape[1]
    chunk = 512
    count = ff // chunk
    normed = xhat[0] * gain[...] + shift[...]
    low = normed.astype(bf16)

    def up(c):
        cols = slice(c * chunk, (c + 1) * chunk)
        return nn(low, wu[:, cols]) + bu[:, cols]

    for c in range(count):
        cols = slice(c * chunk, (c + 1) * chunk)
        a, g = gelu_parts(up(c))
        act[r, :, cols] = a.astype(bf16)
        gp[0, :, cols] = g.astype(bf16)
    total = normed + bd[...] + nn(act[r], wd[...])
    average = jnp.mean(total, axis=-1, keepdims=True)
    centred = total - average
    spread = jnp.mean(centred * centred, axis=-1, keepdims=True)
    rs = lax.rsqrt(spread + 1e-05)
    hat = centred * rs
    result = (hat * fgain[...] + fshift[...]).astype(bf16)
    for i in range(n):
        put_part(outs, n, i, result[i * length : (i + 1) * length, :])
    cot = jnp.concatenate([c[0] for c in cots], axis=0).astype(f32)
    dhat = cot * fgain[...]
    d = rs * (
        dhat
        - jnp.mean(dhat, axis=-1, keepdims=True)
        - hat * jnp.mean(dhat * hat, axis=-1, keepdims=True)
    )
    dh2[0] = d
    d_low = d.astype(bf16)
    seq = d_low.shape[0]
    d_t[:, pl.ds(pl.multiple_of(r * seq, seq), seq)] = d_low.T
    add_to(
        sums,
        jnp.concatenate(
            [col_sum(cot * hat), col_sum(cot), col_sum(d_low.astype(f32)), jnp.zeros((5, d.shape[1]), f32)],
            axis=0,
        ),
        first,
    )


def ffn_fwd(paired, cots, xhat, gain, shift, wu, bu, wd, bd, fgain, fshift):
    rows, length, width = cots[0].shape
    n = len(cots)
    seq = n * length
    ff = wu.shape[1]
    vec = whole((1, width))
    in_specs = [row_block(length, width)] * n + [
        row_block(seq, width),
        vec,
        vec,
        resident(),
        whole((1, ff)),
        resident(),
        vec,
        vec,
        vec,
    ]
    specs, shapes = parts_of(n, rows, length, width, paired)
    more = [((seq, ff), bf16), ((seq, width), f32)]
    return pl.pallas_call(
        functools.partial(ffn_fwd_kernel, n, len(shapes)),
        grid=(rows,),
        in_specs=in_specs,
        out_specs=specs
        + [resident()]
        + [row_block(*shape) for shape, _ in more]
        + [resident()]
        + [whole((8, width))],
        out_shape=[jax.ShapeDtypeStruct(shape, bf16) for shape in shapes]
        + [pltpu.VMEM((rows, seq, ff), bf16)]
        + [jax.ShapeDtypeStruct((rows,) + shape, dt) for shape, dt in more]
        + [jax.ShapeDtypeStruct((width, rows * seq), bf16)]
        + [jax.ShapeDtypeStruct((8, width), f32)],
        compiler_params=kernel_params(26),
        cost_estimate=cost(rows * seq * width * ff * 4, 34e6, rows * seq * ff * 2),
        name="ffn_fwd",
    )(*cots, xhat, gain, shift, wu, bu, wd, bd, fgain, fshift)


def ffn_bwd_kernel(*refs):
    gp, dh2, xhat, rstd, gain, shift, wu, wd, wo = refs[:9]
    dup, dh1, da_t, nl_t, br_t, sums = refs[-6:]
    r = pl.program_id(0)
    first = r == 0
    ff = wu.shape[1]
    chunk = 512
    count = ff // chunk
    d_low = dh2[0].astype(bf16)

    def back(c):
        return nt(d_low, wd[c * chunk : (c + 1) * chunk, :])

    for c in range(count):
        cols = slice(c * chunk, (c + 1) * chunk)
        dup[r, :, cols] = (gp[0, :, cols].astype(f32) * back(c)).astype(bf16)
    tile = min(256, dh2.shape[1])
    for i in range(dh2.shape[1] // tile):
        part = slice(i * tile, (i + 1) * tile)
        for j in range(dh2.shape[2] // 256):
            cols = slice(j * 256, (j + 1) * 256)
            dh1[0, part, cols] = dh2[0, part, cols] + nt(dup[r, part, :], wu[cols, :])
    dn = dh1[0]
    hat = xhat[0]
    dhat = dn * gain[...]
    d = rstd[0, :, 0:1] * (
        dhat
        - jnp.mean(dhat, axis=-1, keepdims=True)
        - hat * jnp.mean(dhat * hat, axis=-1, keepdims=True)
    )
    dh1[0] = d
    branch = d.astype(bf16)
    add_to(
        sums,
        jnp.concatenate(
            [col_sum(dn * hat), col_sum(dn), col_sum(branch.astype(f32)), jnp.zeros((5, d.shape[1]), f32)],
            axis=0,
        ),
        first,
    )
    da_t[0] = nt(wo[...], branch).astype(bf16)
    br_t[...] = branch.T
    nl_t[...] = (hat * gain[...] + shift[...]).astype(bf16).T


def ffn_bwd(gp, dh2, xhat, rstd, gain, shift, wu, wd, wo, after=()):
    rows, seq, ff = gp.shape
    width = wu.shape[0]
    vec = whole((1, width))
    in_specs = [
        row_block(seq, ff),
        row_block(seq, width),
        row_block(seq, width),
        row_block(seq, 128),
        vec,
        vec,
        resident(),
        resident(),
        resident(),
    ] + anywhere(after)
    outs = [((seq, width), f32), ((width, seq), bf16)]
    turned = pl.BlockSpec((width, seq), lambda r: (0, r))
    return pl.pallas_call(
        ffn_bwd_kernel,
        grid=(rows,),
        in_specs=in_specs,
        out_specs=[resident()]
        + [row_block(*shape) for shape, _ in outs]
        + [turned] * 2
        + [whole((8, width))],
        out_shape=[pltpu.VMEM((rows, seq, ff), bf16)]
        + [jax.ShapeDtypeStruct((rows,) + shape, dt) for shape, dt in outs]
        + [jax.ShapeDtypeStruct((width, rows * seq), bf16)] * 2
        + [jax.ShapeDtypeStruct((8, width), f32)],
        compiler_params=kernel_params(26),
        cost_estimate=cost(rows * seq * width * ff * 4.5, 34e6),
        name="ffn_bwd",
    )(gp, dh2, xhat, rstd, gain, shift, wu, wd, wo, *after)


def attn_bwd_kernel(n, n_out, *refs):
    toks = refs[:n]
    q_t, k, v, lse, da_t, comp_t, live_col, wq, wk, wv, dh1 = refs[n : n + 11]
    refs = refs[-(n_out + 6) :]
    outs = refs[:n_out]
    dq_t, dk_t, dv_t, g_bq, small, tok = refs[n_out:]
    length = toks[0].shape[1]
    for i in range(n):
        tok[i * length : (i + 1) * length, :] = toks[i][0]
    lane = lax.broadcasted_iota(jnp.int32, (1, 2 * HD), 1)
    scale = jnp.asarray(1.0 / math.sqrt(HD), f32)
    for pair in range(H // 2):
        cols = slice(2 * HD * pair, 2 * HD * (pair + 1))
        k_pair = k[0, :, cols]
        v_pair = v[0, :, cols]
        k_t = k_pair.T
        for half in range(2):
            h = 2 * pair + half
            head = slice(h * HD, (h + 1) * HD)
            mine = (lane // HD) == half
            s = nn(jnp.where(mine, k_pair, jnp.zeros_like(k_pair)), q_t[0, cols, :])
            w = jnp.exp(s - lse[0, h : h + 1, :])
            dw = nn(jnp.where(mine, v_pair, jnp.zeros_like(v_pair)), da_t[0, cols, :])
            dot = jnp.sum(w * dw, axis=0, keepdims=True)
            ds = (w * (dw - dot)).astype(bf16)
            dv_t[0, head, :] = nt(da_t[0, head, :], w.astype(bf16)).astype(bf16)
            dk_t[0, head, :] = nt(q_t[0, head, :], ds).astype(bf16)
            dq_t[0, head, :] = (nn(k_t[half * HD : (half + 1) * HD, :], ds) * scale).astype(bf16)
    dp_t = (nn(wk[...], dk_t[0]) + nn(wv[...], dv_t[0])).astype(bf16)
    small[0] = (nn(tok[...], dp_t) * live_col[0, :, 0:1]).astype(bf16)
    masked = (comp_t[...].astype(f32) * live_col[0, :, 0:1]).astype(bf16)
    dq = dq_t[0].T
    g_bq[0] = col_sum(dq.astype(f32))
    grad = dh1[0] + nt(dq, wq[...]) + nt(masked, dp_t)
    for i in range(n):
        put_part(outs, n, i, grad[i * length : (i + 1) * length, :].astype(bf16))


def attn_bwd(paired, toks, q_t, k, v, lse, da_t, comp_t, live_col, wq, wk, wv, dh1, after=()):
    rows, length, width = toks[0].shape
    n = len(toks)
    seq = n * length
    keys = comp_t.shape[1]
    in_specs = (
        [row_block(length, width)] * n
        + [
            row_block(width, seq),
            row_block(keys, width),
            row_block(keys, width),
            row_block(16, seq),
            row_block(width, seq),
            whole((seq, keys)),
            row_block(seq, 128),
            whole((width, width)),
            whole((width, width)),
            whole((width, width)),
            row_block(seq, width),
        ]
        + anywhere(after)
    )
    specs, shapes = parts_of(n, rows, length, width, paired)
    outs = [
        ((width, seq), bf16),
        ((width, keys), bf16),
        ((width, keys), bf16),
        ((1, width), f32),
        ((seq, keys), bf16),
    ]
    return pl.pallas_call(
        functools.partial(attn_bwd_kernel, n, len(shapes)),
        grid=(rows,),
        in_specs=in_specs,
        out_specs=specs + [row_block(*shape) for shape, _ in outs],
        out_shape=[jax.ShapeDtypeStruct(shape, bf16) for shape in shapes]
        + [jax.ShapeDtypeStruct((rows,) + shape, dt) for shape, dt in outs],
        scratch_shapes=[pltpu.VMEM((seq, width), bf16)],
        compiler_params=kernel_params(28),
        cost_estimate=cost(rows * 8e9, 24e6, rows * H * seq * keys),
        name="attn_bwd",
    )(*toks, q_t, k, v, lse, da_t, comp_t, live_col, wq, wk, wv, dh1, *after)


class Places:
    def __init__(self, n_dp, n_krow):
        self.x = n_krow // 2
        self.y = n_krow // 2
        self.z = n_dp // self.y
        self.dp = n_dp

    def shape(self, rows, cols):
        return (2, 2, self.z, rows, cols)

    def put(self, out, x, y, z, block, cut, low, high):
        out[x, y, z, low : low + cut] = block[:cut]
        out[y, x, z, high : high + block.shape[0] - cut] = block[cut:]


def down_grad(places, other, cut, ids, d_t, act, after=()):
    width, tokens = d_t.shape
    rows, seq, ff = act.shape
    cols = ff // (2 * places.x)
    height = width // places.dp
    shape = places.shape(height, cols)

    def kernel(ids, d_ref, act_ref, *refs):
        xr = pl.program_id(0)
        start = pl.multiple_of((2 * (ids[3] ^ xr) + (ids[0] ^ other)) * cols, 128)
        block = act_ref[:, :, pl.ds(start, cols)].reshape(rows * seq, cols)
        res = nn(d_ref[...], block).astype(bf16)
        for z in range(places.z):
            for y in range(places.y):
                d = z * places.y + y
                block = res[d * height : (d + 1) * height, :]
                places.put(refs[-1], xr, ids[1] ^ y, ids[2] ^ z, block, cut, 0, cut)

    return pl.pallas_call(
        kernel,
        grid_spec=pltpu.PrefetchScalarGridSpec(
            num_scalar_prefetch=1,
            grid=(places.x,),
            in_specs=[
                resident(),
                resident(),
            ]
            + anywhere(after),
            out_specs=whole(shape),
        ),
        out_shape=jax.ShapeDtypeStruct(shape, bf16),
        compiler_params=kernel_params(16),
        cost_estimate=cost(width * tokens * ff, 8e6),
        name="down_grad",
    )(ids, d_t, act, *after)


def up_grad(places, other, cuts, ids, nl_t, dup, br_t, att, one, two, after=()):
    width, tokens = nl_t.shape
    rows, seq, ff = dup.shape
    krows = width // (2 * places.x)
    cols = ff // places.dp
    half = width // (2 * places.dp)
    step = cols * places.y
    cut_up, cut_out = cuts
    shape = places.shape(krows + half + 32, cols)
    cut = cut_up + cut_out

    def kernel(ids, nl_ref, dup_ref, br_ref, att_ref, one_ref, two_ref, *refs):
        out = refs[-9]
        lhs, temp, att_vm, nl_sems, br_sems, att_sem, g_bu, vecs = refs[-8:]
        zr = pl.program_id(0)

        @pl.when(zr == 0)
        def _():
            copies = []
            for x in range(places.x):
                first = pl.multiple_of((2 * x + (ids[0] ^ other)) * krows, 16)
                copies.append(
                    pltpu.make_async_copy(
                        nl_ref.at[pl.ds(first, krows), :],
                        lhs.at[x * krows : (x + 1) * krows, :],
                        nl_sems.at[x],
                    )
                )
                copies[-1].start()
            fetch_strips(br_ref, temp, br_sems, ids, other, half, places.dp)
            pltpu.make_async_copy(att_ref, att_vm, att_sem).start()
            lhs[places.x * krows :, :] = jnp.ones((16, tokens), bf16)
            for copy in copies:
                copy.wait()

        start = pl.multiple_of((ids[2] ^ zr) * step, 128)
        res = nn(lhs[...], dup_ref[:, :, pl.ds(start, step)].reshape(tokens, step))
        g_bu[:, pl.ds(start, step)] = res[places.x * krows : places.x * krows + 8]
        res = res.astype(bf16)
        for x in range(places.x):
            for y in range(places.y):
                block = res[x * krows : (x + 1) * krows, y * cols : (y + 1) * cols]
                places.put(out, ids[3] ^ x, ids[1] ^ y, zr, block, cut_up, 0, cut)

        @pl.when(zr == places.z - 1)
        def _():
            vecs[...] = jnp.zeros(vecs.shape, f32)
            at = 0
            for ref, count in ((one_ref, 3), (two_ref, 3), (g_bu, 1)):
                for i in range(count):
                    for j in range(ref.shape[1] // cols):
                        vecs[at : at + 1, :] = ref[i : i + 1, j * cols : (j + 1) * cols]
                        at += 1
            low = vecs[...].astype(bf16)
            for i in range(2):
                for j in range(2):
                    for z in range(places.z):
                        out[i, j, z, krows + half :] = low
            pltpu.make_async_copy(att_ref, att_vm, att_sem).wait()
            for d in range(places.dp):
                pltpu.make_async_copy(
                    br_ref.at[d * half : (d + 1) * half, :],
                    temp.at[d * half : (d + 1) * half, :],
                    br_sems.at[d],
                ).wait()
            res = nn(temp[...], att_vm[...].reshape(tokens, width)).astype(bf16)
            for z in range(places.z):
                for y in range(places.y):
                    d = z * places.y + y
                    for x in range(places.x):
                        block = res[d * half : (d + 1) * half, x * cols : (x + 1) * cols]
                        places.put(
                            out, ids[3] ^ x, ids[1] ^ y, ids[2] ^ z, block, cut_out,
                            cut_up, cut + krows - cut_up,
                        )

    return pl.pallas_call(
        kernel,
        grid_spec=pltpu.PrefetchScalarGridSpec(
            num_scalar_prefetch=1,
            grid=(places.z,),
            in_specs=[
                pl.BlockSpec(memory_space=pl.ANY),
                resident(),
                pl.BlockSpec(memory_space=pl.ANY),
                pl.BlockSpec(memory_space=pl.ANY),
                whole(one.shape),
                whole(two.shape),
            ]
            + anywhere(after),
            out_specs=whole(shape),
            scratch_shapes=[
                pltpu.VMEM((places.x * krows + 16, tokens), bf16),
                pltpu.VMEM((width // 2, tokens), bf16),
                pltpu.VMEM(att.shape, bf16),
                pltpu.SemaphoreType.DMA((places.x,)),
                pltpu.SemaphoreType.DMA((places.dp,)),
                pltpu.SemaphoreType.DMA,
                pltpu.VMEM((8, ff), f32),
                pltpu.VMEM((32, cols), f32),
            ],
        ),
        out_shape=jax.ShapeDtypeStruct(shape, bf16),
        compiler_params=kernel_params(18),
        cost_estimate=cost(width * tokens * (ff + width), 12e6),
        name="up_grad",
    )(ids, nl_t, dup, br_t, att, one, two, *after)


def square_grad(places, other, cut, ids, d_ts, sources, small, length, g_bq, after=()):
    n_rows, width, _ = d_ts[0].shape
    half = width // (2 * places.dp)
    cols = width // places.x
    count = len(d_ts)
    _, seq, keys = small.shape
    s_half, s_cols = seq // (2 * places.dp), keys // places.x
    extra = s_half // 2
    shape = places.shape(count * half + extra, cols)
    flat_s = [p for source in sources for p, _ in source]
    specs = [
        pl.BlockSpec((1,) + p.shape[1:], lambda i, ids, own=own: (own, 0, 0))
        for source in sources
        for p, own in source
    ]
    split = len(sources[0])
    index = [range(split)] + [range(split, len(flat_s))] * (count - 1)
    lengths = [n_rows * d.shape[2] for d in d_ts]
    after = list(after)

    def kernel(ids, *refs):
        d_refs, refs = refs[:count], refs[count:]
        s_refs, refs = refs[: len(flat_s)], refs[len(flat_s) :]
        small_ref, refs = refs[0], refs[1:]
        g_bq, refs = refs[0], refs[1 + len(after) :]
        outs, refs = refs[:1], refs[1:]
        lhs, (rhs, total, vec, sems) = refs[:count], refs[count:]
        copies = []
        for m in range(count):
            copies.append([])
            start = 0
            for r in range(n_rows):
                src = d_refs[m]
                for d in range(places.dp):
                    first = pl.multiple_of(2 * half * d + half * (ids[0] ^ other), 16)
                    copy = pltpu.make_async_copy(
                        src.at[r, pl.ds(first, half), :],
                        lhs[m].at[d * half : (d + 1) * half, start : start + src.shape[2]],
                        sems.at[m, r, d],
                    )
                    copy.start()
                    copies[-1].append(copy)
                start += src.shape[2]
        total[...] = total_of([small_ref[r] for r in range(n_rows)])
        for i in range(seq // length):
            for j in range(length // (2 * s_half)):
                d = (ids[4] ^ i) * (length // (2 * s_half)) + j
                yr, zr = ids[1] ^ (d % places.y), ids[2] ^ (d // places.y)
                first = i * length + 2 * s_half * j + s_half * (ids[0] ^ other)
                block = total[pl.ds(pl.multiple_of(first, 16), s_half), :].astype(bf16)
                for x in range(places.x):
                    for part in range(2):
                        outs[0][
                            yr,
                            ids[3] ^ x,
                            zr,
                            count * half :,
                            part * s_cols : (part + 1) * s_cols,
                        ] = block[part * extra : (part + 1) * extra, x * s_cols : (x + 1) * s_cols]
        vec[...] = jnp.zeros(vec.shape, f32)
        acc = total_of([g_bq[r] for r in range(n_rows)])
        for i in range(width // 128):
            vec[i : i + 1, :] = acc[:, i * 128 : (i + 1) * 128]
        low = vec[...].astype(bf16)
        for i in range(2):
            for j in range(2):
                for z in range(places.z):
                    outs[0][i, j, z, count * half :, 2 * s_cols : 2 * s_cols + 128] = low
        for m in range(count):
            start = 0
            for i in index[m]:
                rhs[start : start + s_refs[i].shape[1], :] = s_refs[i][0]
                start += s_refs[i].shape[1]
            for copy in copies[m]:
                copy.wait()
            res = nn(lhs[m][...], rhs[:start, :]).astype(bf16)
            for z in range(places.z):
                for y in range(places.y):
                    d = z * places.y + y
                    for x in range(places.x):
                        block = res[d * half : (d + 1) * half, x * cols : (x + 1) * cols]
                        places.put(
                            outs[0], ids[3] ^ x, ids[1] ^ y, ids[2] ^ z, block, cut,
                            m * cut, count * cut + m * (half - cut),
                        )

    return pl.pallas_call(
        kernel,
        grid_spec=pltpu.PrefetchScalarGridSpec(
            num_scalar_prefetch=1,
            grid=(1,),
            in_specs=anywhere(d_ts)
            + specs
            + [whole(small.shape), whole(g_bq.shape)]
            + anywhere(after),
            out_specs=whole(shape),
            scratch_shapes=[pltpu.VMEM((width // 2, n), bf16) for n in lengths]
            + [
                pltpu.VMEM((max(lengths), width), bf16),
                pltpu.VMEM((seq, keys), f32),
                pltpu.VMEM((extra, 128), f32),
                pltpu.SemaphoreType.DMA((count, n_rows, places.dp)),
            ],
        ),
        out_shape=jax.ShapeDtypeStruct(shape, bf16),
        compiler_params=kernel_params(16),
        cost_estimate=cost(2.2e9, 12e6),
        name="square_grad",
    )(ids, *d_ts, *flat_s, small, g_bq, *after)


def gather_rows(ids, parts, after=()):
    n = len(parts)
    rows, length, width = parts[0].shape
    arrays, specs = [], []
    for part in parts:
        if isinstance(part, tuple):
            array, at = part
            arrays.append(array)
            specs.append(
                pl.BlockSpec((1, rows, length, width), lambda i, ids, at=at: (at, 0, 0, 0))
            )
        else:
            arrays.append(part)
            specs.append(whole((rows, length, width)))

    def kernel(ids, *refs):
        out, token = refs[-2:]
        token[...] = jnp.zeros(token.shape, f32)
        for i in range(n):

            @pl.when(pl.program_id(0) == i)
            def _():
                part = refs[i]
                out[...] = (part[0] if len(part.shape) == 4 else part[...]).astype(f32)

    return pl.pallas_call(
        kernel,
        grid_spec=pltpu.PrefetchScalarGridSpec(
            num_scalar_prefetch=1,
            grid=(n,),
            in_specs=specs + anywhere(after),
            out_specs=[
                pl.BlockSpec((rows, length, width), lambda i, ids: (ids[4] ^ i, 0, 0)),
                whole((8, 128)),
            ],
        ),
        out_shape=[out_hbm((n * rows, length, width), f32), jax.ShapeDtypeStruct((8, 128), f32)],
        compiler_params=kernel_params(10),
        cost_estimate=cost(0, 6 * n * rows * length * width),
        name="gather_rows",
    )(ids, *arrays, *after)


def exchange(value, axis, size, relative):
    pairs = [(i, i ^ relative) for i in range(size)]
    return lax.ppermute(value, axis, pairs)


def total_of(parts):
    acc = parts[0].astype(f32)
    for part in parts[1:]:
        acc = acc + part.astype(f32)
    return acc


def call(name, kernel, grid, ins, specs, outs, out_specs, after=(), scratch=()):
    def wrapped(*refs):
        kernel(*refs[: len(ins)], *refs[len(ins) + len(after) :])

    moved = sum(math.prod(shape) * 8 for shape, _ in outs)
    return pl.pallas_call(
        wrapped,
        grid=grid,
        in_specs=list(specs) + anywhere(after),
        out_specs=out_specs,
        out_shape=[jax.ShapeDtypeStruct(shape, dt) for shape, dt in outs],
        scratch_shapes=list(scratch),
        compiler_params=kernel_params(8),
        cost_estimate=cost(moved, moved),
        name=name,
    )(*ins, *after)


class Reduction:
    def __init__(self, places, n_dp, n_krow, cut):
        self.places, self.n_dp, self.n_krow, self.cut = places, n_dp, n_krow, cut

    def along(self, axis, value, relative):
        if axis == "x":
            return exchange(value, "krow", self.n_krow, 2 * relative)
        if axis == "y":
            return exchange(value, "dp", self.n_dp, relative)
        return exchange(value, "dp", self.n_dp, relative * self.places.y)

    def core(self, send):
        self.came = exchange(send, "krow", self.n_krow, 1)

    def first(self, keep, after=()):
        self.keep = keep
        _, _, nz, rows, cols = keep.shape
        cut = self.cut
        self.heights = (cut, rows - cut)

        def kernel(k, c, first, second):
            total = total_of([k[0], c[0]]).astype(bf16)
            first[...] = total[:, :, :cut]
            second[...] = total[:, :, cut:]

        spec = pl.BlockSpec((1, 2, 1, rows, cols), lambda z: (1, 0, z, 0, 0))
        res = call(
            "first_sum", kernel, (nz,), [keep, self.came], [spec] * 2,
            [((2, nz, h, cols), bf16) for h in self.heights],
            [pl.BlockSpec((2, 1, h, cols), lambda z: (0, z, 0, 0)) for h in self.heights],
            after,
        )
        self.one = [self.along(axis, r, 1) for axis, r in zip("xy", res)]
        return res

    def second(self, after=()):
        _, _, nz, rows, cols = self.keep.shape
        cut = self.cut

        def kernel(k, c, g, h, first, second):
            first[0] = total_of([k[0, 0, 0, :cut], c[0, 0, 0, :cut], g[0, 0]]).astype(bf16)
            second[0] = total_of([k[0, 0, 0, cut:], c[0, 0, 0, cut:], h[0, 0]]).astype(bf16)

        spec = pl.BlockSpec((1, 1, 1, rows, cols), lambda z: (0, 1, z, 0, 0))
        res = call(
            "second_sum", kernel, (nz,), [self.keep, self.came] + self.one,
            [spec] * 2
            + [pl.BlockSpec((1, 1, h, cols), lambda z: (1, z, 0, 0)) for h in self.heights],
            [((nz, h, cols), bf16) for h in self.heights],
            [pl.BlockSpec((1, h, cols), lambda z: (z, 0, 0)) for h in self.heights],
            after,
        )
        self.two = [self.along(axis, r, 1) for axis, r in zip("yx", res)]
        return res

    def third(self, after=()):
        _, _, nz, rows, cols = self.keep.shape
        cut = self.cut

        def kernel(k, c, g1, h1, g2, h2, odd, even):
            for z in range(nz):
                out = odd if z % 2 else even
                for part, one, two in ((slice(0, cut), g1, g2), (slice(cut, rows), h1, h2)):
                    value = total_of([k[0, 0, z, part], c[0, 0, z, part], one[0, z], two[z]])
                    out[z // 2, part, :] = value.astype(out.dtype)

        shape = (nz // 2, rows, cols)
        spec = pl.BlockSpec((1, 1, nz, rows, cols), lambda i: (0, 0, 0, 0, 0))
        odd, self.even = call(
            "third_sum", kernel, (1,), [self.keep, self.came] + self.one + self.two,
            [spec] * 2
            + [pl.BlockSpec((1, nz, h, cols), lambda i: (0, 0, 0, 0)) for h in self.heights]
            + [pl.BlockSpec((nz, h, cols), lambda i: (0, 0, 0)) for h in self.heights],
            [(shape, bf16), (shape, f32)], [whole(shape)] * 2, after,
        )
        self.three = self.along("z", odd, 1)
        return [odd]

    def fourth(self, after=()):
        _, rows, cols = self.even.shape

        def kernel(e, g, send, mine):
            send[...] = total_of([e[1], g[1]]).astype(bf16)
            mine[...] = total_of([e[0], g[0]])

        shape = (rows, cols)
        send, mine = call(
            "fourth_sum", kernel, (1,), [self.even, self.three], [whole(self.even.shape)] * 2,
            [(shape, bf16), (shape, f32)], [whole(shape)] * 2, after,
        )
        self.terms = [mine, self.along("z", send, 2)]
        return [send]


def finish_down(red, after=()):
    rows, cols = red.terms[0].shape
    n = len(red.terms)

    def kernel(*refs):
        refs[n][...] = total_of([r[...] for r in refs[:n]])

    return call(
        "finish_down", kernel, (1,), red.terms, [whole((rows, cols))] * n,
        [((rows, cols), f32)], [whole((rows, cols))], after,
    )


def finish_up(red, cuts, krows, half, width, ff, after=()):
    rows, cols = red.terms[0].shape
    n = len(red.terms)
    cut_up, cut_out = cuts
    rest = krows - cut_up
    sizes = (width,) * 6 + (ff,)

    def kernel(*refs):
        up, out = refs[n], refs[n + 1]
        total = total_of([r[...] for r in refs[:n]])
        low = cut_up + cut_out
        up[:cut_up] = total[:cut_up]
        up[cut_up:] = total[low : low + rest]
        out[:cut_out] = total[cut_up:low]
        out[cut_out:] = total[low + rest : krows + half]
        at = krows + half
        for piece, size in zip(refs[n + 2 :], sizes):
            for i in range(size // cols):
                piece[i * cols : (i + 1) * cols] = total[at, :]
                at += 1

    shapes = [(krows, cols), (half, cols)] + [(size,) for size in sizes]
    return call(
        "finish_up", kernel, (1,), red.terms, [whole((rows, cols))] * n,
        [(shape, f32) for shape in shapes], [whole(shape) for shape in shapes], after,
    )


def finish_square(red, ids, out_rows, cut, half, count, s_cols, after=()):
    rows, cols = red.terms[0].shape
    n = len(red.terms)
    extra = rows - count * half
    mine_cols = cols // 2
    width = cols * red.places.x
    height = (count + 1) * half + 2 * extra

    def kernel(ids, out_ref, *refs):
        terms, (mine, other, g_bq, temp) = refs[:n], refs[n:]
        total = total_of([r[...] for r in terms])
        rest = half - cut
        temp[:half] = out_ref[...]
        for m in range(count):
            at = half * (m + 1)
            temp[at : at + cut] = total[m * cut : (m + 1) * cut]
            low = count * cut + m * rest
            temp[at + cut : at + half] = total[low : low + rest]
        core = ids[0]
        square = (count + 1) * half
        lo, hi = temp[:square, :mine_cols], temp[:square, mine_cols:]
        mine[:square, :] = jnp.where(core == 0, lo, hi)
        other[:square, :] = jnp.where(core == 0, hi, lo).astype(bf16)
        h = s_cols // 2
        mine[square:, :] = jnp.zeros((2 * extra, mine_cols), f32)
        other[square:, :] = jnp.zeros((2 * extra, mine_cols), bf16)
        for part in range(2):
            tail = total[count * half :, part * s_cols : (part + 1) * s_cols]
            at = square + part * extra
            lo, hi = tail[:, :h], tail[:, h:]
            mine[at : at + extra, :h] = jnp.where(core == 0, lo, hi)
            other[at : at + extra, :h] = jnp.where(core == 0, hi, lo).astype(bf16)
        for i in range(width // 128):
            g_bq[i * 128 : (i + 1) * 128] = total[count * half + i, 2 * s_cols : 2 * s_cols + 128]

    return call(
        "finish_square", kernel, (1,), [ids, out_rows] + red.terms,
        [pl.BlockSpec(memory_space=pltpu.SMEM), whole(out_rows.shape)]
        + [whole((rows, cols))] * n,
        [((height, mine_cols), f32), ((height, mine_cols), bf16), ((width,), f32)],
        [whole((height, mine_cols))] * 2 + [whole((width,))],
        after,
        [pltpu.VMEM(((count + 1) * half, cols), f32)],
    )


def finish_columns(ids, mine, there, half, count, extra, s_half_cols):
    mine_cols = mine.shape[1]
    square = count * half

    def kernel(ids, mine, there, *refs):
        outs, temp = refs[:-1], refs[-1]
        core = ids[0]

        def merge(at, height, cols, out):
            a, b = mine[at : at + height, :cols], there[at : at + height, :cols].astype(f32)
            low, high = jnp.where(core == 0, a, b), jnp.where(core == 0, b, a)
            out[...] = jnp.concatenate([low, high], axis=0).T

        for m in range(count):
            merge(m * half, half, mine_cols, outs[m])
        merge(square, 2 * extra, s_half_cols, outs[count])

    shapes = [(mine_cols, 2 * half)] * count + [(s_half_cols, 4 * extra)]
    return call(
        "finish_columns", kernel, (1,), [ids, mine, there],
        [pl.BlockSpec(memory_space=pltpu.SMEM), whole(mine.shape), whole(there.shape)],
        [(shape, f32) for shape in shapes], [whole(shape) for shape in shapes],
        (), [pltpu.VMEM((8, 128), f32)],
    )


def local(
    sizes,
    tokens,
    segment_ids,
    segment_live,
    w_query,
    b_query,
    w_key,
    w_value,
    w_out,
    b_out,
    attn_gain,
    attn_shift,
    w_up,
    b_up,
    w_down,
    b_down,
    ffn_gain,
    ffn_shift,
    compress,
    cotangent,
):
    n_dp, n_krow = sizes
    all_rows, length, width = tokens.shape
    rows = all_rows // n_krow
    seq = n_krow * length
    keys = compress.shape[0]
    ff = w_up.shape[1]
    krow, dp = lax.axis_index("krow"), lax.axis_index("dp")
    places = Places(n_dp, n_krow)
    ids = jnp.stack([krow % 2, dp % places.y, dp // places.y, krow // 2, krow]).astype(jnp.int32)
    fast = (
        width % (2 * places.x * 32) == 0
        and ff % (n_dp * 128) == 0
        and ff % (n_krow * 128) == 0
        and width % (2 * n_dp * 16) == 0
        and seq % (2 * n_dp * 32) == 0
        and width % (places.x * 128) == 0
        and keys % (places.x * 128) == 0
        and length % (seq // n_dp) == 0
        and ff // n_dp == width // places.x
        and 2 * (keys // places.x) + 128 <= width // places.x
        and width <= 128 * (seq // (4 * n_dp))
        and places.x == 2
        and places.y == 2
        and places.z == 4
        and rows > 1
    )

    def spread(value):
        parts = []
        for r in range(n_krow):
            part = lax.dynamic_slice_in_dim(value, (krow ^ r) * rows, rows, 0)
            parts.append(exchange(part, "krow", n_krow, r) if r else part)
        return parts

    def back(parts):
        return [exchange(part, "krow", n_krow, r) if r else part for r, part in enumerate(parts)]

    def second_hop(parts, came, *after):
        late = lax.optimization_barrier((came, after))[0]
        core = exchange(parts[1], "krow", n_krow, 1)
        return [parts[0], core, (came, 0), exchange(late[1], "krow", n_krow, 1)]

    def row(value):
        return value.astype(f32).reshape(1, -1)

    toks = spread(tokens)
    cot_source = lax.optimization_barrier((cotangent, toks[-1]))[0]
    cots = spread(cot_source)

    my_ids = lax.dynamic_slice_in_dim(segment_ids, krow * rows, rows, 0)
    my_live = lax.dynamic_slice_in_dim(segment_live, krow * rows, rows, 0)
    labels = jnp.arange(segment_live.shape[1], dtype=jnp.int32)
    live = jnp.sum(
        jnp.where(my_ids[:, :, None] == labels, my_live[:, None, :], 0).astype(f32), axis=-1
    )

    def relative(value, axis):
        return jnp.concatenate(
            [
                lax.dynamic_slice_in_dim(value, (krow ^ r) * length, length, axis)
                for r in range(n_krow)
            ],
            axis=axis,
        )

    live = relative(live, 1)
    comp = relative(compress, 1)
    live_row = live[:, None, :]
    live_col = jnp.broadcast_to(live[:, :, None], (rows, seq, 128))
    comp_t = comp.T
    gain, shift = row(attn_gain), row(attn_shift)

    q_t, pk, k, v, lse, att, xhat, rstd = attn_fwd(
        toks, live_row, comp, w_query, row(b_query), w_key, w_value, w_out, row(b_out)
    )
    n_parts = 3 if fast else n_krow
    res = ffn_fwd(
        fast, cots, xhat, gain, shift, w_up, row(b_up), w_down, row(b_down), row(ffn_gain), row(ffn_shift)
    )
    outs, (act, gp, dh2, d_t, sums_two) = res[:n_parts], res[n_parts:]
    out_came = exchange(outs[2], "krow", n_krow, 2) if fast else None
    ahead = []
    if fast:
        cut_down = 32
        cuts_up = (width // n_krow // 2, 32)
        cut_square = 16
        half = width // (2 * n_dp)
        down = Reduction(places, n_dp, n_krow, cut_down)
        up = Reduction(places, n_dp, n_krow, sum(cuts_up))
        square = Reduction(places, n_dp, n_krow, 3 * cut_square)
        send = down_grad(places, 1, cut_down, ids, d_t, act)
        down.core(send)
        keep = down_grad(places, 0, cut_down, ids, d_t, act, after=[send])
        ahead = list(down.first(keep))

    dup, dh1, da_t, nl_t, br_t, sums_one = ffn_bwd(
        gp, dh2, xhat, rstd, gain, shift, w_up, w_down, w_out, after=ahead
    )

    if fast:
        ahead = down.second([sums_one, out_came])
        out_parts = second_hop(outs, out_came, *ahead)
        parts = nl_t, dup, br_t, att, sums_one, sums_two
        send = up_grad(places, 1, cuts_up, ids, *parts, after=ahead)
        up.core(send)
        keep = up_grad(places, 0, cuts_up, ids, *parts, after=[send])
        ahead = up.first(keep)
        ahead = down.third(ahead)

    res = attn_bwd(
        fast, toks, q_t, k, v, lse, da_t, comp_t, live_col, w_query, w_key, w_value, dh1, after=ahead
    )
    grad_parts, bwd = res[:n_parts], res[n_parts:]

    if fast:
        sources = [[(t, r) for r in range(rows) for t in toks], [(pk, r) for r in range(rows)]]
        ahead = up.second([bwd[3], down.three])
        ahead = down.fourth(ahead)
        parts = bwd[:3], sources, bwd[4], length, bwd[3]
        send = square_grad(places, 1, cut_square, ids, *parts, after=ahead)
        square.core(send)
        keep = square_grad(places, 0, cut_square, ids, *parts, after=[send])
        (g_down,) = finish_down(down, after=[send])
        ahead = square.first(keep, [g_down])
        ahead = up.third(ahead)
        grad_parts = lax.optimization_barrier((grad_parts, ahead))[0]
        grad_came = exchange(grad_parts[2], "krow", n_krow, 2)
        output, token = gather_rows(ids, out_parts, after=ahead)
        ahead = up.fourth([token])
        ahead = square.second(ahead)
        grad_parts = second_hop(grad_parts, grad_came, *ahead)
        g_up, out_rows, *pieces = finish_up(
            up, cuts_up, width // n_krow, half, width, ff, after=ahead
        )
        ahead = square.third([out_rows])
        grad_tokens, token = gather_rows(ids, grad_parts, after=ahead)
        square.fourth([token])
        g_down = g_down.T
        s_cols = keys // places.x
        mine, other, g_bq = finish_square(square, ids, out_rows, cut_square, half, 3, s_cols)
        pieces = [g_bq] + pieces
        there = exchange(other, "krow", n_krow, 1)
        g_out, g_q, g_k, g_v, g_comp = finish_columns(
            ids, mine, there, half, 4, seq // (4 * n_dp), s_cols // 2
        )
    else:
        grad_parts = back(grad_parts)
        g_bu = jnp.sum(dup.astype(f32), axis=(0, 1)).reshape(-1, width)
        g_bq = jnp.sum(bwd[3], axis=0)
        vectors = jnp.concatenate([g_bq, sums_one[:3], sums_two[:3], g_bu], axis=0)
        output, _ = gather_rows(ids, back(outs))
        grad_tokens, _ = gather_rows(ids, grad_parts)
        vectors = lax.psum(vectors.reshape(-1), ("dp", "krow"))
        pieces = []
        start = 0
        for size in (width,) * 7 + (ff,):
            pieces.append(vectors[start : start + size])
            start += size

        def scattered(value):
            value = value.astype(bf16)
            part = lax.psum_scatter(value, "krow", scatter_dimension=0, tiled=True)
            return lax.psum_scatter(part, "dp", scatter_dimension=1, tiled=True).astype(f32)

        def product(a, b):
            return lax.dot_general(a, b, (((1,), (0,)), ((), ())), preferred_element_type=f32)

        token_rows = jnp.concatenate(toks, axis=1)
        d_q, d_k, d_v = [jnp.swapaxes(d, 0, 1).reshape(width, -1) for d in bwd[:3]]
        pk = pk.reshape(-1, width)
        g_q = scattered(product(d_q, token_rows.reshape(-1, width)).T)
        g_k = scattered(product(d_k, pk).T)
        g_v = scattered(product(d_v, pk).T)
        g_out = scattered(product(br_t, att.reshape(-1, width)).T)
        g_up = scattered(product(nl_t, dup.reshape(-1, ff)))
        g_down = scattered(product(d_t, act.reshape(-1, ff)).T)
        blocks = jnp.sum(bwd[4].astype(f32), axis=0).reshape(n_krow, length, keys)
        blocks = jnp.concatenate(
            [lax.dynamic_slice_in_dim(blocks, krow ^ r, 1, 0) for r in range(n_krow)]
        )
        g_comp = scattered(blocks.reshape(seq, keys).T)

    g_bq, g_gain, g_shift, g_bo, g_fgain, g_fshift, g_bd, g_bu = pieces
    return (
        output,
        grad_tokens,
        g_q,
        g_bq,
        g_k,
        g_v,
        g_out,
        g_bo,
        g_gain,
        g_shift,
        g_up,
        g_bu,
        g_down,
        g_bd,
        g_fgain,
        g_fshift,
        g_comp,
    )


def solution(mesh):
    rows = P("dp", "krow", None)
    per_row = P("dp", None)
    block = P("krow", "dp")
    in_specs = (rows, per_row, per_row) + (P(),) * 15 + (rows,)
    out_specs = (
        (rows, rows, block, P(), block, block, block)
        + (P(),) * 3
        + (block, P(), block)
        + (P(),) * 3
        + (block,)
    )
    sizes = (mesh.shape["dp"], mesh.shape["krow"])
    return jax.shard_map(
        functools.partial(local, sizes),
        mesh=mesh,
        in_specs=in_specs,
        out_specs=out_specs,
        check_vma=False,
    )
```

```python
import functools
import math

import jax
import jax.numpy as jnp
from jax import lax
from jax.experimental import pallas as pl
from jax.experimental.pallas import tpu as pltpu
from jax.sharding import PartitionSpec as P

H = 12
HD = 64
f32 = jnp.float32
bf16 = jnp.bfloat16


def nn(a, b):
    return lax.dot_general(a, b, (((1,), (0,)), ((), ())), preferred_element_type=f32)


def nt(a, b):
    return lax.dot_general(a, b, (((1,), (1,)), ((), ())), preferred_element_type=f32)


def whole(shape):
    rank = len(shape)
    return pl.BlockSpec(shape, lambda *_: (0,) * rank, pipeline_mode=pl.Buffered(1))


def fetch_strips(src, dst, sems, ids, other, half, dp):
    copies = []
    for d in range(dp):
        first = pl.multiple_of(2 * half * d + half * (ids[0] ^ other), 16)
        copies.append(
            pltpu.make_async_copy(
                src.at[pl.ds(first, half), :], dst.at[d * half : (d + 1) * half, :], sems.at[d]
            )
        )
        copies[-1].start()
    return copies


def resident():
    return pl.BlockSpec(memory_space=pltpu.VMEM)


def out_hbm(shape, dtype):
    return pltpu.HBM(shape, dtype)


def in_hbm(*values):
    return [pltpu.with_memory_space_constraint(v, pltpu.HBM) for v in values]


def fetch(sources, places, sems):
    copies = [
        pltpu.make_async_copy(src, dst, sems.at[i])
        for i, (src, dst) in enumerate(zip(sources, places))
    ]

    @pl.when(pl.program_id(0) == 0)
    def _():
        for copy in copies:
            copy.start()

    def wait(*which):
        @pl.when(pl.program_id(0) == 0)
        def _():
            for i in which:
                copies[i].wait()

    return wait


def anywhere(values):
    return [pl.BlockSpec(memory_space=pl.ANY)] * len(values)


def row_block(*shape):
    rank = len(shape)
    return pl.BlockSpec((1,) + shape, lambda r, *_: (r,) + (0,) * rank)


def parts_of(n, rows, length, width, paired):
    single = (row_block(length, width), (rows, length, width))
    if not paired:
        return [single[0]] * n, [single[1]] * n
    both = (pl.BlockSpec((2, 1, length, width), lambda r, *_: (0, r, 0, 0)), (2, rows, length, width))
    return [single[0]] * 2 + [both[0]], [single[1]] * 2 + [both[1]]


def put_part(outs, n, i, value):
    if len(outs) == n or i < 2:
        outs[i][0] = value
    else:
        outs[2][i - 2, 0] = value


def kernel_params(mebibytes):
    return pltpu.CompilerParams(dimension_semantics=("arbitrary",), vmem_limit_bytes=mebibytes * 1024 * 1024)


def cost(flops, moved, trans=0):
    return pl.CostEstimate(flops=int(flops), bytes_accessed=int(moved), transcendentals=int(trans))


def add_to(ref, value, first):
    @pl.when(first)
    def _():
        ref[...] = value

    @pl.when(jnp.logical_not(first))
    def _():
        ref[...] += value


def col_sum(value):
    return jnp.sum(value, axis=0, keepdims=True)


def gelu_parts(u):
    phi = 0.5 + 0.5 * lax.erf(u * (1.0 / math.sqrt(2.0)))
    density = jnp.exp(-0.5 * u * u) * (1.0 / math.sqrt(2.0 * math.pi))
    return u * phi, phi + u * density


def attn_fwd_kernel(n, *refs):
    toks = refs[:n]
    live, comp, wq_hbm, bq, wk_hbm, wv_hbm, wo_hbm, bo = refs[n : n + 8]
    q_t, pk, k, v, lse, att, xhat, rstd = refs[n + 8 : n + 16]
    tok, att_t, wq, wk, wv, wo, sems = refs[n + 16 :]
    wait = fetch((wq_hbm, wk_hbm, wv_hbm, wo_hbm), (wq, wk, wv, wo), sems)
    length = toks[0].shape[1]
    for i in range(n):
        tok[i * length : (i + 1) * length, :] = toks[i][0]
    masked = (comp[...].astype(f32) * live[0]).astype(bf16)
    x = tok[...]
    pk[0] = nn(masked, x).astype(bf16)
    wait(0, 1, 2)
    for c in range(3):
        cols = slice(256 * c, 256 * c + 256)
        q = (nn(x, wq[:, cols]) + bq[:, cols]).astype(bf16) * jnp.asarray(1.0 / math.sqrt(HD), bf16)
        q_t[0, cols, :] = q.T
        k[0, :, cols] = nn(pk[0], wk[:, cols]).astype(bf16)
        v[0, :, cols] = nn(pk[0], wv[:, cols]).astype(bf16)
    lane = lax.broadcasted_iota(jnp.int32, (1, 2 * HD), 1)
    for pair in range(H // 2):
        cols = slice(2 * HD * pair, 2 * HD * (pair + 1))
        k_pair = k[0, :, cols]
        v_t = v[0, :, cols].T
        for half in range(2):
            h = 2 * pair + half
            mine = jnp.where((lane // HD) == half, k_pair, jnp.zeros_like(k_pair))
            s = nn(mine, q_t[0, cols, :])
            top = jnp.max(s, axis=0, keepdims=True)
            e = jnp.exp(s - top)
            total = jnp.sum(e, axis=0, keepdims=True)
            w = (e * (1.0 / total)).astype(bf16)
            lse[0, h : h + 1, :] = top + jnp.log(total)
            att_t[h * HD : (h + 1) * HD, :] = nn(v_t[half * HD : (half + 1) * HD, :], w).astype(bf16)
    for c in range(3):
        cols = slice(256 * c, 256 * c + 256)
        att[0, :, cols] = att_t[cols, :].T
    wait(3)
    hidden = x.astype(f32) + nn(att[0], wo[...]) + bo[...]
    average = jnp.mean(hidden, axis=-1, keepdims=True)
    centred = hidden - average
    spread = jnp.mean(centred * centred, axis=-1, keepdims=True)
    r = lax.rsqrt(spread + 1e-05)
    xhat[0] = centred * r
    rstd[0] = jnp.broadcast_to(r, rstd.shape[1:])


def attn_fwd(toks, live, comp, wq, bq, wk, wv, wo, bo):
    rows, length, width = toks[0].shape
    n = len(toks)
    seq = n * length
    keys = comp.shape[0]
    in_specs = [row_block(length, width)] * n + [
        row_block(1, seq),
        whole((keys, seq)),
        pl.BlockSpec(memory_space=pl.ANY),
        whole((1, width)),
        pl.BlockSpec(memory_space=pl.ANY),
        pl.BlockSpec(memory_space=pl.ANY),
        pl.BlockSpec(memory_space=pl.ANY),
        whole((1, width)),
    ]
    outs = [
        ((width, seq), bf16),
        ((keys, width), bf16),
        ((keys, width), bf16),
        ((keys, width), bf16),
        ((16, seq), f32),
        ((seq, width), bf16),
        ((seq, width), f32),
        ((seq, 128), f32),
    ]
    return pl.pallas_call(
        functools.partial(attn_fwd_kernel, n),
        grid=(rows,),
        in_specs=in_specs,
        out_specs=[row_block(*shape) for shape, _ in outs],
        out_shape=[out_hbm((rows,) + shape, dt) for shape, dt in outs],
        scratch_shapes=[pltpu.VMEM((seq, width), bf16), pltpu.VMEM((width, seq), bf16)]
        + [pltpu.VMEM((width, width), bf16)] * 4
        + [pltpu.SemaphoreType.DMA((4,))],
        compiler_params=kernel_params(30),
        cost_estimate=cost(rows * 5e9, 12e6, rows * H * seq * keys),
        name="attn_fwd",
    )(*toks, live, comp, *in_hbm(wq), bq, *in_hbm(wk, wv, wo), bo)


def ffn_fwd_kernel(n, n_out, *refs):
    cots = refs[:n]
    xhat, gain, shift, wu, bu, wd, bd, fgain, fshift = refs[n : n + 9]
    refs = refs[n + 9 :]
    outs = refs[:n_out]
    act, gp, dh2, d_t, sums = refs[n_out:]
    r = pl.program_id(0)
    first = r == 0
    length = cots[0].shape[1]
    ff = wu.shape[1]
    chunk = 512
    count = ff // chunk
    normed = xhat[0] * gain[...] + shift[...]
    low = normed.astype(bf16)

    def up(c):
        cols = slice(c * chunk, (c + 1) * chunk)
        return nn(low, wu[:, cols]) + bu[:, cols]

    for c in range(count):
        cols = slice(c * chunk, (c + 1) * chunk)
        a, g = gelu_parts(up(c))
        act[r, :, cols] = a.astype(bf16)
        gp[0, :, cols] = g.astype(bf16)
    total = normed + bd[...] + nn(act[r], wd[...])
    average = jnp.mean(total, axis=-1, keepdims=True)
    centred = total - average
    spread = jnp.mean(centred * centred, axis=-1, keepdims=True)
    rs = lax.rsqrt(spread + 1e-05)
    hat = centred * rs
    result = (hat * fgain[...] + fshift[...]).astype(bf16)
    for i in range(n):
        put_part(outs, n, i, result[i * length : (i + 1) * length, :])
    cot = jnp.concatenate([c[0] for c in cots], axis=0).astype(f32)
    dhat = cot * fgain[...]
    d = rs * (
        dhat
        - jnp.mean(dhat, axis=-1, keepdims=True)
        - hat * jnp.mean(dhat * hat, axis=-1, keepdims=True)
    )
    dh2[0] = d
    d_low = d.astype(bf16)
    seq = d_low.shape[0]
    d_t[:, pl.ds(pl.multiple_of(r * seq, seq), seq)] = d_low.T
    add_to(
        sums,
        jnp.concatenate(
            [col_sum(cot * hat), col_sum(cot), col_sum(d_low.astype(f32)), jnp.zeros((5, d.shape[1]), f32)],
            axis=0,
        ),
        first,
    )


def ffn_fwd(paired, cots, xhat, gain, shift, wu, bu, wd, bd, fgain, fshift):
    rows, length, width = cots[0].shape
    n = len(cots)
    seq = n * length
    ff = wu.shape[1]
    vec = whole((1, width))
    in_specs = [row_block(length, width)] * n + [
        row_block(seq, width),
        vec,
        vec,
        resident(),
        whole((1, ff)),
        resident(),
        vec,
        vec,
        vec,
    ]
    specs, shapes = parts_of(n, rows, length, width, paired)
    more = [((seq, ff), bf16), ((seq, width), f32)]
    return pl.pallas_call(
        functools.partial(ffn_fwd_kernel, n, len(shapes)),
        grid=(rows,),
        in_specs=in_specs,
        out_specs=specs
        + [resident()]
        + [row_block(*shape) for shape, _ in more]
        + [resident()]
        + [whole((8, width))],
        out_shape=[jax.ShapeDtypeStruct(shape, bf16) for shape in shapes]
        + [pltpu.VMEM((rows, seq, ff), bf16)]
        + [jax.ShapeDtypeStruct((rows,) + shape, dt) for shape, dt in more]
        + [jax.ShapeDtypeStruct((width, rows * seq), bf16)]
        + [jax.ShapeDtypeStruct((8, width), f32)],
        compiler_params=kernel_params(26),
        cost_estimate=cost(rows * seq * width * ff * 4, 34e6, rows * seq * ff * 2),
        name="ffn_fwd",
    )(*cots, xhat, gain, shift, wu, bu, wd, bd, fgain, fshift)


def ffn_bwd_kernel(*refs):
    gp, dh2, xhat, rstd, gain, shift, wu, wd, wo = refs[:9]
    dup, dh1, da_t, nl_t, br_t, sums = refs[-6:]
    r = pl.program_id(0)
    first = r == 0
    ff = wu.shape[1]
    chunk = 512
    count = ff // chunk
    d_low = dh2[0].astype(bf16)

    def back(c):
        return nt(d_low, wd[c * chunk : (c + 1) * chunk, :])

    for c in range(count):
        cols = slice(c * chunk, (c + 1) * chunk)
        dup[r, :, cols] = (gp[0, :, cols].astype(f32) * back(c)).astype(bf16)
    tile = min(256, dh2.shape[1])
    for i in range(dh2.shape[1] // tile):
        part = slice(i * tile, (i + 1) * tile)
        for j in range(dh2.shape[2] // 256):
            cols = slice(j * 256, (j + 1) * 256)
            dh1[0, part, cols] = dh2[0, part, cols] + nt(dup[r, part, :], wu[cols, :])
    dn = dh1[0]
    hat = xhat[0]
    dhat = dn * gain[...]
    d = rstd[0, :, 0:1] * (
        dhat
        - jnp.mean(dhat, axis=-1, keepdims=True)
        - hat * jnp.mean(dhat * hat, axis=-1, keepdims=True)
    )
    dh1[0] = d
    branch = d.astype(bf16)
    add_to(
        sums,
        jnp.concatenate(
            [col_sum(dn * hat), col_sum(dn), col_sum(branch.astype(f32)), jnp.zeros((5, d.shape[1]), f32)],
            axis=0,
        ),
        first,
    )
    da_t[0] = nt(wo[...], branch).astype(bf16)
    br_t[...] = branch.T
    nl_t[...] = (hat * gain[...] + shift[...]).astype(bf16).T


def ffn_bwd(gp, dh2, xhat, rstd, gain, shift, wu, wd, wo, after=()):
    rows, seq, ff = gp.shape
    width = wu.shape[0]
    vec = whole((1, width))
    in_specs = [
        row_block(seq, ff),
        row_block(seq, width),
        row_block(seq, width),
        row_block(seq, 128),
        vec,
        vec,
        resident(),
        resident(),
        resident(),
    ] + anywhere(after)
    outs = [((seq, width), f32), ((width, seq), bf16)]
    turned = pl.BlockSpec((width, seq), lambda r: (0, r))
    return pl.pallas_call(
        ffn_bwd_kernel,
        grid=(rows,),
        in_specs=in_specs,
        out_specs=[resident()]
        + [row_block(*shape) for shape, _ in outs]
        + [turned] * 2
        + [whole((8, width))],
        out_shape=[pltpu.VMEM((rows, seq, ff), bf16)]
        + [jax.ShapeDtypeStruct((rows,) + shape, dt) for shape, dt in outs]
        + [jax.ShapeDtypeStruct((width, rows * seq), bf16)] * 2
        + [jax.ShapeDtypeStruct((8, width), f32)],
        compiler_params=kernel_params(26),
        cost_estimate=cost(rows * seq * width * ff * 4.5, 34e6),
        name="ffn_bwd",
    )(gp, dh2, xhat, rstd, gain, shift, wu, wd, wo, *after)


def attn_bwd_kernel(n, n_out, *refs):
    toks = refs[:n]
    q_t, k, v, lse, da_t, comp_t, live_col, wq, wk, wv, dh1 = refs[n : n + 11]
    refs = refs[-(n_out + 6) :]
    outs = refs[:n_out]
    dq_t, dk_t, dv_t, g_bq, small, tok = refs[n_out:]
    length = toks[0].shape[1]
    for i in range(n):
        tok[i * length : (i + 1) * length, :] = toks[i][0]
    lane = lax.broadcasted_iota(jnp.int32, (1, 2 * HD), 1)
    scale = jnp.asarray(1.0 / math.sqrt(HD), f32)
    for pair in range(H // 2):
        cols = slice(2 * HD * pair, 2 * HD * (pair + 1))
        k_pair = k[0, :, cols]
        v_pair = v[0, :, cols]
        k_t = k_pair.T
        for half in range(2):
            h = 2 * pair + half
            head = slice(h * HD, (h + 1) * HD)
            mine = (lane // HD) == half
            s = nn(jnp.where(mine, k_pair, jnp.zeros_like(k_pair)), q_t[0, cols, :])
            w = jnp.exp(s - lse[0, h : h + 1, :])
            dw = nn(jnp.where(mine, v_pair, jnp.zeros_like(v_pair)), da_t[0, cols, :])
            dot = jnp.sum(w * dw, axis=0, keepdims=True)
            ds = (w * (dw - dot)).astype(bf16)
            dv_t[0, head, :] = nt(da_t[0, head, :], w.astype(bf16)).astype(bf16)
            dk_t[0, head, :] = nt(q_t[0, head, :], ds).astype(bf16)
            dq_t[0, head, :] = (nn(k_t[half * HD : (half + 1) * HD, :], ds) * scale).astype(bf16)
    dp_t = (nn(wk[...], dk_t[0]) + nn(wv[...], dv_t[0])).astype(bf16)
    small[0] = (nn(tok[...], dp_t) * live_col[0, :, 0:1]).astype(bf16)
    masked = (comp_t[...].astype(f32) * live_col[0, :, 0:1]).astype(bf16)
    dq = dq_t[0].T
    g_bq[0] = col_sum(dq.astype(f32))
    grad = dh1[0] + nt(dq, wq[...]) + nt(masked, dp_t)
    for i in range(n):
        put_part(outs, n, i, grad[i * length : (i + 1) * length, :].astype(bf16))


def attn_bwd(paired, toks, q_t, k, v, lse, da_t, comp_t, live_col, wq, wk, wv, dh1, after=()):
    rows, length, width = toks[0].shape
    n = len(toks)
    seq = n * length
    keys = comp_t.shape[1]
    in_specs = (
        [row_block(length, width)] * n
        + [
            row_block(width, seq),
            row_block(keys, width),
            row_block(keys, width),
            row_block(16, seq),
            row_block(width, seq),
            whole((seq, keys)),
            row_block(seq, 128),
            whole((width, width)),
            whole((width, width)),
            whole((width, width)),
            row_block(seq, width),
        ]
        + anywhere(after)
    )
    specs, shapes = parts_of(n, rows, length, width, paired)
    outs = [
        ((width, seq), bf16),
        ((width, keys), bf16),
        ((width, keys), bf16),
        ((1, width), f32),
        ((seq, keys), bf16),
    ]
    return pl.pallas_call(
        functools.partial(attn_bwd_kernel, n, len(shapes)),
        grid=(rows,),
        in_specs=in_specs,
        out_specs=specs + [row_block(*shape) for shape, _ in outs],
        out_shape=[jax.ShapeDtypeStruct(shape, bf16) for shape in shapes]
        + [jax.ShapeDtypeStruct((rows,) + shape, dt) for shape, dt in outs],
        scratch_shapes=[pltpu.VMEM((seq, width), bf16)],
        compiler_params=kernel_params(28),
        cost_estimate=cost(rows * 8e9, 24e6, rows * H * seq * keys),
        name="attn_bwd",
    )(*toks, q_t, k, v, lse, da_t, comp_t, live_col, wq, wk, wv, dh1, *after)


class Places:
    def __init__(self, n_dp, n_krow):
        self.x = n_krow // 2
        self.y = n_krow // 2
        self.z = n_dp // self.y
        self.dp = n_dp

    def shape(self, rows, cols):
        return (2, 2, self.z, rows, cols)

    def put(self, out, x, y, z, block, cut, low, high):
        out[x, y, z, low : low + cut] = block[:cut]
        out[y, x, z, high : high + block.shape[0] - cut] = block[cut:]


def down_grad(places, other, cut, ids, d_t, act, after=()):
    width, tokens = d_t.shape
    rows, seq, ff = act.shape
    cols = ff // (2 * places.x)
    height = width // places.dp
    shape = places.shape(height, cols)

    def kernel(ids, d_ref, act_ref, *refs):
        xr = pl.program_id(0)
        start = pl.multiple_of((2 * (ids[3] ^ xr) + (ids[0] ^ other)) * cols, 128)
        block = act_ref[:, :, pl.ds(start, cols)].reshape(rows * seq, cols)
        res = nn(d_ref[...], block).astype(bf16)
        for z in range(places.z):
            for y in range(places.y):
                d = z * places.y + y
                block = res[d * height : (d + 1) * height, :]
                places.put(refs[-1], xr, ids[1] ^ y, ids[2] ^ z, block, cut, 0, cut)

    return pl.pallas_call(
        kernel,
        grid_spec=pltpu.PrefetchScalarGridSpec(
            num_scalar_prefetch=1,
            grid=(places.x,),
            in_specs=[
                resident(),
                resident(),
            ]
            + anywhere(after),
            out_specs=whole(shape),
        ),
        out_shape=jax.ShapeDtypeStruct(shape, bf16),
        compiler_params=kernel_params(16),
        cost_estimate=cost(width * tokens * ff, 8e6),
        name="down_grad",
    )(ids, d_t, act, *after)


def up_grad(places, other, cuts, ids, nl_t, dup, br_t, att, one, two, after=()):
    width, tokens = nl_t.shape
    rows, seq, ff = dup.shape
    krows = width // (2 * places.x)
    cols = ff // places.dp
    half = width // (2 * places.dp)
    step = cols * places.y
    cut_up, cut_out = cuts
    shape = places.shape(krows + half + 32, cols)
    cut = cut_up + cut_out

    def kernel(ids, nl_ref, dup_ref, br_ref, att_ref, one_ref, two_ref, *refs):
        out = refs[-9]
        lhs, temp, att_vm, nl_sems, br_sems, att_sem, g_bu, vecs = refs[-8:]
        zr = pl.program_id(0)

        @pl.when(zr == 0)
        def _():
            copies = []
            for x in range(places.x):
                first = pl.multiple_of((2 * x + (ids[0] ^ other)) * krows, 16)
                copies.append(
                    pltpu.make_async_copy(
                        nl_ref.at[pl.ds(first, krows), :],
                        lhs.at[x * krows : (x + 1) * krows, :],
                        nl_sems.at[x],
                    )
                )
                copies[-1].start()
            fetch_strips(br_ref, temp, br_sems, ids, other, half, places.dp)
            pltpu.make_async_copy(att_ref, att_vm, att_sem).start()
            lhs[places.x * krows :, :] = jnp.ones((16, tokens), bf16)
            for copy in copies:
                copy.wait()

        start = pl.multiple_of((ids[2] ^ zr) * step, 128)
        res = nn(lhs[...], dup_ref[:, :, pl.ds(start, step)].reshape(tokens, step))
        g_bu[:, pl.ds(start, step)] = res[places.x * krows : places.x * krows + 8]
        res = res.astype(bf16)
        for x in range(places.x):
            for y in range(places.y):
                block = res[x * krows : (x + 1) * krows, y * cols : (y + 1) * cols]
                places.put(out, ids[3] ^ x, ids[1] ^ y, zr, block, cut_up, 0, cut)

        @pl.when(zr == places.z - 1)
        def _():
            vecs[...] = jnp.zeros(vecs.shape, f32)
            at = 0
            for ref, count in ((one_ref, 3), (two_ref, 3), (g_bu, 1)):
                for i in range(count):
                    for j in range(ref.shape[1] // cols):
                        vecs[at : at + 1, :] = ref[i : i + 1, j * cols : (j + 1) * cols]
                        at += 1
            low = vecs[...].astype(bf16)
            for i in range(2):
                for j in range(2):
                    for z in range(places.z):
                        out[i, j, z, krows + half :] = low
            pltpu.make_async_copy(att_ref, att_vm, att_sem).wait()
            for d in range(places.dp):
                pltpu.make_async_copy(
                    br_ref.at[d * half : (d + 1) * half, :],
                    temp.at[d * half : (d + 1) * half, :],
                    br_sems.at[d],
                ).wait()
            res = nn(temp[...], att_vm[...].reshape(tokens, width)).astype(bf16)
            for z in range(places.z):
                for y in range(places.y):
                    d = z * places.y + y
                    for x in range(places.x):
                        block = res[d * half : (d + 1) * half, x * cols : (x + 1) * cols]
                        places.put(
                            out, ids[3] ^ x, ids[1] ^ y, ids[2] ^ z, block, cut_out,
                            cut_up, cut + krows - cut_up,
                        )

    return pl.pallas_call(
        kernel,
        grid_spec=pltpu.PrefetchScalarGridSpec(
            num_scalar_prefetch=1,
            grid=(places.z,),
            in_specs=[
                pl.BlockSpec(memory_space=pl.ANY),
                resident(),
                pl.BlockSpec(memory_space=pl.ANY),
                pl.BlockSpec(memory_space=pl.ANY),
                whole(one.shape),
                whole(two.shape),
            ]
            + anywhere(after),
            out_specs=whole(shape),
            scratch_shapes=[
                pltpu.VMEM((places.x * krows + 16, tokens), bf16),
                pltpu.VMEM((width // 2, tokens), bf16),
                pltpu.VMEM(att.shape, bf16),
                pltpu.SemaphoreType.DMA((places.x,)),
                pltpu.SemaphoreType.DMA((places.dp,)),
                pltpu.SemaphoreType.DMA,
                pltpu.VMEM((8, ff), f32),
                pltpu.VMEM((32, cols), f32),
            ],
        ),
        out_shape=jax.ShapeDtypeStruct(shape, bf16),
        compiler_params=kernel_params(18),
        cost_estimate=cost(width * tokens * (ff + width), 12e6),
        name="up_grad",
    )(ids, nl_t, dup, br_t, *in_hbm(att), one, two, *after)


def square_grad(places, other, cut, ids, d_ts, sources, small, length, g_bq, after=()):
    n_rows, width, _ = d_ts[0].shape
    half = width // (2 * places.dp)
    cols = width // places.x
    count = len(d_ts)
    _, seq, keys = small.shape
    s_half, s_cols = seq // (2 * places.dp), keys // places.x
    extra = s_half // 2
    shape = places.shape(count * half + extra, cols)
    flat_s = [p for source in sources for p, _ in source]
    specs = [
        pl.BlockSpec((1,) + p.shape[1:], lambda i, ids, own=own: (own, 0, 0))
        for source in sources
        for p, own in source
    ]
    split = len(sources[0])
    index = [range(split)] + [range(split, len(flat_s))] * (count - 1)
    lengths = [n_rows * d.shape[2] for d in d_ts]
    after = list(after)

    def kernel(ids, *refs):
        d_refs, refs = refs[:count], refs[count:]
        s_refs, refs = refs[: len(flat_s)], refs[len(flat_s) :]
        small_ref, refs = refs[0], refs[1:]
        g_bq, refs = refs[0], refs[1 + len(after) :]
        outs, refs = refs[:1], refs[1:]
        lhs, (rhs, total, vec, sems) = refs[:count], refs[count:]
        copies = []
        for m in range(count):
            copies.append([])
            start = 0
            for r in range(n_rows):
                src = d_refs[m]
                for d in range(places.dp):
                    first = pl.multiple_of(2 * half * d + half * (ids[0] ^ other), 16)
                    copy = pltpu.make_async_copy(
                        src.at[r, pl.ds(first, half), :],
                        lhs[m].at[d * half : (d + 1) * half, start : start + src.shape[2]],
                        sems.at[m, r, d],
                    )
                    copy.start()
                    copies[-1].append(copy)
                start += src.shape[2]
        total[...] = total_of([small_ref[r] for r in range(n_rows)])
        for i in range(seq // length):
            for j in range(length // (2 * s_half)):
                d = (ids[4] ^ i) * (length // (2 * s_half)) + j
                yr, zr = ids[1] ^ (d % places.y), ids[2] ^ (d // places.y)
                first = i * length + 2 * s_half * j + s_half * (ids[0] ^ other)
                block = total[pl.ds(pl.multiple_of(first, 16), s_half), :].astype(bf16)
                for x in range(places.x):
                    for part in range(2):
                        outs[0][
                            yr,
                            ids[3] ^ x,
                            zr,
                            count * half :,
                            part * s_cols : (part + 1) * s_cols,
                        ] = block[part * extra : (part + 1) * extra, x * s_cols : (x + 1) * s_cols]
        vec[...] = jnp.zeros(vec.shape, f32)
        acc = total_of([g_bq[r] for r in range(n_rows)])
        for i in range(width // 128):
            vec[i : i + 1, :] = acc[:, i * 128 : (i + 1) * 128]
        low = vec[...].astype(bf16)
        for i in range(2):
            for j in range(2):
                for z in range(places.z):
                    outs[0][i, j, z, count * half :, 2 * s_cols : 2 * s_cols + 128] = low
        for m in range(count):
            start = 0
            for i in index[m]:
                rhs[start : start + s_refs[i].shape[1], :] = s_refs[i][0]
                start += s_refs[i].shape[1]
            for copy in copies[m]:
                copy.wait()
            res = nn(lhs[m][...], rhs[:start, :]).astype(bf16)
            for z in range(places.z):
                for y in range(places.y):
                    d = z * places.y + y
                    for x in range(places.x):
                        block = res[d * half : (d + 1) * half, x * cols : (x + 1) * cols]
                        places.put(
                            outs[0], ids[3] ^ x, ids[1] ^ y, ids[2] ^ z, block, cut,
                            m * cut, count * cut + m * (half - cut),
                        )

    return pl.pallas_call(
        kernel,
        grid_spec=pltpu.PrefetchScalarGridSpec(
            num_scalar_prefetch=1,
            grid=(1,),
            in_specs=anywhere(d_ts)
            + specs
            + [whole(small.shape), whole(g_bq.shape)]
            + anywhere(after),
            out_specs=whole(shape),
            scratch_shapes=[pltpu.VMEM((width // 2, n), bf16) for n in lengths]
            + [
                pltpu.VMEM((max(lengths), width), bf16),
                pltpu.VMEM((seq, keys), f32),
                pltpu.VMEM((extra, 128), f32),
                pltpu.SemaphoreType.DMA((count, n_rows, places.dp)),
            ],
        ),
        out_shape=jax.ShapeDtypeStruct(shape, bf16),
        compiler_params=kernel_params(16),
        cost_estimate=cost(2.2e9, 12e6),
        name="square_grad",
    )(ids, *d_ts, *flat_s, small, g_bq, *after)


def gather_rows(ids, parts, after=()):
    n = len(parts)
    rows, length, width = parts[0].shape
    arrays, specs = [], []
    for part in parts:
        if isinstance(part, tuple):
            array, at = part
            arrays.append(array)
            specs.append(
                pl.BlockSpec((1, rows, length, width), lambda i, ids, at=at: (at, 0, 0, 0))
            )
        else:
            arrays.append(part)
            specs.append(whole((rows, length, width)))

    def kernel(ids, *refs):
        out, token = refs[-2:]
        token[...] = jnp.zeros(token.shape, f32)
        for i in range(n):

            @pl.when(pl.program_id(0) == i)
            def _():
                part = refs[i]
                out[...] = (part[0] if len(part.shape) == 4 else part[...]).astype(f32)

    return pl.pallas_call(
        kernel,
        grid_spec=pltpu.PrefetchScalarGridSpec(
            num_scalar_prefetch=1,
            grid=(n,),
            in_specs=specs + anywhere(after),
            out_specs=[
                pl.BlockSpec((rows, length, width), lambda i, ids: (ids[4] ^ i, 0, 0)),
                whole((8, 128)),
            ],
        ),
        out_shape=[out_hbm((n * rows, length, width), f32), jax.ShapeDtypeStruct((8, 128), f32)],
        compiler_params=kernel_params(10),
        cost_estimate=cost(0, 6 * n * rows * length * width),
        name="gather_rows",
    )(ids, *arrays, *after)


def exchange(value, axis, size, relative):
    pairs = [(i, i ^ relative) for i in range(size)]
    return lax.ppermute(value, axis, pairs)


def total_of(parts):
    acc = parts[0].astype(f32)
    for part in parts[1:]:
        acc = acc + part.astype(f32)
    return acc


def call(name, kernel, grid, ins, specs, outs, out_specs, after=(), scratch=()):
    def wrapped(*refs):
        kernel(*refs[: len(ins)], *refs[len(ins) + len(after) :])

    moved = sum(math.prod(shape) * 8 for shape, _ in outs)
    return pl.pallas_call(
        wrapped,
        grid=grid,
        in_specs=list(specs) + anywhere(after),
        out_specs=out_specs,
        out_shape=[jax.ShapeDtypeStruct(shape, dt) for shape, dt in outs],
        scratch_shapes=list(scratch),
        compiler_params=kernel_params(8),
        cost_estimate=cost(moved, moved),
        name=name,
    )(*ins, *after)


class Reduction:
    def __init__(self, places, n_dp, n_krow, cut):
        self.places, self.n_dp, self.n_krow, self.cut = places, n_dp, n_krow, cut

    def along(self, axis, value, relative):
        if axis == "x":
            return exchange(value, "krow", self.n_krow, 2 * relative)
        if axis == "y":
            return exchange(value, "dp", self.n_dp, relative)
        return exchange(value, "dp", self.n_dp, relative * self.places.y)

    def core(self, send):
        self.came = exchange(send, "krow", self.n_krow, 1)

    def first(self, keep, after=()):
        self.keep = keep
        _, _, nz, rows, cols = keep.shape
        cut = self.cut
        self.heights = (cut, rows - cut)

        def kernel(k, c, first, second):
            total = total_of([k[0], c[0]]).astype(bf16)
            first[...] = total[:, :, :cut]
            second[...] = total[:, :, cut:]

        spec = pl.BlockSpec((1, 2, 1, rows, cols), lambda z: (1, 0, z, 0, 0))
        res = call(
            "first_sum", kernel, (nz,), [keep, self.came], [spec] * 2,
            [((2, nz, h, cols), bf16) for h in self.heights],
            [pl.BlockSpec((2, 1, h, cols), lambda z: (0, z, 0, 0)) for h in self.heights],
            after,
        )
        self.one = [self.along(axis, r, 1) for axis, r in zip("xy", res)]
        return res

    def second(self, after=()):
        _, _, nz, rows, cols = self.keep.shape
        cut = self.cut

        def kernel(k, c, g, h, first, second):
            first[0] = total_of([k[0, 0, 0, :cut], c[0, 0, 0, :cut], g[0, 0]]).astype(bf16)
            second[0] = total_of([k[0, 0, 0, cut:], c[0, 0, 0, cut:], h[0, 0]]).astype(bf16)

        spec = pl.BlockSpec((1, 1, 1, rows, cols), lambda z: (0, 1, z, 0, 0))
        res = call(
            "second_sum", kernel, (nz,), [self.keep, self.came] + self.one,
            [spec] * 2
            + [pl.BlockSpec((1, 1, h, cols), lambda z: (1, z, 0, 0)) for h in self.heights],
            [((nz, h, cols), bf16) for h in self.heights],
            [pl.BlockSpec((1, h, cols), lambda z: (z, 0, 0)) for h in self.heights],
            after,
        )
        self.two = [self.along(axis, r, 1) for axis, r in zip("yx", res)]
        return res

    def third(self, after=()):
        _, _, nz, rows, cols = self.keep.shape
        cut = self.cut

        def kernel(k, c, g1, h1, g2, h2, odd, even):
            for z in range(nz):
                out = odd if z % 2 else even
                for part, one, two in ((slice(0, cut), g1, g2), (slice(cut, rows), h1, h2)):
                    value = total_of([k[0, 0, z, part], c[0, 0, z, part], one[0, z], two[z]])
                    out[z // 2, part, :] = value.astype(out.dtype)

        shape = (nz // 2, rows, cols)
        spec = pl.BlockSpec((1, 1, nz, rows, cols), lambda i: (0, 0, 0, 0, 0))
        odd, self.even = call(
            "third_sum", kernel, (1,), [self.keep, self.came] + self.one + self.two,
            [spec] * 2
            + [pl.BlockSpec((1, nz, h, cols), lambda i: (0, 0, 0, 0)) for h in self.heights]
            + [pl.BlockSpec((nz, h, cols), lambda i: (0, 0, 0)) for h in self.heights],
            [(shape, bf16), (shape, f32)], [whole(shape)] * 2, after,
        )
        self.three = self.along("z", odd, 1)
        return [odd]

    def fourth(self, after=()):
        _, rows, cols = self.even.shape

        def kernel(e, g, send, mine):
            send[...] = total_of([e[1], g[1]]).astype(bf16)
            mine[...] = total_of([e[0], g[0]])

        shape = (rows, cols)
        send, mine = call(
            "fourth_sum", kernel, (1,), [self.even, self.three], [whole(self.even.shape)] * 2,
            [(shape, bf16), (shape, f32)], [whole(shape)] * 2, after,
        )
        self.terms = [mine, self.along("z", send, 2)]
        return [send]


def finish_down(red, after=()):
    rows, cols = red.terms[0].shape
    n = len(red.terms)

    def kernel(*refs):
        refs[n][...] = total_of([r[...] for r in refs[:n]])

    return call(
        "finish_down", kernel, (1,), red.terms, [whole((rows, cols))] * n,
        [((rows, cols), f32)], [whole((rows, cols))], after,
    )


def finish_up(red, cuts, krows, half, width, ff, after=()):
    rows, cols = red.terms[0].shape
    n = len(red.terms)
    cut_up, cut_out = cuts
    rest = krows - cut_up
    sizes = (width,) * 6 + (ff,)

    def kernel(*refs):
        up, out = refs[n], refs[n + 1]
        total = total_of([r[...] for r in refs[:n]])
        low = cut_up + cut_out
        up[:cut_up] = total[:cut_up]
        up[cut_up:] = total[low : low + rest]
        out[:cut_out] = total[cut_up:low]
        out[cut_out:] = total[low + rest : krows + half]
        at = krows + half
        for piece, size in zip(refs[n + 2 :], sizes):
            for i in range(size // cols):
                piece[i * cols : (i + 1) * cols] = total[at, :]
                at += 1

    shapes = [(krows, cols), (half, cols)] + [(size,) for size in sizes]
    return call(
        "finish_up", kernel, (1,), red.terms, [whole((rows, cols))] * n,
        [(shape, f32) for shape in shapes], [whole(shape) for shape in shapes], after,
    )


def finish_square(red, ids, out_rows, cut, half, count, s_cols, after=()):
    rows, cols = red.terms[0].shape
    n = len(red.terms)
    extra = rows - count * half
    mine_cols = cols // 2
    width = cols * red.places.x
    height = (count + 1) * half + 2 * extra

    def kernel(ids, out_ref, *refs):
        terms, (mine, other, g_bq, temp) = refs[:n], refs[n:]
        total = total_of([r[...] for r in terms])
        rest = half - cut
        temp[:half] = out_ref[...]
        for m in range(count):
            at = half * (m + 1)
            temp[at : at + cut] = total[m * cut : (m + 1) * cut]
            low = count * cut + m * rest
            temp[at + cut : at + half] = total[low : low + rest]
        core = ids[0]
        square = (count + 1) * half
        lo, hi = temp[:square, :mine_cols], temp[:square, mine_cols:]
        mine[:square, :] = jnp.where(core == 0, lo, hi)
        other[:square, :] = jnp.where(core == 0, hi, lo).astype(bf16)
        h = s_cols // 2
        mine[square:, :] = jnp.zeros((2 * extra, mine_cols), f32)
        other[square:, :] = jnp.zeros((2 * extra, mine_cols), bf16)
        for part in range(2):
            tail = total[count * half :, part * s_cols : (part + 1) * s_cols]
            at = square + part * extra
            lo, hi = tail[:, :h], tail[:, h:]
            mine[at : at + extra, :h] = jnp.where(core == 0, lo, hi)
            other[at : at + extra, :h] = jnp.where(core == 0, hi, lo).astype(bf16)
        for i in range(width // 128):
            g_bq[i * 128 : (i + 1) * 128] = total[count * half + i, 2 * s_cols : 2 * s_cols + 128]

    return call(
        "finish_square", kernel, (1,), [ids, out_rows] + red.terms,
        [pl.BlockSpec(memory_space=pltpu.SMEM), whole(out_rows.shape)]
        + [whole((rows, cols))] * n,
        [((height, mine_cols), f32), ((height, mine_cols), bf16), ((width,), f32)],
        [whole((height, mine_cols))] * 2 + [whole((width,))],
        after,
        [pltpu.VMEM(((count + 1) * half, cols), f32)],
    )


def finish_columns(ids, mine, there, half, count, extra, s_half_cols):
    mine_cols = mine.shape[1]
    square = count * half

    def kernel(ids, mine, there, *refs):
        outs, temp = refs[:-1], refs[-1]
        core = ids[0]

        def merge(at, height, cols, out):
            a, b = mine[at : at + height, :cols], there[at : at + height, :cols].astype(f32)
            low, high = jnp.where(core == 0, a, b), jnp.where(core == 0, b, a)
            out[...] = jnp.concatenate([low, high], axis=0).T

        for m in range(count):
            merge(m * half, half, mine_cols, outs[m])
        merge(square, 2 * extra, s_half_cols, outs[count])

    shapes = [(mine_cols, 2 * half)] * count + [(s_half_cols, 4 * extra)]
    return call(
        "finish_columns", kernel, (1,), [ids, mine, there],
        [pl.BlockSpec(memory_space=pltpu.SMEM), whole(mine.shape), whole(there.shape)],
        [(shape, f32) for shape in shapes], [whole(shape) for shape in shapes],
        (), [pltpu.VMEM((8, 128), f32)],
    )


def local(
    sizes,
    tokens,
    segment_ids,
    segment_live,
    w_query,
    b_query,
    w_key,
    w_value,
    w_out,
    b_out,
    attn_gain,
    attn_shift,
    w_up,
    b_up,
    w_down,
    b_down,
    ffn_gain,
    ffn_shift,
    compress,
    cotangent,
):
    n_dp, n_krow = sizes
    all_rows, length, width = tokens.shape
    rows = all_rows // n_krow
    seq = n_krow * length
    keys = compress.shape[0]
    ff = w_up.shape[1]
    krow, dp = lax.axis_index("krow"), lax.axis_index("dp")
    places = Places(n_dp, n_krow)
    ids = jnp.stack([krow % 2, dp % places.y, dp // places.y, krow // 2, krow]).astype(jnp.int32)
    fast = (
        width % (2 * places.x * 32) == 0
        and ff % (n_dp * 128) == 0
        and ff % (n_krow * 128) == 0
        and width % (2 * n_dp * 16) == 0
        and seq % (2 * n_dp * 32) == 0
        and width % (places.x * 128) == 0
        and keys % (places.x * 128) == 0
        and length % (seq // n_dp) == 0
        and ff // n_dp == width // places.x
        and 2 * (keys // places.x) + 128 <= width // places.x
        and width <= 128 * (seq // (4 * n_dp))
        and places.x == 2
        and places.y == 2
        and places.z == 4
        and rows > 1
    )

    def spread(value):
        parts = []
        for r in range(n_krow):
            part = lax.dynamic_slice_in_dim(value, (krow ^ r) * rows, rows, 0)
            parts.append(exchange(part, "krow", n_krow, r) if r else part)
        return parts

    def back(parts):
        return [exchange(part, "krow", n_krow, r) if r else part for r, part in enumerate(parts)]

    def second_hop(parts, came, *after):
        late = lax.optimization_barrier((came, after))[0]
        core = exchange(parts[1], "krow", n_krow, 1)
        return [parts[0], core, (came, 0), exchange(late[1], "krow", n_krow, 1)]

    def row(value):
        return value.astype(f32).reshape(1, -1)

    toks = spread(tokens)
    cot_source = lax.optimization_barrier((cotangent, toks[-1]))[0]
    cots = spread(cot_source)

    my_ids = lax.dynamic_slice_in_dim(segment_ids, krow * rows, rows, 0)
    my_live = lax.dynamic_slice_in_dim(segment_live, krow * rows, rows, 0)
    labels = jnp.arange(segment_live.shape[1], dtype=jnp.int32)
    live = jnp.sum(
        jnp.where(my_ids[:, :, None] == labels, my_live[:, None, :], 0).astype(f32), axis=-1
    )

    def relative(value, axis):
        return jnp.concatenate(
            [
                lax.dynamic_slice_in_dim(value, (krow ^ r) * length, length, axis)
                for r in range(n_krow)
            ],
            axis=axis,
        )

    live = relative(live, 1)
    comp = relative(compress, 1)
    live_row = live[:, None, :]
    live_col = jnp.broadcast_to(live[:, :, None], (rows, seq, 128))
    comp_t = comp.T
    gain, shift = row(attn_gain), row(attn_shift)

    q_t, pk, k, v, lse, att, xhat, rstd = attn_fwd(
        toks, live_row, comp, w_query, row(b_query), w_key, w_value, w_out, row(b_out)
    )
    n_parts = 3 if fast else n_krow
    res = ffn_fwd(
        fast, cots, xhat, gain, shift, w_up, row(b_up), w_down, row(b_down), row(ffn_gain), row(ffn_shift)
    )
    outs, (act, gp, dh2, d_t, sums_two) = res[:n_parts], res[n_parts:]
    out_came = exchange(outs[2], "krow", n_krow, 2) if fast else None
    ahead = []
    if fast:
        cut_down = 32
        cuts_up = (width // n_krow // 2, 32)
        cut_square = 16
        half = width // (2 * n_dp)
        down = Reduction(places, n_dp, n_krow, cut_down)
        up = Reduction(places, n_dp, n_krow, sum(cuts_up))
        square = Reduction(places, n_dp, n_krow, 3 * cut_square)
        send = down_grad(places, 1, cut_down, ids, d_t, act)
        down.core(send)
        keep = down_grad(places, 0, cut_down, ids, d_t, act, after=[send])
        ahead = list(down.first(keep))

    dup, dh1, da_t, nl_t, br_t, sums_one = ffn_bwd(
        gp, dh2, xhat, rstd, gain, shift, w_up, w_down, w_out, after=ahead
    )

    if fast:
        ahead = down.second([sums_one, out_came])
        out_parts = second_hop(outs, out_came, *ahead)
        parts = nl_t, dup, br_t, att, sums_one, sums_two
        send = up_grad(places, 1, cuts_up, ids, *parts, after=ahead)
        up.core(send)
        keep = up_grad(places, 0, cuts_up, ids, *parts, after=[send])
        ahead = up.first(keep)
        ahead = down.third(ahead)

    res = attn_bwd(
        fast, toks, q_t, k, v, lse, da_t, comp_t, live_col, w_query, w_key, w_value, dh1, after=ahead
    )
    grad_parts, bwd = res[:n_parts], res[n_parts:]

    if fast:
        sources = [[(t, r) for r in range(rows) for t in toks], [(in_hbm(pk)[0], r) for r in range(rows)]]
        ahead = up.second([bwd[3], down.three])
        ahead = down.fourth(ahead)
        parts = bwd[:3], sources, bwd[4], length, bwd[3]
        send = square_grad(places, 1, cut_square, ids, *parts, after=ahead)
        square.core(send)
        keep = square_grad(places, 0, cut_square, ids, *parts, after=[send])
        ahead = square.first(keep, [down.terms[1]])
        ahead = up.third(ahead)
        grad_parts = lax.optimization_barrier((grad_parts, ahead))[0]
        grad_came = exchange(grad_parts[2], "krow", n_krow, 2)
        output, token = gather_rows(ids, out_parts, after=ahead)
        ahead = up.fourth([token])
        ahead = square.second(ahead)
        grad_parts = second_hop(grad_parts, grad_came, *ahead)
        g_up, out_rows, *pieces = finish_up(
            up, cuts_up, width // n_krow, half, width, ff, after=ahead
        )
        ahead = square.third([out_rows])
        (g_down,) = finish_down(down, after=ahead)
        grad_tokens, token = gather_rows(ids, grad_parts, after=ahead)
        square.fourth([token])
        g_down = g_down.T
        s_cols = keys // places.x
        mine, other, g_bq = finish_square(square, ids, out_rows, cut_square, half, 3, s_cols)
        pieces = [g_bq] + pieces
        there = exchange(other, "krow", n_krow, 1)
        g_out, g_q, g_k, g_v, g_comp = finish_columns(
            ids, mine, there, half, 4, seq // (4 * n_dp), s_cols // 2
        )
    else:
        grad_parts = back(grad_parts)
        g_bu = jnp.sum(dup.astype(f32), axis=(0, 1)).reshape(-1, width)
        g_bq = jnp.sum(bwd[3], axis=0)
        vectors = jnp.concatenate([g_bq, sums_one[:3], sums_two[:3], g_bu], axis=0)
        output, _ = gather_rows(ids, back(outs))
        grad_tokens, _ = gather_rows(ids, grad_parts)
        vectors = lax.psum(vectors.reshape(-1), ("dp", "krow"))
        pieces = []
        start = 0
        for size in (width,) * 7 + (ff,):
            pieces.append(vectors[start : start + size])
            start += size

        def scattered(value):
            value = value.astype(bf16)
            part = lax.psum_scatter(value, "krow", scatter_dimension=0, tiled=True)
            return lax.psum_scatter(part, "dp", scatter_dimension=1, tiled=True).astype(f32)

        def product(a, b):
            return lax.dot_general(a, b, (((1,), (0,)), ((), ())), preferred_element_type=f32)

        token_rows = jnp.concatenate(toks, axis=1)
        d_q, d_k, d_v = [jnp.swapaxes(d, 0, 1).reshape(width, -1) for d in bwd[:3]]
        pk = pk.reshape(-1, width)
        g_q = scattered(product(d_q, token_rows.reshape(-1, width)).T)
        g_k = scattered(product(d_k, pk).T)
        g_v = scattered(product(d_v, pk).T)
        g_out = scattered(product(br_t, att.reshape(-1, width)).T)
        g_up = scattered(product(nl_t, dup.reshape(-1, ff)))
        g_down = scattered(product(d_t, act.reshape(-1, ff)).T)
        blocks = jnp.sum(bwd[4].astype(f32), axis=0).reshape(n_krow, length, keys)
        blocks = jnp.concatenate(
            [lax.dynamic_slice_in_dim(blocks, krow ^ r, 1, 0) for r in range(n_krow)]
        )
        g_comp = scattered(blocks.reshape(seq, keys).T)

    g_bq, g_gain, g_shift, g_bo, g_fgain, g_fshift, g_bd, g_bu = pieces
    return (
        output,
        grad_tokens,
        g_q,
        g_bq,
        g_k,
        g_v,
        g_out,
        g_bo,
        g_gain,
        g_shift,
        g_up,
        g_bu,
        g_down,
        g_bd,
        g_fgain,
        g_fshift,
        g_comp,
    )


def solution(mesh):
    rows = P("dp", "krow", None)
    per_row = P("dp", None)
    block = P("krow", "dp")
    in_specs = (rows, per_row, per_row) + (P(),) * 15 + (rows,)
    out_specs = (
        (rows, rows, block, P(), block, block, block)
        + (P(),) * 3
        + (block, P(), block)
        + (P(),) * 3
        + (block,)
    )
    sizes = (mesh.shape["dp"], mesh.shape["krow"])
    return jax.shard_map(
        functools.partial(local, sizes),
        mesh=mesh,
        in_specs=in_specs,
        out_specs=out_specs,
        check_vma=False,
    )
```

```python
import functools
import math

import jax
import jax.numpy as jnp
from jax import lax
from jax.experimental import pallas as pl
from jax.experimental.pallas import tpu as pltpu
from jax.sharding import PartitionSpec as P

H = 12
HD = 64
f32 = jnp.float32
bf16 = jnp.bfloat16


def nn(a, b):
    return lax.dot_general(a, b, (((1,), (0,)), ((), ())), preferred_element_type=f32)


def nt(a, b):
    return lax.dot_general(a, b, (((1,), (1,)), ((), ())), preferred_element_type=f32)


def whole(shape):
    rank = len(shape)
    return pl.BlockSpec(shape, lambda *_: (0,) * rank, pipeline_mode=pl.Buffered(1))


def fetch_strips(src, dst, sems, ids, other, half, dp):
    copies = []
    for d in range(dp):
        first = pl.multiple_of(2 * half * d + half * (ids[0] ^ other), 16)
        copies.append(
            pltpu.make_async_copy(
                src.at[pl.ds(first, half), :], dst.at[d * half : (d + 1) * half, :], sems.at[d]
            )
        )
        copies[-1].start()
    return copies


def resident():
    return pl.BlockSpec(memory_space=pltpu.VMEM)


def out_hbm(shape, dtype):
    return pltpu.HBM(shape, dtype)


def in_hbm(*values):
    return [pltpu.with_memory_space_constraint(v, pltpu.HBM) for v in values]


def fetch(sources, places, sems):
    copies = [
        pltpu.make_async_copy(src, dst, sems.at[i])
        for i, (src, dst) in enumerate(zip(sources, places))
    ]

    @pl.when(pl.program_id(0) == 0)
    def _():
        for copy in copies:
            copy.start()

    def wait(*which):
        @pl.when(pl.program_id(0) == 0)
        def _():
            for i in which:
                copies[i].wait()

    return wait


def anywhere(values):
    return [pl.BlockSpec(memory_space=pl.ANY)] * len(values)


def row_block(*shape):
    rank = len(shape)
    return pl.BlockSpec((1,) + shape, lambda r, *_: (r,) + (0,) * rank)


def parts_of(n, rows, length, width, paired):
    single = (row_block(length, width), (rows, length, width))
    if not paired:
        return [single[0]] * n, [single[1]] * n
    both = (pl.BlockSpec((2, 1, length, width), lambda r, *_: (0, r, 0, 0)), (2, rows, length, width))
    return [single[0]] * 2 + [both[0]], [single[1]] * 2 + [both[1]]


def put_part(outs, n, i, value):
    if len(outs) == n or i < 2:
        outs[i][0] = value
    else:
        outs[2][i - 2, 0] = value


def kernel_params(mebibytes):
    return pltpu.CompilerParams(dimension_semantics=("arbitrary",), vmem_limit_bytes=mebibytes * 1024 * 1024)


def cost(flops, moved, trans=0):
    return pl.CostEstimate(flops=int(flops), bytes_accessed=int(moved), transcendentals=int(trans))


def add_to(ref, value, first):
    @pl.when(first)
    def _():
        ref[...] = value

    @pl.when(jnp.logical_not(first))
    def _():
        ref[...] += value


def col_sum(value):
    return jnp.sum(value, axis=0, keepdims=True)


def gelu_parts(u):
    phi = 0.5 + 0.5 * lax.erf(u * (1.0 / math.sqrt(2.0)))
    density = jnp.exp(-0.5 * u * u) * (1.0 / math.sqrt(2.0 * math.pi))
    return u * phi, phi + u * density


def attn_fwd_kernel(n, *refs):
    toks = refs[:n]
    live, comp, wq_hbm, bq, wk_hbm, wv_hbm, wo_hbm, bo = refs[n : n + 8]
    q_t, pk, k, v, lse, att, xhat, rstd = refs[n + 8 : n + 16]
    tok, att_t, wq, wk, wv, wo, sems = refs[n + 16 :]
    wait = fetch((wq_hbm, wk_hbm, wv_hbm, wo_hbm), (wq, wk, wv, wo), sems)
    length = toks[0].shape[1]
    for i in range(n):
        tok[i * length : (i + 1) * length, :] = toks[i][0]
    masked = (comp[...].astype(f32) * live[0]).astype(bf16)
    x = tok[...]
    pk[0] = nn(masked, x).astype(bf16)
    wait(0, 1, 2)
    for c in range(3):
        cols = slice(256 * c, 256 * c + 256)
        q = (nn(x, wq[:, cols]) + bq[:, cols]).astype(bf16) * jnp.asarray(1.0 / math.sqrt(HD), bf16)
        q_t[0, cols, :] = q.T
        k[0, :, cols] = nn(pk[0], wk[:, cols]).astype(bf16)
        v[0, :, cols] = nn(pk[0], wv[:, cols]).astype(bf16)
    lane = lax.broadcasted_iota(jnp.int32, (1, 2 * HD), 1)
    for pair in range(H // 2):
        cols = slice(2 * HD * pair, 2 * HD * (pair + 1))
        k_pair = k[0, :, cols]
        v_t = v[0, :, cols].T
        for half in range(2):
            h = 2 * pair + half
            mine = jnp.where((lane // HD) == half, k_pair, jnp.zeros_like(k_pair))
            s = nn(mine, q_t[0, cols, :])
            top = jnp.max(s, axis=0, keepdims=True)
            e = jnp.exp(s - top)
            total = jnp.sum(e, axis=0, keepdims=True)
            w = (e * (1.0 / total)).astype(bf16)
            lse[0, h : h + 1, :] = top + jnp.log(total)
            att_t[h * HD : (h + 1) * HD, :] = nn(v_t[half * HD : (half + 1) * HD, :], w).astype(bf16)
    for c in range(3):
        cols = slice(256 * c, 256 * c + 256)
        att[0, :, cols] = att_t[cols, :].T
    wait(3)
    hidden = x.astype(f32) + nn(att[0], wo[...]) + bo[...]
    average = jnp.mean(hidden, axis=-1, keepdims=True)
    centred = hidden - average
    spread = jnp.mean(centred * centred, axis=-1, keepdims=True)
    r = lax.rsqrt(spread + 1e-05)
    xhat[0] = centred * r
    rstd[0] = jnp.broadcast_to(r, rstd.shape[1:])


def attn_fwd(toks, live, comp, wq, bq, wk, wv, wo, bo):
    rows, length, width = toks[0].shape
    n = len(toks)
    seq = n * length
    keys = comp.shape[0]
    in_specs = [row_block(length, width)] * n + [
        row_block(1, seq),
        whole((keys, seq)),
        pl.BlockSpec(memory_space=pl.ANY),
        whole((1, width)),
        pl.BlockSpec(memory_space=pl.ANY),
        pl.BlockSpec(memory_space=pl.ANY),
        pl.BlockSpec(memory_space=pl.ANY),
        whole((1, width)),
    ]
    outs = [
        ((width, seq), bf16),
        ((keys, width), bf16),
        ((keys, width), bf16),
        ((keys, width), bf16),
        ((16, seq), f32),
        ((seq, width), bf16),
        ((seq, width), f32),
        ((seq, 128), f32),
    ]
    return pl.pallas_call(
        functools.partial(attn_fwd_kernel, n),
        grid=(rows,),
        in_specs=in_specs,
        out_specs=[row_block(*shape) for shape, _ in outs],
        out_shape=[out_hbm((rows,) + shape, dt) for shape, dt in outs],
        scratch_shapes=[pltpu.VMEM((seq, width), bf16), pltpu.VMEM((width, seq), bf16)]
        + [pltpu.VMEM((width, width), bf16)] * 4
        + [pltpu.SemaphoreType.DMA((4,))],
        compiler_params=kernel_params(30),
        cost_estimate=cost(rows * 5e9, 12e6, rows * H * seq * keys),
        name="attn_fwd",
    )(*toks, live, comp, *in_hbm(wq), bq, *in_hbm(wk, wv, wo), bo)


def ffn_fwd_kernel(n, n_out, *refs):
    cots = refs[:n]
    xhat, gain, shift, wu, bu, wd, bd, fgain, fshift = refs[n : n + 9]
    refs = refs[n + 9 :]
    outs = refs[:n_out]
    act, gp, dh2, d_t, sums = refs[n_out:]
    r = pl.program_id(0)
    first = r == 0
    length = cots[0].shape[1]
    ff = wu.shape[1]
    chunk = 512
    count = ff // chunk
    normed = xhat[0] * gain[...] + shift[...]
    low = normed.astype(bf16)

    def up(c):
        cols = slice(c * chunk, (c + 1) * chunk)
        return nn(low, wu[:, cols]) + bu[:, cols]

    for c in range(count):
        cols = slice(c * chunk, (c + 1) * chunk)
        a, g = gelu_parts(up(c))
        act[r, :, cols] = a.astype(bf16)
        gp[0, :, cols] = g.astype(bf16)
    total = normed + bd[...] + nn(act[r], wd[...])
    average = jnp.mean(total, axis=-1, keepdims=True)
    centred = total - average
    spread = jnp.mean(centred * centred, axis=-1, keepdims=True)
    rs = lax.rsqrt(spread + 1e-05)
    hat = centred * rs
    result = (hat * fgain[...] + fshift[...]).astype(bf16)
    for i in range(n):
        put_part(outs, n, i, result[i * length : (i + 1) * length, :])
    cot = jnp.concatenate([c[0] for c in cots], axis=0).astype(f32)
    dhat = cot * fgain[...]
    d = rs * (
        dhat
        - jnp.mean(dhat, axis=-1, keepdims=True)
        - hat * jnp.mean(dhat * hat, axis=-1, keepdims=True)
    )
    dh2[0] = d
    d_low = d.astype(bf16)
    seq = d_low.shape[0]
    d_t[:, pl.ds(pl.multiple_of(r * seq, seq), seq)] = d_low.T
    add_to(
        sums,
        jnp.concatenate(
            [col_sum(cot * hat), col_sum(cot), col_sum(d_low.astype(f32)), jnp.zeros((5, d.shape[1]), f32)],
            axis=0,
        ),
        first,
    )


def ffn_fwd(paired, cots, xhat, gain, shift, wu, bu, wd, bd, fgain, fshift):
    rows, length, width = cots[0].shape
    n = len(cots)
    seq = n * length
    ff = wu.shape[1]
    vec = whole((1, width))
    in_specs = [row_block(length, width)] * n + [
        row_block(seq, width),
        vec,
        vec,
        resident(),
        whole((1, ff)),
        resident(),
        vec,
        vec,
        vec,
    ]
    specs, shapes = parts_of(n, rows, length, width, paired)
    more = [((seq, ff), bf16), ((seq, width), f32)]
    return pl.pallas_call(
        functools.partial(ffn_fwd_kernel, n, len(shapes)),
        grid=(rows,),
        in_specs=in_specs,
        out_specs=specs
        + [resident()]
        + [row_block(*shape) for shape, _ in more]
        + [resident()]
        + [whole((8, width))],
        out_shape=[jax.ShapeDtypeStruct(shape, bf16) for shape in shapes]
        + [pltpu.VMEM((rows, seq, ff), bf16)]
        + [jax.ShapeDtypeStruct((rows,) + shape, dt) for shape, dt in more]
        + [jax.ShapeDtypeStruct((width, rows * seq), bf16)]
        + [jax.ShapeDtypeStruct((8, width), f32)],
        compiler_params=kernel_params(26),
        cost_estimate=cost(rows * seq * width * ff * 4, 34e6, rows * seq * ff * 2),
        name="ffn_fwd",
    )(*cots, *in_hbm(xhat), gain, shift, wu, bu, wd, bd, fgain, fshift)


def ffn_bwd_kernel(*refs):
    gp, dh2, xhat, rstd, gain, shift, wu, wd, wo = refs[:9]
    dup, dh1, da_t, nl_t, br_t, sums = refs[-6:]
    r = pl.program_id(0)
    first = r == 0
    ff = wu.shape[1]
    chunk = 512
    count = ff // chunk
    d_low = dh2[0].astype(bf16)

    def back(c):
        return nt(d_low, wd[c * chunk : (c + 1) * chunk, :])

    for c in range(count):
        cols = slice(c * chunk, (c + 1) * chunk)
        dup[r, :, cols] = (gp[0, :, cols].astype(f32) * back(c)).astype(bf16)
    tile = min(256, dh2.shape[1])
    for i in range(dh2.shape[1] // tile):
        part = slice(i * tile, (i + 1) * tile)
        for j in range(dh2.shape[2] // 256):
            cols = slice(j * 256, (j + 1) * 256)
            dh1[0, part, cols] = dh2[0, part, cols] + nt(dup[r, part, :], wu[cols, :])
    dn = dh1[0]
    hat = xhat[0]
    dhat = dn * gain[...]
    d = rstd[0, :, 0:1] * (
        dhat
        - jnp.mean(dhat, axis=-1, keepdims=True)
        - hat * jnp.mean(dhat * hat, axis=-1, keepdims=True)
    )
    dh1[0] = d
    branch = d.astype(bf16)
    add_to(
        sums,
        jnp.concatenate(
            [col_sum(dn * hat), col_sum(dn), col_sum(branch.astype(f32)), jnp.zeros((5, d.shape[1]), f32)],
            axis=0,
        ),
        first,
    )
    da_t[0] = nt(wo[...], branch).astype(bf16)
    br_t[...] = branch.T
    nl_t[...] = (hat * gain[...] + shift[...]).astype(bf16).T


def ffn_bwd(gp, dh2, xhat, rstd, gain, shift, wu, wd, wo, after=()):
    rows, seq, ff = gp.shape
    width = wu.shape[0]
    vec = whole((1, width))
    in_specs = [
        row_block(seq, ff),
        row_block(seq, width),
        row_block(seq, width),
        row_block(seq, 128),
        vec,
        vec,
        resident(),
        resident(),
        resident(),
    ] + anywhere(after)
    outs = [((seq, width), f32), ((width, seq), bf16)]
    turned = pl.BlockSpec((width, seq), lambda r: (0, r))
    return pl.pallas_call(
        ffn_bwd_kernel,
        grid=(rows,),
        in_specs=in_specs,
        out_specs=[resident()]
        + [row_block(*shape) for shape, _ in outs]
        + [turned] * 2
        + [whole((8, width))],
        out_shape=[pltpu.VMEM((rows, seq, ff), bf16)]
        + [jax.ShapeDtypeStruct((rows,) + shape, dt) for shape, dt in outs]
        + [jax.ShapeDtypeStruct((width, rows * seq), bf16)] * 2
        + [jax.ShapeDtypeStruct((8, width), f32)],
        compiler_params=kernel_params(26),
        cost_estimate=cost(rows * seq * width * ff * 4.5, 34e6),
        name="ffn_bwd",
    )(gp, dh2, xhat, rstd, gain, shift, wu, wd, wo, *after)


def attn_bwd_kernel(n, n_out, *refs):
    toks = refs[:n]
    q_t, k, v, lse, da_t, comp_t, live_col, wq, wk, wv, dh1 = refs[n : n + 11]
    refs = refs[-(n_out + 6) :]
    outs = refs[:n_out]
    dq_t, dk_t, dv_t, g_bq, small, tok = refs[n_out:]
    length = toks[0].shape[1]
    for i in range(n):
        tok[i * length : (i + 1) * length, :] = toks[i][0]
    lane = lax.broadcasted_iota(jnp.int32, (1, 2 * HD), 1)
    scale = jnp.asarray(1.0 / math.sqrt(HD), f32)
    for pair in range(H // 2):
        cols = slice(2 * HD * pair, 2 * HD * (pair + 1))
        k_pair = k[0, :, cols]
        v_pair = v[0, :, cols]
        k_t = k_pair.T
        for half in range(2):
            h = 2 * pair + half
            head = slice(h * HD, (h + 1) * HD)
            mine = (lane // HD) == half
            s = nn(jnp.where(mine, k_pair, jnp.zeros_like(k_pair)), q_t[0, cols, :])
            w = jnp.exp(s - lse[0, h : h + 1, :])
            dw = nn(jnp.where(mine, v_pair, jnp.zeros_like(v_pair)), da_t[0, cols, :])
            dot = jnp.sum(w * dw, axis=0, keepdims=True)
            ds = (w * (dw - dot)).astype(bf16)
            dv_t[0, head, :] = nt(da_t[0, head, :], w.astype(bf16)).astype(bf16)
            dk_t[0, head, :] = nt(q_t[0, head, :], ds).astype(bf16)
            dq_t[0, head, :] = (nn(k_t[half * HD : (half + 1) * HD, :], ds) * scale).astype(bf16)
    dp_t = (nn(wk[...], dk_t[0]) + nn(wv[...], dv_t[0])).astype(bf16)
    small[0] = (nn(tok[...], dp_t) * live_col[0, :, 0:1]).astype(bf16)
    masked = (comp_t[...].astype(f32) * live_col[0, :, 0:1]).astype(bf16)
    dq = dq_t[0].T
    g_bq[0] = col_sum(dq.astype(f32))
    grad = dh1[0] + nt(dq, wq[...]) + nt(masked, dp_t)
    for i in range(n):
        put_part(outs, n, i, grad[i * length : (i + 1) * length, :].astype(bf16))


def attn_bwd(paired, toks, q_t, k, v, lse, da_t, comp_t, live_col, wq, wk, wv, dh1, after=()):
    rows, length, width = toks[0].shape
    n = len(toks)
    seq = n * length
    keys = comp_t.shape[1]
    in_specs = (
        [row_block(length, width)] * n
        + [
            row_block(width, seq),
            row_block(keys, width),
            row_block(keys, width),
            row_block(16, seq),
            row_block(width, seq),
            whole((seq, keys)),
            row_block(seq, 128),
            whole((width, width)),
            whole((width, width)),
            whole((width, width)),
            row_block(seq, width),
        ]
        + anywhere(after)
    )
    specs, shapes = parts_of(n, rows, length, width, paired)
    outs = [
        ((width, seq), bf16),
        ((width, keys), bf16),
        ((width, keys), bf16),
        ((1, width), f32),
        ((seq, keys), bf16),
    ]
    return pl.pallas_call(
        functools.partial(attn_bwd_kernel, n, len(shapes)),
        grid=(rows,),
        in_specs=in_specs,
        out_specs=specs + [row_block(*shape) for shape, _ in outs],
        out_shape=[jax.ShapeDtypeStruct(shape, bf16) for shape in shapes]
        + [jax.ShapeDtypeStruct((rows,) + shape, dt) for shape, dt in outs],
        scratch_shapes=[pltpu.VMEM((seq, width), bf16)],
        compiler_params=kernel_params(28),
        cost_estimate=cost(rows * 8e9, 24e6, rows * H * seq * keys),
        name="attn_bwd",
    )(*toks, q_t, k, v, lse, da_t, comp_t, live_col, wq, wk, wv, dh1, *after)


class Places:
    def __init__(self, n_dp, n_krow):
        self.x = n_krow // 2
        self.y = n_krow // 2
        self.z = n_dp // self.y
        self.dp = n_dp

    def shape(self, rows, cols):
        return (2, 2, self.z, rows, cols)

    def put(self, out, x, y, z, block, cut, low, high):
        out[x, y, z, low : low + cut] = block[:cut]
        out[y, x, z, high : high + block.shape[0] - cut] = block[cut:]


def down_grad(places, other, cut, ids, d_t, act, after=()):
    width, tokens = d_t.shape
    rows, seq, ff = act.shape
    cols = ff // (2 * places.x)
    height = width // places.dp
    shape = places.shape(height, cols)

    def kernel(ids, d_ref, act_ref, *refs):
        xr = pl.program_id(0)
        start = pl.multiple_of((2 * (ids[3] ^ xr) + (ids[0] ^ other)) * cols, 128)
        block = act_ref[:, :, pl.ds(start, cols)].reshape(rows * seq, cols)
        res = nn(d_ref[...], block).astype(bf16)
        for z in range(places.z):
            for y in range(places.y):
                d = z * places.y + y
                block = res[d * height : (d + 1) * height, :]
                places.put(refs[-1], xr, ids[1] ^ y, ids[2] ^ z, block, cut, 0, cut)

    return pl.pallas_call(
        kernel,
        grid_spec=pltpu.PrefetchScalarGridSpec(
            num_scalar_prefetch=1,
            grid=(places.x,),
            in_specs=[
                resident(),
                resident(),
            ]
            + anywhere(after),
            out_specs=whole(shape),
        ),
        out_shape=jax.ShapeDtypeStruct(shape, bf16),
        compiler_params=kernel_params(16),
        cost_estimate=cost(width * tokens * ff, 8e6),
        name="down_grad",
    )(ids, d_t, act, *after)


def up_grad(places, other, cuts, ids, nl_t, dup, br_t, att, one, two, after=()):
    width, tokens = nl_t.shape
    rows, seq, ff = dup.shape
    krows = width // (2 * places.x)
    cols = ff // places.dp
    half = width // (2 * places.dp)
    step = cols * places.y
    cut_up, cut_out = cuts
    shape = places.shape(krows + half + 32, cols)
    cut = cut_up + cut_out

    def kernel(ids, nl_ref, dup_ref, br_ref, att_ref, one_ref, two_ref, *refs):
        out = refs[-9]
        lhs, temp, att_vm, nl_sems, br_sems, att_sem, g_bu, vecs = refs[-8:]
        zr = pl.program_id(0)

        @pl.when(zr == 0)
        def _():
            copies = []
            for x in range(places.x):
                first = pl.multiple_of((2 * x + (ids[0] ^ other)) * krows, 16)
                copies.append(
                    pltpu.make_async_copy(
                        nl_ref.at[pl.ds(first, krows), :],
                        lhs.at[x * krows : (x + 1) * krows, :],
                        nl_sems.at[x],
                    )
                )
                copies[-1].start()
            fetch_strips(br_ref, temp, br_sems, ids, other, half, places.dp)
            pltpu.make_async_copy(att_ref, att_vm, att_sem).start()
            lhs[places.x * krows :, :] = jnp.ones((16, tokens), bf16)
            for copy in copies:
                copy.wait()

        start = pl.multiple_of((ids[2] ^ zr) * step, 128)
        res = nn(lhs[...], dup_ref[:, :, pl.ds(start, step)].reshape(tokens, step))
        g_bu[:, pl.ds(start, step)] = res[places.x * krows : places.x * krows + 8]
        res = res.astype(bf16)
        for x in range(places.x):
            for y in range(places.y):
                block = res[x * krows : (x + 1) * krows, y * cols : (y + 1) * cols]
                places.put(out, ids[3] ^ x, ids[1] ^ y, zr, block, cut_up, 0, cut)

        @pl.when(zr == places.z - 1)
        def _():
            vecs[...] = jnp.zeros(vecs.shape, f32)
            at = 0
            for ref, count in ((one_ref, 3), (two_ref, 3), (g_bu, 1)):
                for i in range(count):
                    for j in range(ref.shape[1] // cols):
                        vecs[at : at + 1, :] = ref[i : i + 1, j * cols : (j + 1) * cols]
                        at += 1
            low = vecs[...].astype(bf16)
            for i in range(2):
                for j in range(2):
                    for z in range(places.z):
                        out[i, j, z, krows + half :] = low
            pltpu.make_async_copy(att_ref, att_vm, att_sem).wait()
            for d in range(places.dp):
                pltpu.make_async_copy(
                    br_ref.at[d * half : (d + 1) * half, :],
                    temp.at[d * half : (d + 1) * half, :],
                    br_sems.at[d],
                ).wait()
            res = nn(temp[...], att_vm[...].reshape(tokens, width)).astype(bf16)
            for z in range(places.z):
                for y in range(places.y):
                    d = z * places.y + y
                    for x in range(places.x):
                        block = res[d * half : (d + 1) * half, x * cols : (x + 1) * cols]
                        places.put(
                            out, ids[3] ^ x, ids[1] ^ y, ids[2] ^ z, block, cut_out,
                            cut_up, cut + krows - cut_up,
                        )

    return pl.pallas_call(
        kernel,
        grid_spec=pltpu.PrefetchScalarGridSpec(
            num_scalar_prefetch=1,
            grid=(places.z,),
            in_specs=[
                pl.BlockSpec(memory_space=pl.ANY),
                resident(),
                pl.BlockSpec(memory_space=pl.ANY),
                pl.BlockSpec(memory_space=pl.ANY),
                whole(one.shape),
                whole(two.shape),
            ]
            + anywhere(after),
            out_specs=whole(shape),
            scratch_shapes=[
                pltpu.VMEM((places.x * krows + 16, tokens), bf16),
                pltpu.VMEM((width // 2, tokens), bf16),
                pltpu.VMEM(att.shape, bf16),
                pltpu.SemaphoreType.DMA((places.x,)),
                pltpu.SemaphoreType.DMA((places.dp,)),
                pltpu.SemaphoreType.DMA,
                pltpu.VMEM((8, ff), f32),
                pltpu.VMEM((32, cols), f32),
            ],
        ),
        out_shape=jax.ShapeDtypeStruct(shape, bf16),
        compiler_params=kernel_params(18),
        cost_estimate=cost(width * tokens * (ff + width), 12e6),
        name="up_grad",
    )(ids, nl_t, dup, br_t, *in_hbm(att), one, two, *after)


def square_grad(places, other, cut, ids, d_ts, sources, small, length, g_bq, after=()):
    n_rows, width, _ = d_ts[0].shape
    half = width // (2 * places.dp)
    cols = width // places.x
    count = len(d_ts)
    _, seq, keys = small.shape
    s_half, s_cols = seq // (2 * places.dp), keys // places.x
    extra = s_half // 2
    shape = places.shape(count * half + extra, cols)
    flat_s = [p for source in sources for p, _ in source]
    specs = [
        pl.BlockSpec((1,) + p.shape[1:], lambda i, ids, own=own: (own, 0, 0))
        for source in sources
        for p, own in source
    ]
    split = len(sources[0])
    index = [range(split)] + [range(split, len(flat_s))] * (count - 1)
    lengths = [n_rows * d.shape[2] for d in d_ts]
    after = list(after)

    def kernel(ids, *refs):
        d_refs, refs = refs[:count], refs[count:]
        s_refs, refs = refs[: len(flat_s)], refs[len(flat_s) :]
        small_ref, refs = refs[0], refs[1:]
        g_bq, refs = refs[0], refs[1 + len(after) :]
        outs, refs = refs[:1], refs[1:]
        lhs, (rhs, total, vec, sems) = refs[:count], refs[count:]
        copies = []
        for m in range(count):
            copies.append([])
            start = 0
            for r in range(n_rows):
                src = d_refs[m]
                for d in range(places.dp):
                    first = pl.multiple_of(2 * half * d + half * (ids[0] ^ other), 16)
                    copy = pltpu.make_async_copy(
                        src.at[r, pl.ds(first, half), :],
                        lhs[m].at[d * half : (d + 1) * half, start : start + src.shape[2]],
                        sems.at[m, r, d],
                    )
                    copy.start()
                    copies[-1].append(copy)
                start += src.shape[2]
        total[...] = total_of([small_ref[r] for r in range(n_rows)])
        for i in range(seq // length):
            for j in range(length // (2 * s_half)):
                d = (ids[4] ^ i) * (length // (2 * s_half)) + j
                yr, zr = ids[1] ^ (d % places.y), ids[2] ^ (d // places.y)
                first = i * length + 2 * s_half * j + s_half * (ids[0] ^ other)
                block = total[pl.ds(pl.multiple_of(first, 16), s_half), :].astype(bf16)
                for x in range(places.x):
                    for part in range(2):
                        outs[0][
                            yr,
                            ids[3] ^ x,
                            zr,
                            count * half :,
                            part * s_cols : (part + 1) * s_cols,
                        ] = block[part * extra : (part + 1) * extra, x * s_cols : (x + 1) * s_cols]
        vec[...] = jnp.zeros(vec.shape, f32)
        acc = total_of([g_bq[r] for r in range(n_rows)])
        for i in range(width // 128):
            vec[i : i + 1, :] = acc[:, i * 128 : (i + 1) * 128]
        low = vec[...].astype(bf16)
        for i in range(2):
            for j in range(2):
                for z in range(places.z):
                    outs[0][i, j, z, count * half :, 2 * s_cols : 2 * s_cols + 128] = low
        for m in range(count):
            start = 0
            for i in index[m]:
                rhs[start : start + s_refs[i].shape[1], :] = s_refs[i][0]
                start += s_refs[i].shape[1]
            for copy in copies[m]:
                copy.wait()
            res = nn(lhs[m][...], rhs[:start, :]).astype(bf16)
            for z in range(places.z):
                for y in range(places.y):
                    d = z * places.y + y
                    for x in range(places.x):
                        block = res[d * half : (d + 1) * half, x * cols : (x + 1) * cols]
                        places.put(
                            outs[0], ids[3] ^ x, ids[1] ^ y, ids[2] ^ z, block, cut,
                            m * cut, count * cut + m * (half - cut),
                        )

    return pl.pallas_call(
        kernel,
        grid_spec=pltpu.PrefetchScalarGridSpec(
            num_scalar_prefetch=1,
            grid=(1,),
            in_specs=anywhere(d_ts)
            + specs
            + [whole(small.shape), whole(g_bq.shape)]
            + anywhere(after),
            out_specs=whole(shape),
            scratch_shapes=[pltpu.VMEM((width // 2, n), bf16) for n in lengths]
            + [
                pltpu.VMEM((max(lengths), width), bf16),
                pltpu.VMEM((seq, keys), f32),
                pltpu.VMEM((extra, 128), f32),
                pltpu.SemaphoreType.DMA((count, n_rows, places.dp)),
            ],
        ),
        out_shape=jax.ShapeDtypeStruct(shape, bf16),
        compiler_params=kernel_params(16),
        cost_estimate=cost(2.2e9, 12e6),
        name="square_grad",
    )(ids, *d_ts, *flat_s, small, g_bq, *after)


def gather_rows(ids, parts, after=()):
    n = len(parts)
    rows, length, width = parts[0].shape
    arrays, specs = [], []
    for part in parts:
        if isinstance(part, tuple):
            array, at = part
            arrays.append(array)
            specs.append(
                pl.BlockSpec((1, rows, length, width), lambda i, ids, at=at: (at, 0, 0, 0))
            )
        else:
            arrays.append(part)
            specs.append(whole((rows, length, width)))

    def kernel(ids, *refs):
        out, token = refs[-2:]
        token[...] = jnp.zeros(token.shape, f32)
        for i in range(n):

            @pl.when(pl.program_id(0) == i)
            def _():
                part = refs[i]
                out[...] = (part[0] if len(part.shape) == 4 else part[...]).astype(f32)

    return pl.pallas_call(
        kernel,
        grid_spec=pltpu.PrefetchScalarGridSpec(
            num_scalar_prefetch=1,
            grid=(n,),
            in_specs=specs + anywhere(after),
            out_specs=[
                pl.BlockSpec((rows, length, width), lambda i, ids: (ids[4] ^ i, 0, 0)),
                whole((8, 128)),
            ],
        ),
        out_shape=[out_hbm((n * rows, length, width), f32), jax.ShapeDtypeStruct((8, 128), f32)],
        compiler_params=kernel_params(10),
        cost_estimate=cost(0, 6 * n * rows * length * width),
        name="gather_rows",
    )(ids, *arrays, *after)


def exchange(value, axis, size, relative):
    pairs = [(i, i ^ relative) for i in range(size)]
    return lax.ppermute(value, axis, pairs)


def total_of(parts):
    acc = parts[0].astype(f32)
    for part in parts[1:]:
        acc = acc + part.astype(f32)
    return acc


def call(name, kernel, grid, ins, specs, outs, out_specs, after=(), scratch=()):
    def wrapped(*refs):
        kernel(*refs[: len(ins)], *refs[len(ins) + len(after) :])

    moved = sum(math.prod(shape) * 8 for shape, _ in outs)
    return pl.pallas_call(
        wrapped,
        grid=grid,
        in_specs=list(specs) + anywhere(after),
        out_specs=out_specs,
        out_shape=[jax.ShapeDtypeStruct(shape, dt) for shape, dt in outs],
        scratch_shapes=list(scratch),
        compiler_params=kernel_params(8),
        cost_estimate=cost(moved, moved),
        name=name,
    )(*ins, *after)


class Reduction:
    def __init__(self, places, n_dp, n_krow, cut):
        self.places, self.n_dp, self.n_krow, self.cut = places, n_dp, n_krow, cut

    def along(self, axis, value, relative):
        if axis == "x":
            return exchange(value, "krow", self.n_krow, 2 * relative)
        if axis == "y":
            return exchange(value, "dp", self.n_dp, relative)
        return exchange(value, "dp", self.n_dp, relative * self.places.y)

    def core(self, send):
        self.came = exchange(send, "krow", self.n_krow, 1)

    def first(self, keep, after=()):
        self.keep = keep
        _, _, nz, rows, cols = keep.shape
        cut = self.cut
        self.heights = (cut, rows - cut)

        def kernel(k, c, first, second):
            total = total_of([k[0], c[0]]).astype(bf16)
            first[...] = total[:, :, :cut]
            second[...] = total[:, :, cut:]

        spec = pl.BlockSpec((1, 2, 1, rows, cols), lambda z: (1, 0, z, 0, 0))
        res = call(
            "first_sum", kernel, (nz,), [keep, self.came], [spec] * 2,
            [((2, nz, h, cols), bf16) for h in self.heights],
            [pl.BlockSpec((2, 1, h, cols), lambda z: (0, z, 0, 0)) for h in self.heights],
            after,
        )
        self.one = [self.along(axis, r, 1) for axis, r in zip("xy", res)]
        return res

    def second(self, after=()):
        _, _, nz, rows, cols = self.keep.shape
        cut = self.cut

        def kernel(k, c, g, h, first, second):
            first[0] = total_of([k[0, 0, 0, :cut], c[0, 0, 0, :cut], g[0, 0]]).astype(bf16)
            second[0] = total_of([k[0, 0, 0, cut:], c[0, 0, 0, cut:], h[0, 0]]).astype(bf16)

        spec = pl.BlockSpec((1, 1, 1, rows, cols), lambda z: (0, 1, z, 0, 0))
        res = call(
            "second_sum", kernel, (nz,), [self.keep, self.came] + self.one,
            [spec] * 2
            + [pl.BlockSpec((1, 1, h, cols), lambda z: (1, z, 0, 0)) for h in self.heights],
            [((nz, h, cols), bf16) for h in self.heights],
            [pl.BlockSpec((1, h, cols), lambda z: (z, 0, 0)) for h in self.heights],
            after,
        )
        self.two = [self.along(axis, r, 1) for axis, r in zip("yx", res)]
        return res

    def third(self, after=()):
        _, _, nz, rows, cols = self.keep.shape
        cut = self.cut

        def kernel(k, c, g1, h1, g2, h2, odd, even):
            for z in range(nz):
                out = odd if z % 2 else even
                for part, one, two in ((slice(0, cut), g1, g2), (slice(cut, rows), h1, h2)):
                    value = total_of([k[0, 0, z, part], c[0, 0, z, part], one[0, z], two[z]])
                    out[z // 2, part, :] = value.astype(out.dtype)

        shape = (nz // 2, rows, cols)
        spec = pl.BlockSpec((1, 1, nz, rows, cols), lambda i: (0, 0, 0, 0, 0))
        odd, self.even = call(
            "third_sum", kernel, (1,), [self.keep, self.came] + self.one + self.two,
            [spec] * 2
            + [pl.BlockSpec((1, nz, h, cols), lambda i: (0, 0, 0, 0)) for h in self.heights]
            + [pl.BlockSpec((nz, h, cols), lambda i: (0, 0, 0)) for h in self.heights],
            [(shape, bf16), (shape, f32)], [whole(shape)] * 2, after,
        )
        self.three = self.along("z", odd, 1)
        return [odd]

    def fourth(self, after=()):
        _, rows, cols = self.even.shape

        def kernel(e, g, send, mine):
            send[...] = total_of([e[1], g[1]]).astype(bf16)
            mine[...] = total_of([e[0], g[0]])

        shape = (rows, cols)
        send, mine = call(
            "fourth_sum", kernel, (1,), [self.even, self.three], [whole(self.even.shape)] * 2,
            [(shape, bf16), (shape, f32)], [whole(shape)] * 2, after,
        )
        self.terms = [mine, self.along("z", send, 2)]
        return [send]


def finish_down(red, after=()):
    rows, cols = red.terms[0].shape
    n = len(red.terms)

    def kernel(*refs):
        refs[n][...] = total_of([r[...] for r in refs[:n]])

    return call(
        "finish_down", kernel, (1,), red.terms, [whole((rows, cols))] * n,
        [((rows, cols), f32)], [whole((rows, cols))], after,
    )


def finish_up(red, cuts, krows, half, width, ff, after=()):
    rows, cols = red.terms[0].shape
    n = len(red.terms)
    cut_up, cut_out = cuts
    rest = krows - cut_up
    sizes = (width,) * 6 + (ff,)

    def kernel(*refs):
        up, out = refs[n], refs[n + 1]
        total = total_of([r[...] for r in refs[:n]])
        low = cut_up + cut_out
        up[:cut_up] = total[:cut_up]
        up[cut_up:] = total[low : low + rest]
        out[:cut_out] = total[cut_up:low]
        out[cut_out:] = total[low + rest : krows + half]
        at = krows + half
        for piece, size in zip(refs[n + 2 :], sizes):
            for i in range(size // cols):
                piece[i * cols : (i + 1) * cols] = total[at, :]
                at += 1

    shapes = [(krows, cols), (half, cols)] + [(size,) for size in sizes]
    return call(
        "finish_up", kernel, (1,), red.terms, [whole((rows, cols))] * n,
        [(shape, f32) for shape in shapes], [whole(shape) for shape in shapes], after,
    )


def finish_square(red, ids, out_rows, cut, half, count, s_cols, after=()):
    rows, cols = red.terms[0].shape
    n = len(red.terms)
    extra = rows - count * half
    mine_cols = cols // 2
    width = cols * red.places.x
    height = (count + 1) * half + 2 * extra

    def kernel(ids, out_ref, *refs):
        terms, (mine, other, g_bq, temp) = refs[:n], refs[n:]
        total = total_of([r[...] for r in terms])
        rest = half - cut
        temp[:half] = out_ref[...]
        for m in range(count):
            at = half * (m + 1)
            temp[at : at + cut] = total[m * cut : (m + 1) * cut]
            low = count * cut + m * rest
            temp[at + cut : at + half] = total[low : low + rest]
        core = ids[0]
        square = (count + 1) * half
        lo, hi = temp[:square, :mine_cols], temp[:square, mine_cols:]
        mine[:square, :] = jnp.where(core == 0, lo, hi)
        other[:square, :] = jnp.where(core == 0, hi, lo).astype(bf16)
        h = s_cols // 2
        mine[square:, :] = jnp.zeros((2 * extra, mine_cols), f32)
        other[square:, :] = jnp.zeros((2 * extra, mine_cols), bf16)
        for part in range(2):
            tail = total[count * half :, part * s_cols : (part + 1) * s_cols]
            at = square + part * extra
            lo, hi = tail[:, :h], tail[:, h:]
            mine[at : at + extra, :h] = jnp.where(core == 0, lo, hi)
            other[at : at + extra, :h] = jnp.where(core == 0, hi, lo).astype(bf16)
        for i in range(width // 128):
            g_bq[i * 128 : (i + 1) * 128] = total[count * half + i, 2 * s_cols : 2 * s_cols + 128]

    return call(
        "finish_square", kernel, (1,), [ids, out_rows] + red.terms,
        [pl.BlockSpec(memory_space=pltpu.SMEM), whole(out_rows.shape)]
        + [whole((rows, cols))] * n,
        [((height, mine_cols), f32), ((height, mine_cols), bf16), ((width,), f32)],
        [whole((height, mine_cols))] * 2 + [whole((width,))],
        after,
        [pltpu.VMEM(((count + 1) * half, cols), f32)],
    )


def finish_columns(ids, mine, there, half, count, extra, s_half_cols):
    mine_cols = mine.shape[1]
    square = count * half

    def kernel(ids, mine, there, *refs):
        outs, temp = refs[:-1], refs[-1]
        core = ids[0]

        def merge(at, height, cols, out):
            a, b = mine[at : at + height, :cols], there[at : at + height, :cols].astype(f32)
            low, high = jnp.where(core == 0, a, b), jnp.where(core == 0, b, a)
            out[...] = jnp.concatenate([low, high], axis=0).T

        for m in range(count):
            merge(m * half, half, mine_cols, outs[m])
        merge(square, 2 * extra, s_half_cols, outs[count])

    shapes = [(mine_cols, 2 * half)] * count + [(s_half_cols, 4 * extra)]
    return call(
        "finish_columns", kernel, (1,), [ids, mine, there],
        [pl.BlockSpec(memory_space=pltpu.SMEM), whole(mine.shape), whole(there.shape)],
        [(shape, f32) for shape in shapes], [whole(shape) for shape in shapes],
        (), [pltpu.VMEM((8, 128), f32)],
    )


def local(
    sizes,
    tokens,
    segment_ids,
    segment_live,
    w_query,
    b_query,
    w_key,
    w_value,
    w_out,
    b_out,
    attn_gain,
    attn_shift,
    w_up,
    b_up,
    w_down,
    b_down,
    ffn_gain,
    ffn_shift,
    compress,
    cotangent,
):
    n_dp, n_krow = sizes
    all_rows, length, width = tokens.shape
    rows = all_rows // n_krow
    seq = n_krow * length
    keys = compress.shape[0]
    ff = w_up.shape[1]
    krow, dp = lax.axis_index("krow"), lax.axis_index("dp")
    places = Places(n_dp, n_krow)
    ids = jnp.stack([krow % 2, dp % places.y, dp // places.y, krow // 2, krow]).astype(jnp.int32)
    fast = (
        width % (2 * places.x * 32) == 0
        and ff % (n_dp * 128) == 0
        and ff % (n_krow * 128) == 0
        and width % (2 * n_dp * 16) == 0
        and seq % (2 * n_dp * 32) == 0
        and width % (places.x * 128) == 0
        and keys % (places.x * 128) == 0
        and length % (seq // n_dp) == 0
        and ff // n_dp == width // places.x
        and 2 * (keys // places.x) + 128 <= width // places.x
        and width <= 128 * (seq // (4 * n_dp))
        and places.x == 2
        and places.y == 2
        and places.z == 4
        and rows > 1
    )

    def spread(value):
        parts = []
        for r in range(n_krow):
            part = lax.dynamic_slice_in_dim(value, (krow ^ r) * rows, rows, 0)
            parts.append(exchange(part, "krow", n_krow, r) if r else part)
        return parts

    def back(parts):
        return [exchange(part, "krow", n_krow, r) if r else part for r, part in enumerate(parts)]

    def second_hop(parts, came, *after):
        late = lax.optimization_barrier((came, after))[0]
        core = exchange(parts[1], "krow", n_krow, 1)
        return [parts[0], core, (came, 0), exchange(late[1], "krow", n_krow, 1)]

    def row(value):
        return value.astype(f32).reshape(1, -1)

    toks = spread(tokens)
    cot_source = lax.optimization_barrier((cotangent, toks[-1]))[0]
    cots = spread(cot_source)

    my_ids = lax.dynamic_slice_in_dim(segment_ids, krow * rows, rows, 0)
    my_live = lax.dynamic_slice_in_dim(segment_live, krow * rows, rows, 0)
    labels = jnp.arange(segment_live.shape[1], dtype=jnp.int32)
    live = jnp.sum(
        jnp.where(my_ids[:, :, None] == labels, my_live[:, None, :], 0).astype(f32), axis=-1
    )

    def relative(value, axis):
        return jnp.concatenate(
            [
                lax.dynamic_slice_in_dim(value, (krow ^ r) * length, length, axis)
                for r in range(n_krow)
            ],
            axis=axis,
        )

    live = relative(live, 1)
    comp = relative(compress, 1)
    live_row = live[:, None, :]
    live_col = jnp.broadcast_to(live[:, :, None], (rows, seq, 128))
    comp_t = comp.T
    gain, shift = row(attn_gain), row(attn_shift)

    q_t, pk, k, v, lse, att, xhat, rstd = attn_fwd(
        toks, live_row, comp, w_query, row(b_query), w_key, w_value, w_out, row(b_out)
    )
    n_parts = 3 if fast else n_krow
    res = ffn_fwd(
        fast, cots, xhat, gain, shift, w_up, row(b_up), w_down, row(b_down), row(ffn_gain), row(ffn_shift)
    )
    outs, (act, gp, dh2, d_t, sums_two) = res[:n_parts], res[n_parts:]
    out_came = exchange(outs[2], "krow", n_krow, 2) if fast else None
    ahead = []
    if fast:
        cut_down = 32
        cuts_up = (width // n_krow // 2, 32)
        cut_square = 16
        half = width // (2 * n_dp)
        down = Reduction(places, n_dp, n_krow, cut_down)
        up = Reduction(places, n_dp, n_krow, sum(cuts_up))
        square = Reduction(places, n_dp, n_krow, 3 * cut_square)
        send = down_grad(places, 1, cut_down, ids, d_t, act)
        down.core(send)
        keep = down_grad(places, 0, cut_down, ids, d_t, act, after=[send])
        ahead = list(down.first(keep))

    dup, dh1, da_t, nl_t, br_t, sums_one = ffn_bwd(
        gp, dh2, xhat, rstd, gain, shift, w_up, w_down, w_out, after=ahead
    )

    if fast:
        ahead = down.second([sums_one, out_came])
        out_parts = second_hop(outs, out_came, *ahead)
        parts = nl_t, dup, br_t, att, sums_one, sums_two
        send = up_grad(places, 1, cuts_up, ids, *parts, after=ahead)
        up.core(send)
        keep = up_grad(places, 0, cuts_up, ids, *parts, after=[send])
        ahead = up.first(keep)
        ahead = down.third(ahead)

    res = attn_bwd(
        fast, toks, q_t, k, v, lse, da_t, comp_t, live_col, w_query, w_key, w_value, dh1, after=ahead
    )
    grad_parts, bwd = res[:n_parts], res[n_parts:]

    if fast:
        sources = [[(t, r) for r in range(rows) for t in toks], [(in_hbm(pk)[0], r) for r in range(rows)]]
        ahead = up.second([bwd[3], down.three])
        ahead = down.fourth(ahead)
        parts = bwd[:3], sources, bwd[4], length, bwd[3]
        send = square_grad(places, 1, cut_square, ids, *parts, after=ahead)
        square.core(send)
        keep = square_grad(places, 0, cut_square, ids, *parts, after=[send])
        ahead = square.first(keep, [down.terms[1]])
        ahead = up.third(ahead)
        grad_parts = lax.optimization_barrier((grad_parts, ahead))[0]
        grad_came = exchange(grad_parts[2], "krow", n_krow, 2)
        output, token = gather_rows(ids, out_parts, after=ahead)
        ahead = up.fourth([token])
        ahead = square.second(ahead)
        grad_parts = second_hop(grad_parts, grad_came, *ahead)
        g_up, out_rows, *pieces = finish_up(
            up, cuts_up, width // n_krow, half, width, ff, after=ahead
        )
        ahead = square.third([out_rows])
        (g_down,) = finish_down(down, after=ahead)
        grad_tokens, token = gather_rows(ids, grad_parts, after=ahead)
        square.fourth([token])
        g_down = g_down.T
        s_cols = keys // places.x
        mine, other, g_bq = finish_square(square, ids, out_rows, cut_square, half, 3, s_cols)
        pieces = [g_bq] + pieces
        there = exchange(other, "krow", n_krow, 1)
        g_out, g_q, g_k, g_v, g_comp = finish_columns(
            ids, mine, there, half, 4, seq // (4 * n_dp), s_cols // 2
        )
    else:
        grad_parts = back(grad_parts)
        g_bu = jnp.sum(dup.astype(f32), axis=(0, 1)).reshape(-1, width)
        g_bq = jnp.sum(bwd[3], axis=0)
        vectors = jnp.concatenate([g_bq, sums_one[:3], sums_two[:3], g_bu], axis=0)
        output, _ = gather_rows(ids, back(outs))
        grad_tokens, _ = gather_rows(ids, grad_parts)
        vectors = lax.psum(vectors.reshape(-1), ("dp", "krow"))
        pieces = []
        start = 0
        for size in (width,) * 7 + (ff,):
            pieces.append(vectors[start : start + size])
            start += size

        def scattered(value):
            value = value.astype(bf16)
            part = lax.psum_scatter(value, "krow", scatter_dimension=0, tiled=True)
            return lax.psum_scatter(part, "dp", scatter_dimension=1, tiled=True).astype(f32)

        def product(a, b):
            return lax.dot_general(a, b, (((1,), (0,)), ((), ())), preferred_element_type=f32)

        token_rows = jnp.concatenate(toks, axis=1)
        d_q, d_k, d_v = [jnp.swapaxes(d, 0, 1).reshape(width, -1) for d in bwd[:3]]
        pk = pk.reshape(-1, width)
        g_q = scattered(product(d_q, token_rows.reshape(-1, width)).T)
        g_k = scattered(product(d_k, pk).T)
        g_v = scattered(product(d_v, pk).T)
        g_out = scattered(product(br_t, att.reshape(-1, width)).T)
        g_up = scattered(product(nl_t, dup.reshape(-1, ff)))
        g_down = scattered(product(d_t, act.reshape(-1, ff)).T)
        blocks = jnp.sum(bwd[4].astype(f32), axis=0).reshape(n_krow, length, keys)
        blocks = jnp.concatenate(
            [lax.dynamic_slice_in_dim(blocks, krow ^ r, 1, 0) for r in range(n_krow)]
        )
        g_comp = scattered(blocks.reshape(seq, keys).T)

    g_bq, g_gain, g_shift, g_bo, g_fgain, g_fshift, g_bd, g_bu = pieces
    return (
        output,
        grad_tokens,
        g_q,
        g_bq,
        g_k,
        g_v,
        g_out,
        g_bo,
        g_gain,
        g_shift,
        g_up,
        g_bu,
        g_down,
        g_bd,
        g_fgain,
        g_fshift,
        g_comp,
    )


def solution(mesh):
    rows = P("dp", "krow", None)
    per_row = P("dp", None)
    block = P("krow", "dp")
    in_specs = (rows, per_row, per_row) + (P(),) * 15 + (rows,)
    out_specs = (
        (rows, rows, block, P(), block, block, block)
        + (P(),) * 3
        + (block, P(), block)
        + (P(),) * 3
        + (block,)
    )
    sizes = (mesh.shape["dp"], mesh.shape["krow"])
    return jax.shard_map(
        functools.partial(local, sizes),
        mesh=mesh,
        in_specs=in_specs,
        out_specs=out_specs,
        check_vma=False,
    )
```
